128 devices in a mesh: seq: 8 (over z, core), tp: 16 (over x, y).
Axes of the slice: x: 4, y: 4, z: 4, core: 2. Of those that a mesh axis runs over, the one named last changes fastest.
Arguments:
- hidden_in: bfloat16 [2048, 6144], P('seq', 'tp'), may hold values from -6 to 6
- norm_gain: bfloat16 [6144], replicated, may hold values from 0.099609375 to 1.8984375
- w_query: bfloat16 [6144, 6144], P(None, 'tp'), may hold values from -0.078125 to 0.078125
- w_keyval: bfloat16 [6144, 2048], P(None, 'tp'), may hold values from -0.15625 to 0.15625
- w_out: bfloat16 [6144, 6144], P('tp'), may hold values from -0.5 to 0.5
- key_pool: bfloat16 [1024, 128, 1024], P(('seq', 'tp')), may hold values from -512 to 512
- value_pool: bfloat16 [1024, 128, 1024], P(('seq', 'tp')), may hold values from -6 to 6
- block_table: int32 [32, 64], replicated, may hold values from -1 to 1023, as said below
- prefix_lengths: int32 [32], replicated, may hold values from 1 to 8192, as said below
- row_request: int32 [2048], P('seq'), may hold values from 0 to 31, as said below
Outputs:
- attention_out: bfloat16 [2048, 6144], P(('seq', 'tp'))
The draws below stay inside these ranges and needn't reach their ends.
Inputs may be any that keep to these rules, and one draw needn't show every extreme that they name: `block_table`: row r lists its request's pool blocks: the first ceil(prefix_lengths[r] / 128) entries are distinct block ids b with b % 8 equal to r // 4, the rest are -1; no block is listed by two requests; the blocks listed by one group hold at most 128 blocks. `prefix_lengths`: in every group one request has exactly 8192 tokens. `row_request`: row i names a request of group i // 256, that is a request r with r // 4 == i // 256.
All inputs are finite; a program needn't handle non-finite values.
Results may differ from the reference program's by a relative error of at most 0.02.
The reference program's roundings to bfloat16 on the way (of `normed`, `queries`, `keyvals` and `attended`) count: a program that leaves them out, or rounds other values in their place, can miss the bound.
Values may be sent and summed in bfloat16 or wider, within the bound.
A program may use at most 128 MiB of HBM per device.

```python
import jax
import jax.numpy as jnp
from jax import lax

D = 6144
QH = 48
KVH = 8
HD = 128
BLK = 128
REQ_GRP = 4
ROW_GRP = 256
ROWS = 2048
REQS = 32
GB = 128
POOL = 1024
MAXB = 64
N_SEQ = 8


def block_counts(key):
    key = jax.random.fold_in(key, 101)
    key_full, key_rest = jax.random.split(key)
    spare = (GB - MAXB) // (REQ_GRP - 1)
    others = jax.random.randint(key_rest, (N_SEQ, REQ_GRP), 1, spare + 1)
    full_index = jax.random.randint(key_full, (N_SEQ,), 0, REQ_GRP)
    slots = jnp.arange(REQ_GRP, dtype=jnp.int32)[None, :]
    counts = jnp.where(slots == full_index[:, None], MAXB, others)
    return (counts.astype(jnp.int32), slots == full_index[:, None])


def draw_prefix_lengths(key, part):
    counts, is_full = block_counts(key)
    key = jax.random.fold_in(key, 7)
    tail = jax.random.randint(key, (N_SEQ, REQ_GRP), 1, BLK + 1)
    tail = jnp.where(is_full, BLK, tail)
    lengths = (counts - 1) * BLK + tail
    return lengths.reshape(REQS).astype(jnp.int32)


def draw_block_table(key, part):
    counts, is_full = block_counts(key)
    key = jax.random.fold_in(key, 11)
    group_keys = jax.random.split(key, N_SEQ)
    perms = jax.vmap(lambda one_key: jax.random.permutation(one_key, GB))(group_keys).astype(jnp.int32)
    offsets = jnp.cumsum(counts, axis=1) - counts
    slots = jnp.arange(MAXB, dtype=jnp.int32)
    picks = jnp.minimum(offsets[:, :, None] + slots[None, None, :], GB - 1)
    entries = jax.vmap(lambda perm, pick: perm[pick])(perms, picks)
    groups = jnp.arange(N_SEQ, dtype=jnp.int32)[:, None, None]
    table = jnp.where(slots[None, None, :] < counts[:, :, None], entries * N_SEQ + groups, -1)
    return table.reshape(REQS, MAXB).astype(jnp.int32)


def draw_row_request(key, part):
    key = jax.random.fold_in(key, 13)
    local = jax.random.randint(key, (N_SEQ, ROW_GRP), 0, REQ_GRP)
    base = jnp.arange(N_SEQ, dtype=jnp.int32)[:, None] * REQ_GRP
    return (local + base).reshape(ROWS).astype(jnp.int32)


def draw_key_pool(key, part):
    key = jax.random.fold_in(key, 17)
    key_body = jax.random.fold_in(key, 0)
    values = 2.0 * jnp.clip(jax.random.normal(key_body, (POOL, BLK, KVH * HD), jnp.float32), -4.0, 4.0)
    return values.astype(jnp.bfloat16)


def steps_of(key, extent, cuts, least, largest):
    def one(position, shards_of):
        steps = jax.random.uniform(jax.random.fold_in(jax.random.fold_in(key, 6), position), (shards_of,), jnp.float32, least / len(cuts), largest / len(cuts))
        return jnp.repeat(jnp.exp(steps), extent[position] // shards_of).reshape((-1,) + (1,) * (len(extent) - position - 1))

    loudness = one(*cuts[0])
    for cut in cuts[1:]:
        loudness = loudness * one(*cut)
    return loudness


def normal_values(rng, extent, width, reach, cuts=(), kind=jnp.bfloat16):
    factor_of = steps_of(rng, extent, cuts, -0.22, 0.18) if cuts else 1.0
    result = jax.random.normal(rng, extent, jnp.float32) * width * factor_of
    return jnp.minimum(jnp.maximum(result, -reach), reach).astype(kind)


def setup_inputs(seed: int = 0) -> dict:
    keys = jax.random.split(jax.random.key(seed), 11)
    hidden_in = normal_values(keys[0], (ROWS, D), 1.0, 6.0, ((0, 8), (1, 16)))
    norm_gain = jnp.clip(1.0 + 0.18 * jax.random.normal(keys[1], (D,), jnp.float32), 0.099609375, 1.8984375).astype(jnp.bfloat16)
    w_query = normal_values(keys[2], (D, QH * HD), D ** -0.5, 0.078125, ((1, 16),))
    w_keyval = normal_values(keys[3], (D, 2 * KVH * HD), (D // 4) ** -0.5, 0.15625, ((1, 16),))
    w_out = normal_values(keys[4], (QH * HD, D), HD ** -0.5, 0.5, ((0, 16),))
    key_pool = draw_key_pool(jax.random.fold_in(keys[10], 71), 0)
    value_pool = normal_values(keys[6], (POOL, BLK, KVH * HD), 1.0, 6.0, ((0, 128),))
    block_table = draw_block_table(jax.random.fold_in(keys[10], 71), 0)
    prefix_lengths = draw_prefix_lengths(jax.random.fold_in(keys[10], 71), 0)
    row_request = draw_row_request(jax.random.fold_in(keys[10], 71), 0)
    return dict(hidden_in=hidden_in, norm_gain=norm_gain, w_query=w_query, w_keyval=w_keyval, w_out=w_out, key_pool=key_pool, value_pool=value_pool, block_table=block_table, prefix_lengths=prefix_lengths, row_request=row_request)


EPSILON = 1e-05

def reference(hidden_in, norm_gain, w_query, w_keyval, w_out, key_pool, value_pool, block_table, prefix_lengths, row_request):
    widened = hidden_in.astype(jnp.float32)
    normed = (widened * lax.rsqrt(lax.optimization_barrier(jnp.mean(widened * widened, axis=1, keepdims=True)) + EPSILON) * norm_gain.astype(jnp.float32)).astype(jnp.bfloat16)
    queries = jnp.dot(normed, w_query, preferred_element_type=jnp.float32).astype(jnp.bfloat16).reshape(ROWS, QH, HD)
    keyvals = jnp.dot(normed, w_keyval, preferred_element_type=jnp.float32).astype(jnp.bfloat16).reshape(ROWS, KVH, 2, HD)
    key_new = keyvals[:, :, 0, :]
    value_new = keyvals[:, :, 1, :]
    per_head = QH // KVH
    score_scale = 1.0 / HD ** 0.5
    key_groups = key_pool.reshape(GB, N_SEQ, BLK, KVH, HD)
    value_groups = value_pool.reshape(GB, N_SEQ, BLK, KVH, HD)

    def one_group(group_index):
        keys_all = lax.dynamic_index_in_dim(key_groups, group_index, 1, keepdims=False).reshape(GB * BLK, KVH, HD)
        values_all = lax.dynamic_index_in_dim(value_groups, group_index, 1, keepdims=False).reshape(GB * BLK, KVH, HD)
        group_table = lax.dynamic_slice_in_dim(block_table, group_index * REQ_GRP, REQ_GRP, 0)
        group_lengths = lax.dynamic_slice_in_dim(prefix_lengths, group_index * REQ_GRP, REQ_GRP, 0)
        req_ids = (group_index * REQ_GRP + jnp.arange(REQ_GRP, dtype=jnp.int32)).astype(jnp.int32)
        listed = group_table >= 0
        local_ids = jnp.where(listed, group_table // N_SEQ, GB).astype(jnp.int32)
        owner_src = jnp.broadcast_to(req_ids[:, None], (REQ_GRP, MAXB)).astype(jnp.int32)
        pos_src = jnp.broadcast_to(jnp.arange(MAXB, dtype=jnp.int32)[None, :], (REQ_GRP, MAXB)).astype(jnp.int32)
        block_owner = jnp.full((GB,), -1, jnp.int32).at[local_ids.reshape(-1)].set(owner_src.reshape(-1), mode='drop')
        block_pos = jnp.zeros((GB,), jnp.int32).at[local_ids.reshape(-1)].set(pos_src.reshape(-1), mode='drop')
        owner_tok = jnp.repeat(block_owner, BLK)
        pos_tok = (block_pos[:, None] * BLK + jnp.arange(BLK, dtype=jnp.int32)[None, :]).reshape(-1)
        group_rows = lax.dynamic_slice_in_dim(row_request, group_index * ROW_GRP, ROW_GRP, 0)
        matches = (group_rows[:, None] == req_ids[None, :]).astype(jnp.int32)
        row_len = lax.optimization_barrier(jnp.sum(matches * group_lengths[None, :], axis=1))
        allowed = (owner_tok[None, :] == group_rows[:, None]) & (pos_tok[None, :] < row_len[:, None])
        group_queries = lax.dynamic_slice_in_dim(queries, group_index * ROW_GRP, ROW_GRP, 0)
        group_keynew = lax.dynamic_slice_in_dim(key_new, group_index * ROW_GRP, ROW_GRP, 0)
        group_valnew = lax.dynamic_slice_in_dim(value_new, group_index * ROW_GRP, ROW_GRP, 0)

        def one_head(head_index):
            head_keys = lax.dynamic_index_in_dim(keys_all, head_index, 1, keepdims=False).astype(jnp.float32)
            head_values = lax.dynamic_index_in_dim(values_all, head_index, 1, keepdims=False).astype(jnp.float32)
            head_queries = lax.dynamic_slice_in_dim(group_queries, head_index * per_head, per_head, 1).astype(jnp.float32)
            own_key = lax.dynamic_index_in_dim(group_keynew, head_index, 1, keepdims=False).astype(jnp.float32)
            own_value = lax.dynamic_index_in_dim(group_valnew, head_index, 1, keepdims=False).astype(jnp.float32)
            scores = jnp.einsum('rhd,td->rht', head_queries, head_keys) * score_scale
            scores = jnp.where(allowed[:, None, :], scores, -1e+30)
            self_score = jnp.einsum('rhd,rd->rh', head_queries, own_key) * score_scale
            top = jnp.maximum(lax.optimization_barrier(jnp.max(scores, axis=2)), self_score)
            weights = jnp.exp(scores - top[:, :, None])
            own_weight = jnp.exp(self_score - top)
            total = lax.optimization_barrier(jnp.sum(weights, axis=2)) + own_weight
            numer = jnp.einsum('rht,td->rhd', weights.astype(jnp.bfloat16).astype(jnp.float32), head_values)
            numer = numer + own_weight.astype(jnp.bfloat16).astype(jnp.float32)[:, :, None] * own_value[:, None, :]
            return (numer / total[:, :, None]).astype(jnp.bfloat16)
        heads_out = lax.map(one_head, jnp.arange(KVH, dtype=jnp.int32))
        return jnp.transpose(heads_out, (1, 0, 2, 3)).reshape(ROW_GRP, QH * HD)
    attended = lax.map(one_group, jnp.arange(N_SEQ, dtype=jnp.int32)).reshape(ROWS, QH * HD)
    return jnp.dot(attended, w_out, preferred_element_type=jnp.float32).astype(jnp.bfloat16)
```

```python
import functools

import jax
import jax.numpy as jnp
from jax import lax
from jax.experimental import pallas as pl
from jax.experimental.pallas import tpu as pltpu
from jax.sharding import PartitionSpec as P

MESH = pl.DeviceIdType.MESH
HD = 128
BLK = 128
ROWS = 256
FEAT = 384
SHARDS = 16
HEADS = 3
SLOTS = 64
CHUNK = 8
CHUNKS = 8
TILE = 512
TILES = 6
MASKED = -1e30
LOG2_SCALE = 1.4426950408889634 / HD**0.5


def ring_partner(y, o):
    return (3 - (y + 4 - o) % 4 + o) % 4


def body(
    hidden,
    gain,
    w_query,
    w_keyval,
    w_out,
    key_pool,
    value_pool,
    table,
    caps,
    row_req,
    out,
    hbuf,
    wqkv,
    wo,
    kbuf,
    vbuf,
    qaug,
    qown,
    kvown,
    acc,
    top,
    tot,
    osend,
    ssend,
    orecv,
    srecv,
    att,
    part,
    rs_a,
    rs_b,
    mid_a,
    mid_b,
    fin_a,
    fin_b,
    load_sem,
    ag_send,
    ag_recv,
    kv_send,
    k_recv,
    v_recv,
    q_send,
    q_recv,
    own_send,
    own_recv,
    o_send,
    o_recv,
    s_send,
    s_recv,
    rs1_send,
    rs1_recv,
    rs2_send,
    rs2_recv,
):
    seq = lax.axis_index("seq")
    tp = lax.axis_index("tp")
    x, y = tp // 4, tp % 4

    def remote(src, dst, send, recv, s, t):
        return pltpu.make_async_remote_copy(
            src, dst, send, recv, device_id=(s, t), device_id_type=MESH
        )

    own_load = pltpu.make_async_copy(hidden, hbuf.at[tp], load_sem.at[0])
    own_load.start()
    loads = [
        pltpu.make_async_copy(w_query, wqkv.at[:, pl.ds(0, 384)], load_sem.at[1]),
        pltpu.make_async_copy(w_keyval, wqkv.at[:, pl.ds(384, 128)], load_sem.at[2]),
        pltpu.make_async_copy(w_out, wo, load_sem.at[3]),
    ]
    for load in loads:
        load.start()

    barrier = pltpu.get_barrier_semaphore()

    def greet(s, t):
        pl.semaphore_signal(barrier, inc=1, device_id=(s, t), device_id_type=MESH)

    def greet_plane(i, carry):
        greet(seq, (tp + i) % 16)
        return carry

    lax.fori_loop(1, 16, greet_plane, 0)
    o_here, o_next = x % 2, (x + 1) % 2
    near = [
        (x, y),
        (x, ring_partner(y, 0)),
        (x, ring_partner(y, 1)),
        ((x + 3) % 4, y),
        ((x + 3) % 4, ring_partner(y, o_here)),
        ((x + 1) % 4, y),
        ((x + 1) % 4, ring_partner(y, o_next)),
    ]

    def greet_near(i, carry):
        for nx, ny in near:
            greet((seq + i) % 8, nx * 4 + ny)
        return carry

    lax.fori_loop(1, 8, greet_near, 0)
    own_load.wait()
    pl.semaphore_wait(barrier, 15 + 7 * 7)

    half = ROWS // 2
    for d in (1, 3, 2):
        remote(hbuf.at[tp], hbuf.at[tp], ag_send, ag_recv.at[tp, 0], seq, (x + d) % 4 * 4 + y).start()
        remote(hbuf.at[tp], hbuf.at[tp], ag_send, ag_recv.at[tp, 0], seq, x * 4 + (y + d) % 4).start()

    def send_chunk(ch, carry):
        u = ch % 2
        ix = ch // 4
        iy = (ch // 2) % 2
        kx = (x + 4 - (u + ix * (3 - 2 * u))) % 4
        o = kx % 2
        yy = (y + 4 - o) % 4
        ky = (yy // 2 + iy) % 2
        xd = (kx + u) % 4
        yd = iy * ((3 - yy + o) % 4) + (1 - iy) * y
        lanes = pl.ds(pl.multiple_of((2 * kx + ky) * HD, HD), HD)
        slot = ch * CHUNK + seq
        dest = xd * 4 + yd

        def send_one(i, c):
            g = (seq + i) % 8
            here = (i == 0) & (dest == tp)

            @pl.when(here)
            def _():
                pltpu.make_async_copy(
                    key_pool.at[g, :, lanes], kbuf.at[slot, :, pl.ds(0, HD)], k_recv.at[ch]
                ).start()
                pltpu.make_async_copy(
                    value_pool.at[g, :, lanes], vbuf.at[slot], v_recv.at[ch]
                ).start()

            @pl.when(jnp.logical_not(here))
            def _():
                remote(
                    key_pool.at[g, :, lanes], kbuf.at[slot, :, pl.ds(0, HD)],
                    kv_send.at[0], k_recv.at[ch], g, dest,
                ).start()
                remote(
                    value_pool.at[g, :, lanes], vbuf.at[slot],
                    kv_send.at[1], v_recv.at[ch], g, dest,
                ).start()

            return c

        return lax.fori_loop(0, 8, send_one, carry)

    lax.fori_loop(0, 2, send_chunk, 0)

    top_rows, low_rows = pl.ds(0, half), pl.ds(half, half)
    for d in (1, 3, 2):
        from_x = (x + 4 - d) % 4 * 4 + y
        pltpu.make_async_copy(hbuf.at[from_x], hbuf.at[from_x], ag_recv.at[from_x, 0]).wait()
        for e in (1, 3, 2):
            remote(
                hbuf.at[from_x, top_rows], hbuf.at[from_x, top_rows],
                ag_send, ag_recv.at[from_x, 0], seq, x * 4 + (y + e) % 4,
            ).start()
        from_y = x * 4 + (y + 4 - d) % 4
        pltpu.make_async_copy(hbuf.at[from_y], hbuf.at[from_y], ag_recv.at[from_y, 0]).wait()
        for e in (1, 3, 2):
            remote(
                hbuf.at[from_y, low_rows], hbuf.at[from_y, low_rows],
                ag_send, ag_recv.at[from_y, 1], seq, (x + e) % 4 * 4 + y,
            ).start()

    lax.fori_loop(2, CHUNKS, send_chunk, 0)

    lane = lax.broadcasted_iota(jnp.int32, (ROWS, HD), 1)
    onehot = jnp.where(row_req[...] == lane + seq * 4, 1.0, 0.0).astype(jnp.bfloat16)
    for u in range(2):
        for h in range(2 * HEADS):
            qaug[u, h, :, HD:] = onehot
    token = lax.broadcasted_iota(jnp.int32, (BLK, HD), 0)

    def mask_slot(slot, carry):
        ch, s = slot // 8, slot % 8
        u = ch % 2
        ix = ch // 4
        iy = (ch // 2) % 2
        kx = (x + 4 - u) % 4
        o = kx % 2
        xs = (x + 4 + ix * (2 * u - 1)) % 4
        ys = iy * ring_partner(y, o) + (1 - iy) * y
        block = (s * 16 + xs * 4 + ys) * 8 + seq
        valid = jnp.sum(jnp.where(table[...] == block, caps[...], 0), axis=0, keepdims=True)
        kbuf[slot, :, HD:] = jnp.where(token < valid, 0.0, MASKED).astype(jnp.bfloat16)
        return carry

    lax.fori_loop(0, SLOTS, mask_slot, 0)
    top[...] = jnp.full_like(top, 2 * MASKED)
    tot[...] = jnp.zeros_like(tot)
    acc[...] = jnp.zeros_like(acc)

    for d in (1, 3, 2):
        for e in (1, 3, 2):
            shard = (x + 4 - d) % 4 * 4 + (y + 4 - e) % 4
            pltpu.make_async_copy(
                hbuf.at[shard, top_rows], hbuf.at[shard, top_rows], ag_recv.at[shard, 0]
            ).wait()
            pltpu.make_async_copy(
                hbuf.at[shard, low_rows], hbuf.at[shard, low_rows], ag_recv.at[shard, 1]
            ).wait()

    def squares(t, total):
        wide = hbuf[t].astype(jnp.float32)
        return total + jnp.sum(wide * wide, axis=1, keepdims=True)

    square_sum = lax.fori_loop(0, SHARDS, squares, jnp.zeros((ROWS, 1), jnp.float32))
    factor = lax.rsqrt(square_sum / (SHARDS * FEAT) + 1e-5)
    loads[0].wait()
    loads[1].wait()

    def project(t, total):
        normed = (hbuf[t].astype(jnp.float32) * factor * gain[t].astype(jnp.float32)).astype(
            jnp.bfloat16
        )
        rows = pl.ds(pl.multiple_of(t * FEAT, FEAT), FEAT)
        return total + jnp.dot(normed, wqkv[rows, :], preferred_element_type=jnp.float32)

    projected = lax.fori_loop(0, SHARDS, project, jnp.zeros((ROWS, 512), jnp.float32)).astype(
        jnp.bfloat16
    )
    for h in range(HEADS):
        qown[h] = projected[:, h * HD : (h + 1) * HD]
    kvown[tp % 2] = projected[:, HEADS * HD :]

    own_copy = remote(
        kvown.at[tp % 2], kvown.at[tp % 2], own_send, own_recv.at[tp % 2], seq, tp + 1 - 2 * (tp % 2)
    )
    own_half = tp % 2

    def q_copies(u, j):
        t = (x + u) % 4 * 4 + (y // 2 * 2 + j + o_here) % 4
        dst = qaug.at[u, pl.ds(own_half * HEADS, HEADS), :, pl.ds(0, HD)]
        there = remote(qown, dst, q_send.at[u, j], q_recv.at[u, own_half], seq, t)
        here = pltpu.make_async_copy(qown, dst, q_recv.at[u, own_half])
        return t == tp, here, there

    for u in range(2):
        for j in range(2):
            same, here, there = q_copies(u, j)
            pl.when(same)(here.start)
            pl.when(jnp.logical_not(same))(there.start)
    own_copy.start()
    for u in range(2):
        for part_half in range(2):
            dst = qaug.at[u, pl.ds(part_half * HEADS, HEADS), :, pl.ds(0, HD)]
            pltpu.make_async_copy(dst, dst, q_recv.at[u, part_half]).wait()

    def attend_chunk(ch, carry):
        u = ch % 2
        slots = pl.ds(pl.multiple_of(ch * CHUNK, CHUNK), CHUNK)
        k_dst = kbuf.at[slots, :, pl.ds(0, HD)]
        pltpu.make_async_copy(k_dst, k_dst, k_recv.at[ch]).wait()
        pltpu.make_async_copy(vbuf.at[slots], vbuf.at[slots], v_recv.at[ch]).wait()

        def attend_head(h, c):
            keys = kbuf[slots].reshape(CHUNK * BLK, 2 * HD)
            values = vbuf[slots].reshape(CHUNK * BLK, HD)
            scores = lax.dot_general(
                qaug[u, h], keys, (((1,), (1,)), ((), ())), preferred_element_type=jnp.float32
            )
            old = top[u, h]
            new = jnp.maximum(old, jnp.max(scores, axis=1, keepdims=True))
            shrink = jnp.exp2((old - new) * LOG2_SCALE)
            weights = jnp.exp2(scores * LOG2_SCALE - new[:, :1] * LOG2_SCALE)
            top[u, h] = new
            tot[u, h] = tot[u, h] * shrink + jnp.sum(weights, axis=1, keepdims=True)
            acc[u, h] = acc[u, h] * shrink + jnp.dot(
                weights.astype(jnp.bfloat16), values, preferred_element_type=jnp.float32
            )
            return c

        return lax.fori_loop(0, 2 * HEADS, attend_head, carry)

    lax.fori_loop(0, CHUNKS, attend_chunk, 0)

    def o_copies(u, to):
        kx = (x + 4 - u) % 4
        o = kx % 2
        yy = (y + 4 - o) % 4
        t = kx * 4 + yy // 2 * 2 + to
        index = u * 2 + yy % 2
        o_src, o_dst = osend.at[u, to], orecv.at[index]
        s_src, s_dst = ssend.at[u, to], srecv.at[pl.ds(pl.multiple_of(index * 8, 8), 8)]
        return (
            t == tp,
            pltpu.make_async_copy(o_src, o_dst, o_recv.at[index]),
            remote(o_src, o_dst, o_send.at[u, to], o_recv.at[index], seq, t),
            pltpu.make_async_copy(s_src, s_dst, s_recv.at[index]),
            remote(s_src, s_dst, s_send.at[u, to], s_recv.at[index], seq, t),
        )

    srecv[pl.ds(32, 96), :] = jnp.zeros((96, ROWS), jnp.float32)
    for u in range(2):
        for to in range(2):
            stats = jnp.zeros((ROWS, HD), jnp.float32)
            for h in range(HEADS):
                stats = jnp.where(lane == h, top[u, to * HEADS + h], stats)
                stats = jnp.where(lane == HEADS + h, tot[u, to * HEADS + h], stats)
                osend[u, to, h] = acc[u, to * HEADS + h].astype(jnp.bfloat16)
            ssend[u, to] = stats.T[:8]
            same, o_here_copy, o_there, s_here_copy, s_there = o_copies(u, to)

            @pl.when(same)
            def _():
                o_here_copy.start()
                s_here_copy.start()

            @pl.when(jnp.logical_not(same))
            def _():
                o_there.start()
                s_there.start()

    own_copy.wait_send()
    other = 1 - tp % 2
    pltpu.make_async_copy(kvown.at[other], kvown.at[other], own_recv.at[other]).wait()
    own_key = kvown[0].astype(jnp.float32)
    own_value = kvown[1].astype(jnp.float32)
    self_scores = [
        jnp.sum(qown[h].astype(jnp.float32) * own_key, axis=1, keepdims=True) for h in range(HEADS)
    ]
    for i in range(4):
        pltpu.make_async_copy(orecv.at[i], orecv.at[i], o_recv.at[i]).wait()
        s_dst = srecv.at[pl.ds(i * 8, 8)]
        pltpu.make_async_copy(s_dst, s_dst, s_recv.at[i]).wait()
    stats = srecv[...].T
    for h in range(HEADS):
        tops = [stats[:, i * 8 + h : i * 8 + h + 1] for i in range(4)]
        best = self_scores[h]
        for one in tops:
            best = jnp.maximum(best, one)
        own_weight = jnp.exp2((self_scores[h] - best) * LOG2_SCALE)
        total = own_weight
        numer = own_weight.astype(jnp.bfloat16).astype(jnp.float32) * own_value
        for i in range(4):
            scale = jnp.exp2((tops[i] - best) * LOG2_SCALE)
            total = total + scale * stats[:, i * 8 + HEADS + h : i * 8 + HEADS + h + 1]
            numer = numer + scale * orecv[i, h].astype(jnp.float32)
        att[:, h * HD : (h + 1) * HD] = (numer / total).astype(jnp.bfloat16)

    loads[2].wait()

    def columns(tile, first=0):
        return pl.ds(pl.multiple_of(first + tile * TILE, TILE), TILE)

    def project_out(tile, carry):
        for side in range(2):
            cols = columns(tile, side * TILES * TILE)
            part[:, :, :, cols] = (
                jnp.dot(att[...], wo[:, cols], preferred_element_type=jnp.float32)
                .astype(jnp.bfloat16)
                .reshape(4, 4, 16, TILE)
            )
            for d in (1, 3, 2):
                if side == 0:
                    src, t = part.at[(x + d) % 4, :, :, cols], (x + d) % 4 * 4 + y
                else:
                    src, t = part.at[:, (y + d) % 4, :, cols], x * 4 + (y + d) % 4
                dst = (rs_a, rs_b)[side].at[d - 1, :, :, columns(tile)]
                remote(
                    src, dst, rs1_send.at[side], rs1_recv.at[side, tile, d - 1], seq, t
                ).start()
        return carry

    lax.fori_loop(0, TILES, project_out, 0)

    def sum_first(tile, carry):
        for side in range(2):
            cols = columns(tile, side * TILES * TILE)
            here = columns(tile)
            landed = (rs_a, rs_b)[side]
            mid = (mid_a, mid_b)[side]
            if side == 0:
                total = part[x, :, :, cols].astype(jnp.float32)
            else:
                total = part[:, y, :, cols].astype(jnp.float32)
            for d in range(3):
                dst = landed.at[d, :, :, here]
                pltpu.make_async_copy(dst, dst, rs1_recv.at[side, tile, d]).wait()
                total = total + landed[d, :, :, here].astype(jnp.float32)
            mid[:, :, here] = total.astype(jnp.bfloat16)
            for d in (1, 3, 2):
                if side == 0:
                    src, t = mid.at[(y + d) % 4, :, here], x * 4 + (y + d) % 4
                else:
                    src, t = mid.at[(x + d) % 4, :, here], (x + d) % 4 * 4 + y
                dst = (fin_a, fin_b)[side].at[d - 1, :, here]
                remote(
                    src, dst, rs2_send.at[side], rs2_recv.at[side, tile, d - 1], seq, t
                ).start()
        return carry

    lax.fori_loop(0, TILES, sum_first, 0)

    def sum_last(tile, carry):
        for side in range(2):
            here = columns(tile)
            landed = (fin_a, fin_b)[side]
            if side == 0:
                total = mid_a[y, :, here].astype(jnp.float32)
            else:
                total = mid_b[x, :, here].astype(jnp.float32)
            for d in range(3):
                dst = landed.at[d, :, here]
                pltpu.make_async_copy(dst, dst, rs2_recv.at[side, tile, d]).wait()
                total = total + landed[d, :, here].astype(jnp.float32)
            out[:, columns(tile, side * TILES * TILE)] = total.astype(jnp.bfloat16)
        return carry

    lax.fori_loop(0, TILES, sum_last, 0)

    sent = hbuf.at[pl.ds(0, SHARDS - 1)]
    pltpu.make_async_copy(sent, sent, ag_send).wait()
    sent = kbuf.at[pl.ds(0, SLOTS - 2), :, pl.ds(0, HD)]
    pltpu.make_async_copy(sent, sent, kv_send.at[0]).wait()
    sent = vbuf.at[pl.ds(0, SLOTS - 2)]
    pltpu.make_async_copy(sent, sent, kv_send.at[1]).wait()
    for u in range(2):
        for j in range(2):
            same, _, there = q_copies(u, j)
            pl.when(jnp.logical_not(same))(there.wait_send)
            same, _, o_there, _, s_there = o_copies(u, j)

            @pl.when(jnp.logical_not(same))
            def _():
                o_there.wait_send()
                s_there.wait_send()

    for side in range(2):
        sent = (rs_a, rs_b)[side]
        pltpu.make_async_copy(sent, sent, rs1_send.at[side]).wait()
        sent = (fin_a, fin_b)[side]
        pltpu.make_async_copy(sent, sent, rs2_send.at[side]).wait()


def per_device(
    hidden_in,
    norm_gain,
    w_query,
    w_keyval,
    w_out,
    key_pool,
    value_pool,
    block_table,
    prefix_lengths,
    row_request,
):
    seq = lax.axis_index("seq")
    table = lax.dynamic_slice_in_dim(block_table, seq * 4, 4, 0)
    lengths = lax.dynamic_slice_in_dim(prefix_lengths, seq * 4, 4, 0)
    starts = jnp.arange(64, dtype=jnp.int32)[:, None] * BLK
    caps = jnp.clip(lengths[None, :] - starts, 0, BLK)
    table = jnp.pad(table.T, ((0, 0), (0, HD - 4)), constant_values=-1)
    caps = jnp.pad(caps, ((0, 0), (0, HD - 4)))
    bf16, f32 = jnp.bfloat16, jnp.float32
    vmem = functools.partial(pltpu.VMEM)
    dma = pltpu.SemaphoreType.DMA
    any_spec = pl.BlockSpec(memory_space=pl.ANY)
    vmem_spec = pl.BlockSpec(memory_space=pltpu.VMEM)
    return pl.pallas_call(
        body,
        out_shape=jax.ShapeDtypeStruct((16, 6144), bf16),
        in_specs=[any_spec, vmem_spec] + [any_spec] * 5 + [vmem_spec] * 3,
        out_specs=vmem_spec,
        scratch_shapes=[
            vmem((SHARDS, ROWS, FEAT), bf16),
            vmem((SHARDS * FEAT, 512), bf16),
            vmem((FEAT, 6144), bf16),
            vmem((SLOTS, BLK, 2 * HD), bf16),
            vmem((SLOTS, BLK, HD), bf16),
            vmem((2, 2 * HEADS, ROWS, 2 * HD), bf16),
            vmem((HEADS, ROWS, HD), bf16),
            vmem((2, ROWS, HD), bf16),
            vmem((2, 2 * HEADS, ROWS, HD), f32),
            vmem((2, 2 * HEADS, ROWS, HD), f32),
            vmem((2, 2 * HEADS, ROWS, HD), f32),
            vmem((2, 2, HEADS, ROWS, HD), bf16),
            vmem((2, 2, 8, ROWS), f32),
            vmem((4, HEADS, ROWS, HD), bf16),
            vmem((128, ROWS), f32),
            vmem((ROWS, FEAT), bf16),
            vmem((4, 4, 16, 6144), bf16),
            vmem((3, 4, 16, 3072), bf16),
            vmem((3, 4, 16, 3072), bf16),
            vmem((4, 16, 3072), bf16),
            vmem((4, 16, 3072), bf16),
            vmem((3, 16, 3072), bf16),
            vmem((3, 16, 3072), bf16),
            dma((4,)),
            dma,
            dma((SHARDS, 2)),
            dma((2,)),
            dma((CHUNKS,)),
            dma((CHUNKS,)),
            dma((2, 2)),
            dma((2, 2)),
            dma,
            dma((2,)),
            dma((2, 2)),
            dma((4,)),
            dma((2, 2)),
            dma((4,)),
            dma((2,)),
            dma((2, TILES, 3)),
            dma((2,)),
            dma((2, TILES, 3)),
        ],
        compiler_params=pltpu.CompilerParams(
            collective_id=0, has_side_effects=True, vmem_limit_bytes=56 << 20
        ),
        cost_estimate=pl.CostEstimate(
            flops=10_000_000_000, bytes_accessed=20_000_000, transcendentals=13_000_000
        ),
    )(
        hidden_in,
        norm_gain.reshape(SHARDS, 1, FEAT),
        w_query,
        w_keyval,
        w_out,
        key_pool,
        value_pool,
        table,
        caps,
        row_request.reshape(ROWS, 1),
    )


def solution(mesh):
    return jax.shard_map(
        per_device,
        mesh=mesh,
        in_specs=(
            P("seq", "tp"),
            P(),
            P(None, "tp"),
            P(None, "tp"),
            P("tp", None),
            P(("seq", "tp"), None, None),
            P(("seq", "tp"), None, None),
            P(),
            P(),
            P("seq"),
        ),
        out_specs=P(("seq", "tp"), None),
        check_vma=False,
    )
```

```python
import functools

import jax
import jax.numpy as jnp
from jax import lax
from jax.experimental import pallas as pl
from jax.experimental.pallas import tpu as pltpu
from jax.sharding import PartitionSpec as P

MESH = pl.DeviceIdType.MESH
HD = 128
BLK = 128
ROWS = 256
FEAT = 384
SHARDS = 16
HEADS = 3
SLOTS = 64
CHUNK = 8
CHUNKS = 8
TILE = 512
TILES = 6
MASKED = -1e30
LOG2_SCALE = 1.4426950408889634 / HD**0.5


def ring_partner(y, shift):
    return (7 - (y + 4 - shift) % 4 + shift) % 4


def body(
    hidden,
    gain,
    w_query,
    w_keyval,
    w_out,
    key_pool,
    value_pool,
    table,
    lengths,
    row_req,
    out,
    hbuf,
    wqkv,
    wo,
    kbuf,
    vbuf,
    qaug,
    qown,
    kvown,
    acc,
    top,
    tot,
    osend,
    ssend,
    orecv,
    srecv,
    squares_own,
    squares_x,
    squares_mid,
    squares_y,
    table_wide,
    table_cols,
    caps,
    att,
    part,
    rs_a,
    rs_b,
    mid_a,
    mid_b,
    fin_a,
    fin_b,
    load_sem,
    column_sem,
    plane_sem,
    sq_send,
    sq_recv,
    ag_send,
    ag_recv,
    kv_send,
    k_recv,
    v_recv,
    q_send,
    q_recv,
    own_send,
    own_recv,
    o_send,
    o_recv,
    s_send,
    s_recv,
    rs1_send,
    rs1_recv,
    rs2_send,
    rs2_recv,
):
    seq = lax.axis_index("seq")
    tp = lax.axis_index("tp")
    x, y = tp // 4, tp % 4
    sign = 1 - 2 * (seq % 2)

    def remote(src, dst, send, recv, s, t):
        return pltpu.make_async_remote_copy(
            src, dst, send, recv, device_id=(s, t), device_id_type=MESH
        )

    def signal(sem, s, t):
        pl.semaphore_signal(sem, inc=1, device_id=(s, t), device_id_type=MESH)

    def x_peer(d):
        return (x + d) % 4 * 4 + y

    def y_peer(d):
        return x * 4 + (y + d) % 4

    barrier = pltpu.get_barrier_semaphore()
    for d in (1, 3, 2):
        signal(barrier, seq, x_peer(d))
        signal(barrier, seq, y_peer(d))
    for i in range(1, 8):
        signal(barrier, (seq + i) % 8, tp)

    own_load = pltpu.make_async_copy(hidden, hbuf.at[tp], load_sem.at[0])
    own_load.start()
    loads = [
        pltpu.make_async_copy(w_query, wqkv.at[:, pl.ds(0, 384)], load_sem.at[1]),
        pltpu.make_async_copy(w_keyval, wqkv.at[:, pl.ds(384, 128)], load_sem.at[2]),
        pltpu.make_async_copy(w_out, wo, load_sem.at[3]),
    ]
    for load in loads:
        load.start()
    own_load.wait()
    wide = hbuf[tp].astype(jnp.float32)
    own_sum = jnp.broadcast_to(jnp.sum(wide * wide, axis=1, keepdims=True), (ROWS, HD))
    squares_own[...] = own_sum.T[:8]
    pl.semaphore_wait(barrier, 13)
    for d in (1, 3, 2):
        signal(column_sem, seq, y_peer(d))

    half = ROWS // 2
    for d in (1, 3, 2):
        remote(
            squares_own, squares_x.at[d - 1], sq_send.at[0], sq_recv.at[0, d - 1], seq, x_peer(d)
        ).start()
    for d in (1, 3, 2):
        remote(hbuf.at[tp], hbuf.at[tp], ag_send, ag_recv.at[tp, 0], seq, x_peer(d)).start()
        remote(hbuf.at[tp], hbuf.at[tp], ag_send, ag_recv.at[tp, 0], seq, y_peer(d)).start()

    def send_chunk(ch, carry):
        u = ch % 2
        ix = ch // 4
        iy = (ch // 2) % 2
        slot = ch * CHUNK + seq
        back = u + ix * (3 - 2 * u)

        def send_one(i, c):
            g = (seq + i) % 8
            turn = 1 - 2 * (g % 2)
            kx = (x + 4 - turn * back) % 4
            shift = (kx % 2) * turn
            ky = ((y + 4 - shift) % 4 // 2 + iy) % 2
            xd = (kx + 4 + turn * u) % 4
            yd = iy * ring_partner(y, shift) + (1 - iy) * y
            lanes = pl.ds(pl.multiple_of((2 * kx + ky) * HD, HD), HD)
            dest = xd * 4 + yd
            here = (i == 0) & (dest == tp)

            @pl.when(here)
            def _():
                pltpu.make_async_copy(
                    key_pool.at[g, :, lanes], kbuf.at[slot, :, pl.ds(0, HD)], k_recv.at[ch]
                ).start()
                pltpu.make_async_copy(
                    value_pool.at[g, :, lanes], vbuf.at[slot], v_recv.at[ch]
                ).start()

            @pl.when(jnp.logical_not(here))
            def _():
                remote(
                    key_pool.at[g, :, lanes], kbuf.at[slot, :, pl.ds(0, HD)],
                    kv_send.at[0], k_recv.at[ch], g, dest,
                ).start()
                remote(
                    value_pool.at[g, :, lanes], vbuf.at[slot],
                    kv_send.at[1], v_recv.at[ch], g, dest,
                ).start()

            return c

        return lax.fori_loop(0, 8, send_one, carry)

    lax.fori_loop(0, 2, send_chunk, 0)

    def landed(ref, sem):
        pltpu.make_async_copy(ref, ref, sem).wait()

    square_sums = squares_own[...]
    for d in range(3):
        landed(squares_x.at[d], sq_recv.at[0, d])
        square_sums = square_sums + squares_x[d]
    squares_mid[...] = square_sums
    for d in (1, 3, 2):
        remote(
            squares_mid, squares_y.at[d - 1], sq_send.at[1], sq_recv.at[1, d - 1], seq, y_peer(d)
        ).start()

    pl.semaphore_wait(column_sem, 3)
    signal(plane_sem, seq, x_peer(1))
    signal(plane_sem, seq, x_peer(3))

    top_rows, low_rows = pl.ds(0, half), pl.ds(half, half)
    for d in (1, 3, 2):
        from_x = x_peer(4 - d)
        landed(hbuf.at[from_x], ag_recv.at[from_x, 0])
        for e in (1, 3, 2):
            remote(
                hbuf.at[from_x, top_rows], hbuf.at[from_x, top_rows],
                ag_send, ag_recv.at[from_x, 0], seq, y_peer(e),
            ).start()
        from_y = y_peer(4 - d)
        landed(hbuf.at[from_y], ag_recv.at[from_y, 0])
        for e in (1, 3, 2):
            remote(
                hbuf.at[from_y, low_rows], hbuf.at[from_y, low_rows],
                ag_send, ag_recv.at[from_y, 1], seq, x_peer(e),
            ).start()

    pl.semaphore_wait(plane_sem, 2)
    lax.fori_loop(2, CHUNKS, send_chunk, 0)

    lane = lax.broadcasted_iota(jnp.int32, (ROWS, HD), 1)
    first_request = seq // 2 * 8
    requests = jnp.broadcast_to(row_req[...], (HD, ROWS)).T
    onehot = jnp.where(requests == lane + first_request, 1.0, 0.0).astype(jnp.bfloat16)
    for u in range(2):
        for h in range(2 * HEADS):
            qaug[u, h, :, HD:] = onehot
    table_wide[...] = jnp.full_like(table_wide, -1)
    table_wide[:8, :64] = table[pl.ds(pl.multiple_of(first_request, 8), 8), :]
    table_cols[...] = table_wide[...].T[:64]
    table_lane = lax.broadcasted_iota(jnp.int32, (64, HD), 1)
    ends = jnp.zeros((64, HD), jnp.int32)
    for r in range(8):
        ends = jnp.where(table_lane == r, lengths[first_request + r], ends)
    caps[...] = jnp.clip(ends - BLK * lax.broadcasted_iota(jnp.int32, (64, HD), 0), 0, BLK)
    token = lax.broadcasted_iota(jnp.int32, (BLK, HD), 0)

    def mask_slot(slot, carry):
        ch, s = slot // 8, slot % 8
        u = ch % 2
        ix = ch // 4
        iy = (ch // 2) % 2
        shift = ((x + 4 - sign * u) % 4) % 2 * sign
        xs = (x + 4 + sign * ix * (2 * u - 1)) % 4
        ys = iy * ring_partner(y, shift) + (1 - iy) * y
        block = (s * 16 + xs * 4 + ys) * 8 + seq
        valid = jnp.sum(jnp.where(table_cols[...] == block, caps[...], 0), axis=0, keepdims=True)
        kbuf[slot, :, HD:] = jnp.where(token < valid, 0.0, MASKED).astype(jnp.bfloat16)
        return carry

    lax.fori_loop(0, SLOTS, mask_slot, 0)
    top[...] = jnp.full_like(top, 2 * MASKED)
    tot[...] = jnp.zeros_like(tot)
    acc[...] = jnp.zeros_like(acc)

    for d in range(3):
        landed(squares_y.at[d], sq_recv.at[1, d])
        square_sums = square_sums + squares_y[d]
    square_cols = jnp.broadcast_to(square_sums[:1], (HD, ROWS)).T
    factor = lax.rsqrt(square_cols[:, :1] / (SHARDS * FEAT) + 1e-5)
    loads[0].wait()
    loads[1].wait()

    def project(t, total):
        feats = pl.ds(pl.multiple_of(t * FEAT, FEAT), FEAT)
        normed = (
            hbuf[t].astype(jnp.float32) * factor * gain[:, feats].astype(jnp.float32)
        ).astype(jnp.bfloat16)
        return total + jnp.dot(normed, wqkv[feats, :], preferred_element_type=jnp.float32)

    def project_line(i, total):
        along = i // 4
        d = i % 4
        return project((x + (1 - along) * d) % 4 * 4 + (y + along * d) % 4, total)

    def project_far(i, total):
        shard = (x + 1 + i // 3) % 4 * 4 + (y + 1 + i % 3) % 4
        landed(hbuf.at[shard, top_rows], ag_recv.at[shard, 0])
        landed(hbuf.at[shard, low_rows], ag_recv.at[shard, 1])
        return project(shard, total)

    projected = lax.fori_loop(0, 4, project_line, jnp.zeros((ROWS, 512), jnp.float32))
    projected = lax.fori_loop(5, 8, project_line, projected)
    projected = lax.fori_loop(0, 9, project_far, projected).astype(jnp.bfloat16)
    for h in range(HEADS):
        qown[h] = projected[:, h * HD : (h + 1) * HD]
    kvown[tp % 2] = projected[:, HEADS * HD :]

    own_copy = remote(
        kvown.at[tp % 2], kvown.at[tp % 2], own_send, own_recv.at[tp % 2], seq, tp + 1 - 2 * (tp % 2)
    )
    own_half = tp % 2

    def q_copies(u, j):
        t = (x + 4 + sign * u) % 4 * 4 + (y // 2 * 2 + j + 4 + x % 2 * sign) % 4
        dst = qaug.at[u, pl.ds(own_half * HEADS, HEADS), :, pl.ds(0, HD)]
        there = remote(qown, dst, q_send.at[u, j], q_recv.at[u, own_half], seq, t)
        here = pltpu.make_async_copy(qown, dst, q_recv.at[u, own_half])
        return t == tp, here, there

    for u in range(2):
        for j in range(2):
            same, here, there = q_copies(u, j)
            pl.when(same)(here.start)
            pl.when(jnp.logical_not(same))(there.start)
    own_copy.start()
    for u in range(2):
        for part_half in range(2):
            dst = qaug.at[u, pl.ds(part_half * HEADS, HEADS), :, pl.ds(0, HD)]
            pltpu.make_async_copy(dst, dst, q_recv.at[u, part_half]).wait()

    def o_copies(u, to):
        kx = (x + 4 - sign * u) % 4
        shift = kx % 2 * sign
        yy = (y + 4 - shift) % 4
        t = kx * 4 + yy // 2 * 2 + to
        index = u * 2 + yy % 2
        o_src, o_dst = osend.at[u, to], orecv.at[index]
        s_src = ssend.at[u, to]
        s_dst = srecv.at[pl.ds(pl.multiple_of(index * 8, 8), 8)]
        return (
            t == tp,
            pltpu.make_async_copy(o_src, o_dst, o_recv.at[index]),
            remote(o_src, o_dst, o_send.at[u, to], o_recv.at[index], seq, t),
            pltpu.make_async_copy(s_src, s_dst, s_recv.at[index]),
            remote(s_src, s_dst, s_send.at[u, to], s_recv.at[index], seq, t),
        )

    srecv[pl.ds(32, 96), :] = jnp.zeros((96, ROWS), jnp.float32)

    def send_partials(u):
        for to in range(2):
            stats = jnp.zeros((ROWS, HD), jnp.float32)
            for h in range(HEADS):
                rows = pl.ds((to * HEADS + h) * ROWS, ROWS)
                stats = jnp.where(lane == h, top[u, rows, :], stats)
                stats = jnp.where(lane == HEADS + h, tot[u, rows, :], stats)
                osend[u, to, h] = acc[u, rows, :].astype(jnp.bfloat16)
            ssend[u, to] = stats.T[:8]
            same, o_here_copy, o_there, s_here_copy, s_there = o_copies(u, to)

            @pl.when(same)
            def _():
                o_here_copy.start()
                s_here_copy.start()

            @pl.when(jnp.logical_not(same))
            def _():
                o_there.start()
                s_there.start()

    def attend_chunk(ch, carry):
        u = ch % 2
        slots = pl.ds(pl.multiple_of(ch * CHUNK, CHUNK), CHUNK)
        k_dst = kbuf.at[slots, :, pl.ds(0, HD)]
        pltpu.make_async_copy(k_dst, k_dst, k_recv.at[ch]).wait()
        pltpu.make_async_copy(vbuf.at[slots], vbuf.at[slots], v_recv.at[ch]).wait()

        keys = kbuf[slots].reshape(CHUNK * BLK, 2 * HD)
        values = vbuf[slots].reshape(CHUNK * BLK, HD)
        scores = lax.dot_general(
            qaug[u].reshape(2 * HEADS * ROWS, 2 * HD),
            keys,
            (((1,), (1,)), ((), ())),
            preferred_element_type=jnp.float32,
        )
        old = top[u]
        new = jnp.maximum(old, jnp.max(scores, axis=1, keepdims=True))
        shrink = jnp.exp2((old - new) * LOG2_SCALE)
        weights = jnp.exp2(scores * LOG2_SCALE - new[:, :1] * LOG2_SCALE)
        top[u] = new
        tot[u] = tot[u] * shrink + jnp.sum(weights, axis=1, keepdims=True)
        acc[u] = acc[u] * shrink + jnp.dot(
            weights.astype(jnp.bfloat16), values, preferred_element_type=jnp.float32
        )

        @pl.when(ch >= CHUNKS - 2)
        def _():
            send_partials(u)

        return carry

    lax.fori_loop(0, CHUNKS, attend_chunk, 0)

    own_copy.wait_send()
    other = 1 - tp % 2
    pltpu.make_async_copy(kvown.at[other], kvown.at[other], own_recv.at[other]).wait()
    own_key = kvown[0].astype(jnp.float32)
    own_value = kvown[1].astype(jnp.float32)
    self_scores = [
        jnp.sum(qown[h].astype(jnp.float32) * own_key, axis=1, keepdims=True) for h in range(HEADS)
    ]
    for i in range(4):
        pltpu.make_async_copy(orecv.at[i], orecv.at[i], o_recv.at[i]).wait()
        s_dst = srecv.at[pl.ds(i * 8, 8)]
        pltpu.make_async_copy(s_dst, s_dst, s_recv.at[i]).wait()
    stats = srecv[...].T
    for h in range(HEADS):
        tops = [stats[:, i * 8 + h : i * 8 + h + 1] for i in range(4)]
        best = self_scores[h]
        for one in tops:
            best = jnp.maximum(best, one)
        own_weight = jnp.exp2((self_scores[h] - best) * LOG2_SCALE)
        total = own_weight
        numer = own_weight.astype(jnp.bfloat16).astype(jnp.float32) * own_value
        for i in range(4):
            scale = jnp.exp2((tops[i] - best) * LOG2_SCALE)
            total = total + scale * stats[:, i * 8 + HEADS + h : i * 8 + HEADS + h + 1]
            numer = numer + scale * orecv[i, h].astype(jnp.float32)
        att[:, h * HD : (h + 1) * HD] = (numer / total).astype(jnp.bfloat16)

    loads[2].wait()

    def columns(tile, first=0):
        return pl.ds(pl.multiple_of(first + tile * TILE, TILE), TILE)

    def project_out(tile, carry):
        for side in range(2):
            cols = columns(tile, side * TILES * TILE)
            part[:, :, :, cols] = (
                jnp.dot(att[...], wo[:, cols], preferred_element_type=jnp.float32)
                .astype(jnp.bfloat16)
                .reshape(4, 4, 16, TILE)
            )
            for d in (1, 3, 2):
                if side == 0:
                    src, t = part.at[(x + d) % 4, :, :, cols], (x + d) % 4 * 4 + y
                else:
                    src, t = part.at[:, (y + d) % 4, :, cols], x * 4 + (y + d) % 4
                dst = (rs_a, rs_b)[side].at[d - 1, :, :, columns(tile)]
                remote(
                    src, dst, rs1_send.at[side], rs1_recv.at[side, tile, d - 1], seq, t
                ).start()
        return carry

    lax.fori_loop(0, TILES, project_out, 0)

    def sum_first(tile, carry):
        for side in range(2):
            cols = columns(tile, side * TILES * TILE)
            here = columns(tile)
            landed = (rs_a, rs_b)[side]
            mid = (mid_a, mid_b)[side]
            if side == 0:
                total = part[x, :, :, cols].astype(jnp.float32)
            else:
                total = part[:, y, :, cols].astype(jnp.float32)
            for d in range(3):
                dst = landed.at[d, :, :, here]
                pltpu.make_async_copy(dst, dst, rs1_recv.at[side, tile, d]).wait()
                total = total + landed[d, :, :, here].astype(jnp.float32)
            mid[:, :, here] = total.astype(jnp.bfloat16)
            for d in (1, 3, 2):
                if side == 0:
                    src, t = mid.at[(y + d) % 4, :, here], x * 4 + (y + d) % 4
                else:
                    src, t = mid.at[(x + d) % 4, :, here], (x + d) % 4 * 4 + y
                dst = (fin_a, fin_b)[side].at[d - 1, :, here]
                remote(
                    src, dst, rs2_send.at[side], rs2_recv.at[side, tile, d - 1], seq, t
                ).start()
        return carry

    lax.fori_loop(0, TILES, sum_first, 0)

    def sum_last(tile, carry):
        for side in range(2):
            here = columns(tile)
            landed = (fin_a, fin_b)[side]
            if side == 0:
                total = mid_a[y, :, here].astype(jnp.float32)
            else:
                total = mid_b[x, :, here].astype(jnp.float32)
            for d in range(3):
                dst = landed.at[d, :, here]
                pltpu.make_async_copy(dst, dst, rs2_recv.at[side, tile, d]).wait()
                total = total + landed[d, :, here].astype(jnp.float32)
            out[:, columns(tile, side * TILES * TILE)] = total.astype(jnp.bfloat16)
        return carry

    lax.fori_loop(0, TILES, sum_last, 0)

    for i in range(2):
        landed((squares_x, squares_y)[i], sq_send.at[i])
    sent = hbuf.at[pl.ds(0, SHARDS - 1)]
    pltpu.make_async_copy(sent, sent, ag_send).wait()
    sent = kbuf.at[pl.ds(0, SLOTS - 2), :, pl.ds(0, HD)]
    pltpu.make_async_copy(sent, sent, kv_send.at[0]).wait()
    sent = vbuf.at[pl.ds(0, SLOTS - 2)]
    pltpu.make_async_copy(sent, sent, kv_send.at[1]).wait()
    for u in range(2):
        for j in range(2):
            same, _, there = q_copies(u, j)
            pl.when(jnp.logical_not(same))(there.wait_send)
            same, _, o_there, _, s_there = o_copies(u, j)

            @pl.when(jnp.logical_not(same))
            def _():
                o_there.wait_send()
                s_there.wait_send()

    for side in range(2):
        sent = (rs_a, rs_b)[side]
        pltpu.make_async_copy(sent, sent, rs1_send.at[side]).wait()
        sent = (fin_a, fin_b)[side]
        pltpu.make_async_copy(sent, sent, rs2_send.at[side]).wait()


def per_device(
    hidden_in,
    norm_gain,
    w_query,
    w_keyval,
    w_out,
    key_pool,
    value_pool,
    block_table,
    prefix_lengths,
    row_request,
):
    bf16, f32 = jnp.bfloat16, jnp.float32
    vmem = functools.partial(pltpu.VMEM)
    dma = pltpu.SemaphoreType.DMA
    any_spec = pl.BlockSpec(memory_space=pl.ANY)
    vmem_spec = pl.BlockSpec(memory_space=pltpu.VMEM)
    smem_spec = pl.BlockSpec(memory_space=pltpu.SMEM)
    return pl.pallas_call(
        body,
        out_shape=jax.ShapeDtypeStruct((16, 6144), bf16),
        in_specs=[any_spec, vmem_spec] + [any_spec] * 5 + [vmem_spec, smem_spec, vmem_spec],
        out_specs=vmem_spec,
        scratch_shapes=[
            vmem((SHARDS, ROWS, FEAT), bf16),
            vmem((SHARDS * FEAT, 512), bf16),
            vmem((FEAT, 6144), bf16),
            vmem((SLOTS, BLK, 2 * HD), bf16),
            vmem((SLOTS, BLK, HD), bf16),
            vmem((2, 2 * HEADS, ROWS, 2 * HD), bf16),
            vmem((HEADS, ROWS, HD), bf16),
            vmem((2, ROWS, HD), bf16),
            vmem((2, 2 * HEADS * ROWS, HD), f32),
            vmem((2, 2 * HEADS * ROWS, HD), f32),
            vmem((2, 2 * HEADS * ROWS, HD), f32),
            vmem((2, 2, HEADS, ROWS, HD), bf16),
            vmem((2, 2, 8, ROWS), f32),
            vmem((4, HEADS, ROWS, HD), bf16),
            vmem((128, ROWS), f32),
            vmem((8, ROWS), f32),
            vmem((3, 8, ROWS), f32),
            vmem((8, ROWS), f32),
            vmem((3, 8, ROWS), f32),
            vmem((HD, HD), jnp.int32),
            vmem((64, HD), jnp.int32),
            vmem((64, HD), jnp.int32),
            vmem((ROWS, FEAT), bf16),
            vmem((4, 4, 16, 6144), bf16),
            vmem((3, 4, 16, 3072), bf16),
            vmem((3, 4, 16, 3072), bf16),
            vmem((4, 16, 3072), bf16),
            vmem((4, 16, 3072), bf16),
            vmem((3, 16, 3072), bf16),
            vmem((3, 16, 3072), bf16),
            dma((4,)),
            pltpu.SemaphoreType.REGULAR,
            pltpu.SemaphoreType.REGULAR,
            dma((2,)),
            dma((2, 3)),
            dma,
            dma((SHARDS, 2)),
            dma((2,)),
            dma((CHUNKS,)),
            dma((CHUNKS,)),
            dma((2, 2)),
            dma((2, 2)),
            dma,
            dma((2,)),
            dma((2, 2)),
            dma((4,)),
            dma((2, 2)),
            dma((4,)),
            dma((2,)),
            dma((2, TILES, 3)),
            dma((2,)),
            dma((2, TILES, 3)),
        ],
        compiler_params=pltpu.CompilerParams(
            collective_id=0, has_side_effects=True, vmem_limit_bytes=60 << 20
        ),
        cost_estimate=pl.CostEstimate(
            flops=10_000_000_000, bytes_accessed=20_000_000, transcendentals=13_000_000
        ),
    )(
        hidden_in,
        norm_gain.reshape(1, SHARDS * FEAT),
        w_query,
        w_keyval,
        w_out,
        key_pool,
        value_pool,
        block_table,
        prefix_lengths,
        row_request.reshape(1, ROWS),
    )


def solution(mesh):
    return jax.shard_map(
        per_device,
        mesh=mesh,
        in_specs=(
            P("seq", "tp"),
            P(),
            P(None, "tp"),
            P(None, "tp"),
            P("tp", None),
            P(("seq", "tp"), None, None),
            P(("seq", "tp"), None, None),
            P(),
            P(),
            P("seq"),
        ),
        out_specs=P(("seq", "tp"), None),
        check_vma=False,
    )
```

```python
import functools

import jax
import jax.numpy as jnp
from jax import lax
from jax.experimental import pallas as pl
from jax.experimental.pallas import tpu as pltpu
from jax.sharding import PartitionSpec as P

MESH = pl.DeviceIdType.MESH
HD = 128
BLK = 128
ROWS = 256
FEAT = 384
SHARDS = 16
HEADS = 3
SLOTS = 64
CHUNK = 8
CHUNKS = 8
STAGED = 6
TILE = 512
TILES = 6
MASKED = -1e30
LOG2_SCALE = 1.4426950408889634 / HD**0.5


def ring_partner(y, shift):
    return (7 - (y + 4 - shift) % 4 + shift) % 4


def body(
    hidden,
    gain,
    w_query,
    w_keyval,
    w_out,
    key_pool,
    value_pool,
    table,
    lengths,
    row_req,
    out,
    hbuf,
    wqkv,
    wo,
    kbuf,
    vbuf,
    kstage,
    vstage,
    qaug,
    qown,
    kvown,
    acc,
    top,
    tot,
    osend,
    ssend,
    orecv,
    srecv,
    squares_own,
    squares_x,
    squares_mid,
    squares_y,
    table_wide,
    table_cols,
    caps,
    att,
    part,
    rs_a,
    rs_b,
    mid_a,
    mid_b,
    fin_a,
    fin_b,
    load_sem,
    plane_sem,
    sq_send,
    sq_recv,
    ag_send,
    ag_recv,
    kv_send,
    leg_send,
    k_stage,
    v_stage,
    k_recv,
    v_recv,
    q_send,
    q_recv,
    own_send,
    own_recv,
    o_send,
    o_recv,
    s_send,
    s_recv,
    rs1_send,
    rs1_recv,
    rs2_send,
    rs2_recv,
):
    seq = lax.axis_index("seq")
    tp = lax.axis_index("tp")
    x, y = tp // 4, tp % 4
    sign = 1 - 2 * (seq % 2)

    def remote(src, dst, send, recv, s, t):
        return pltpu.make_async_remote_copy(
            src, dst, send, recv, device_id=(s, t), device_id_type=MESH
        )

    def signal(sem, s, t):
        pl.semaphore_signal(sem, inc=1, device_id=(s, t), device_id_type=MESH)

    def x_peer(d):
        return (x + d) % 4 * 4 + y

    def y_peer(d):
        return x * 4 + (y + d) % 4

    barrier = pltpu.get_barrier_semaphore()
    for d in (1, 3, 2):
        signal(barrier, seq, x_peer(d))
        signal(barrier, seq, y_peer(d))
    for i in range(1, 8):
        signal(barrier, (seq + i) % 8, tp)

    own_load = pltpu.make_async_copy(hidden, hbuf.at[tp], load_sem.at[0])
    own_load.start()
    loads = [
        pltpu.make_async_copy(w_query, wqkv.at[:, pl.ds(0, 384)], load_sem.at[1]),
        pltpu.make_async_copy(w_keyval, wqkv.at[:, pl.ds(384, 128)], load_sem.at[2]),
        pltpu.make_async_copy(w_out, wo, load_sem.at[3]),
    ]
    for load in loads:
        load.start()
    own_load.wait()
    wide = hbuf[tp].astype(jnp.float32)
    own_sum = jnp.broadcast_to(jnp.sum(wide * wide, axis=1, keepdims=True), (ROWS, HD))
    squares_own[...] = own_sum.T[:8]
    pl.semaphore_wait(barrier, 13)
    signal(plane_sem, seq, x_peer(1))
    signal(plane_sem, seq, x_peer(3))

    half = ROWS // 2
    for d in (1, 3, 2):
        remote(
            squares_own, squares_x.at[d - 1], sq_send.at[0], sq_recv.at[0, d - 1], seq, x_peer(d)
        ).start()
    for d in (1, 3, 2):
        remote(hbuf.at[tp], hbuf.at[tp], ag_send, ag_recv.at[tp, 0], seq, x_peer(d)).start()
        remote(hbuf.at[tp], hbuf.at[tp], ag_send, ag_recv.at[tp, 0], seq, y_peer(d)).start()

    def place(ch):
        pair = ch // 2
        return ch % 2, (pair + 1) // 2 % 2, (pair + 1) % 2

    def send_stage(ch, carry):
        u, ix, iy = place(ch)
        back = u + ix * (3 - 2 * u)

        def send_one(i, c):
            g = (seq + i) % 8
            turn = 1 - 2 * (g % 2)
            kx = (x + 4 - turn * back) % 4
            shift = (kx % 2) * turn
            ky = ((y + 4 - shift) % 4 // 2 + iy) % 2
            lanes = pl.ds(pl.multiple_of((2 * kx + ky) * HD, HD), HD)
            k_src, v_src = key_pool.at[g, :, lanes], value_pool.at[g, :, lanes]

            def send(k_dst, v_dst):
                @pl.when(i == 0)
                def _():
                    pltpu.make_async_copy(k_src, k_dst, k_stage.at[ch]).start()
                    pltpu.make_async_copy(v_src, v_dst, v_stage.at[ch]).start()

                @pl.when(i != 0)
                def _():
                    remote(k_src, k_dst, kv_send.at[0], k_stage.at[ch], g, tp).start()
                    remote(v_src, v_dst, kv_send.at[1], v_stage.at[ch], g, tp).start()

            @pl.when(ch < STAGED)
            def _():
                send(kstage.at[ch, seq], vstage.at[ch, seq])

            @pl.when(ch >= STAGED)
            def _():
                slot = ch * CHUNK + seq
                send(kbuf.at[slot, :, pl.ds(0, HD)], vbuf.at[slot])

            return c

        return lax.fori_loop(0, 8, send_one, carry)

    lax.fori_loop(0, 4, send_stage, 0)

    def landed(ref, sem):
        pltpu.make_async_copy(ref, ref, sem).wait()

    square_sums = squares_own[...]
    for d in range(3):
        landed(squares_x.at[d], sq_recv.at[0, d])
        square_sums = square_sums + squares_x[d]
    squares_mid[...] = square_sums
    for d in (1, 3, 2):
        remote(
            squares_mid, squares_y.at[d - 1], sq_send.at[1], sq_recv.at[1, d - 1], seq, y_peer(d)
        ).start()

    def send_leg(ch, carry):
        u, ix, iy = place(ch)
        kx = (x + 4 - sign * (u + ix * (3 - 2 * u))) % 4
        shift = (kx % 2) * sign
        xd = (kx + 4 + sign * u) % 4
        yd = iy * ring_partner(y, shift) + (1 - iy) * y
        slots = pl.ds(pl.multiple_of(ch * CHUNK, CHUNK), CHUNK)
        dest = xd * 4 + yd
        landed(kstage.at[ch], k_stage.at[ch])
        landed(vstage.at[ch], v_stage.at[ch])
        k_dst = kbuf.at[slots, :, pl.ds(0, HD)]
        remote(kstage.at[ch], k_dst, leg_send.at[0], k_recv.at[ch], seq, dest).start()
        remote(vstage.at[ch], vbuf.at[slots], leg_send.at[1], v_recv.at[ch], seq, dest).start()
        return carry

    top_rows, low_rows = pl.ds(0, half), pl.ds(half, half)
    for d in (1, 3, 2):
        from_x = x_peer(4 - d)
        landed(hbuf.at[from_x], ag_recv.at[from_x, 0])
        for e in (1, 3, 2):
            remote(
                hbuf.at[from_x, top_rows], hbuf.at[from_x, top_rows],
                ag_send, ag_recv.at[from_x, 0], seq, y_peer(e),
            ).start()
        from_y = y_peer(4 - d)
        landed(hbuf.at[from_y], ag_recv.at[from_y, 0])
        for e in (1, 3, 2):
            remote(
                hbuf.at[from_y, low_rows], hbuf.at[from_y, low_rows],
                ag_send, ag_recv.at[from_y, 1], seq, x_peer(e),
            ).start()

    pl.semaphore_wait(plane_sem, 2)

    lane = lax.broadcasted_iota(jnp.int32, (ROWS, HD), 1)
    first_request = seq // 2 * 8
    requests = jnp.broadcast_to(row_req[...], (HD, ROWS)).T
    onehot = jnp.where(requests == lane + first_request, 1.0, 0.0).astype(jnp.bfloat16)
    for u in range(2):
        for h in range(2 * HEADS):
            qaug[u, h, :, HD:] = onehot
    table_wide[...] = jnp.full_like(table_wide, -1)
    table_wide[:8, :64] = table[pl.ds(pl.multiple_of(first_request, 8), 8), :]
    table_cols[...] = table_wide[...].T[:64]
    table_lane = lax.broadcasted_iota(jnp.int32, (64, HD), 1)
    ends = jnp.zeros((64, HD), jnp.int32)
    for r in range(8):
        ends = jnp.where(table_lane == r, lengths[first_request + r], ends)
    caps[...] = jnp.clip(ends - BLK * lax.broadcasted_iota(jnp.int32, (64, HD), 0), 0, BLK)
    token = lax.broadcasted_iota(jnp.int32, (BLK, HD), 0)

    def mask_slot(slot, carry):
        ch, s = slot // 8, slot % 8
        u, ix, iy = place(ch)
        shift = ((x + 4 - sign * u) % 4) % 2 * sign
        xs = (x + 4 + sign * ix * (2 * u - 1)) % 4
        ys = iy * ring_partner(y, shift) + (1 - iy) * y
        block = (s * 16 + xs * 4 + ys) * 8 + seq
        valid = jnp.sum(jnp.where(table_cols[...] == block, caps[...], 0), axis=0, keepdims=True)
        kbuf[slot, :, HD:] = jnp.where(token < valid, 0.0, MASKED).astype(jnp.bfloat16)
        return carry

    lax.fori_loop(0, SLOTS, mask_slot, 0)
    top[...] = jnp.full_like(top, 2 * MASKED)
    tot[...] = jnp.zeros_like(tot)
    acc[...] = jnp.zeros_like(acc)

    lax.fori_loop(4, 6, send_stage, 0)
    for d in range(3):
        landed(squares_y.at[d], sq_recv.at[1, d])
        square_sums = square_sums + squares_y[d]
    square_cols = jnp.broadcast_to(square_sums[:1], (HD, ROWS)).T
    factor = lax.rsqrt(square_cols[:, :1] / (SHARDS * FEAT) + 1e-5)
    loads[0].wait()
    loads[1].wait()

    def project(t, total):
        feats = pl.ds(pl.multiple_of(t * FEAT, FEAT), FEAT)
        normed = (
            hbuf[t].astype(jnp.float32) * factor * gain[:, feats].astype(jnp.float32)
        ).astype(jnp.bfloat16)
        return total + jnp.dot(normed, wqkv[feats, :], preferred_element_type=jnp.float32)

    def project_line(i, total):
        along = i // 4
        d = i % 4
        return project((x + (1 - along) * d) % 4 * 4 + (y + along * d) % 4, total)

    def project_far(i, total):
        shard = (x + 1 + i // 3) % 4 * 4 + (y + 1 + i % 3) % 4
        landed(hbuf.at[shard, top_rows], ag_recv.at[shard, 0])
        landed(hbuf.at[shard, low_rows], ag_recv.at[shard, 1])
        return project(shard, total)

    projected = lax.fori_loop(0, 4, project_line, jnp.zeros((ROWS, 512), jnp.float32))
    projected = lax.fori_loop(5, 8, project_line, projected)
    projected = lax.fori_loop(0, 9, project_far, projected).astype(jnp.bfloat16)
    for h in range(HEADS):
        qown[h] = projected[:, h * HD : (h + 1) * HD]
    kvown[tp % 2] = projected[:, HEADS * HD :]

    own_copy = remote(
        kvown.at[tp % 2], kvown.at[tp % 2], own_send, own_recv.at[tp % 2], seq, tp + 1 - 2 * (tp % 2)
    )
    own_half = tp % 2

    def q_copies(u, j):
        t = (x + 4 + sign * u) % 4 * 4 + (y // 2 * 2 + j + 4 + x % 2 * sign) % 4
        dst = qaug.at[u, pl.ds(own_half * HEADS, HEADS), :, pl.ds(0, HD)]
        there = remote(qown, dst, q_send.at[u, j], q_recv.at[u, own_half], seq, t)
        here = pltpu.make_async_copy(qown, dst, q_recv.at[u, own_half])
        return t == tp, here, there

    for u in range(2):
        for j in range(2):
            same, here, there = q_copies(u, j)
            pl.when(same)(here.start)
            pl.when(jnp.logical_not(same))(there.start)
    own_copy.start()
    lax.fori_loop(0, 4, send_leg, 0)
    lax.fori_loop(6, CHUNKS, send_stage, 0)
    for u in range(2):
        for part_half in range(2):
            dst = qaug.at[u, pl.ds(part_half * HEADS, HEADS), :, pl.ds(0, HD)]
            pltpu.make_async_copy(dst, dst, q_recv.at[u, part_half]).wait()

    def o_copies(u, to):
        kx = (x + 4 - sign * u) % 4
        shift = kx % 2 * sign
        yy = (y + 4 - shift) % 4
        t = kx * 4 + yy // 2 * 2 + to
        index = u * 2 + yy % 2
        o_src, o_dst = osend.at[u, to], orecv.at[index]
        s_src = ssend.at[u, to]
        s_dst = srecv.at[pl.ds(pl.multiple_of(index * 8, 8), 8)]
        return (
            t == tp,
            pltpu.make_async_copy(o_src, o_dst, o_recv.at[index]),
            remote(o_src, o_dst, o_send.at[u, to], o_recv.at[index], seq, t),
            pltpu.make_async_copy(s_src, s_dst, s_recv.at[index]),
            remote(s_src, s_dst, s_send.at[u, to], s_recv.at[index], seq, t),
        )

    srecv[pl.ds(32, 96), :] = jnp.zeros((96, ROWS), jnp.float32)

    def send_partials(u):
        for to in range(2):
            stats = jnp.zeros((ROWS, HD), jnp.float32)
            for h in range(HEADS):
                rows = pl.ds((to * HEADS + h) * ROWS, ROWS)
                stats = jnp.where(lane == h, top[u, rows, :], stats)
                stats = jnp.where(lane == HEADS + h, tot[u, rows, :], stats)
                osend[u, to, h] = acc[u, rows, :].astype(jnp.bfloat16)
            ssend[u, to] = stats.T[:8]
            same, o_here_copy, o_there, s_here_copy, s_there = o_copies(u, to)

            @pl.when(same)
            def _():
                o_here_copy.start()
                s_here_copy.start()

            @pl.when(jnp.logical_not(same))
            def _():
                o_there.start()
                s_there.start()

    def attend_chunk(ch, carry):
        u = ch % 2
        slots = pl.ds(pl.multiple_of(ch * CHUNK, CHUNK), CHUNK)

        @pl.when(ch == 1)
        def _():
            lax.fori_loop(4, STAGED, send_leg, 0)

        k_dst = kbuf.at[slots, :, pl.ds(0, HD)]

        @pl.when(ch < STAGED)
        def _():
            landed(k_dst, k_recv.at[ch])
            landed(vbuf.at[slots], v_recv.at[ch])

        @pl.when(ch >= STAGED)
        def _():
            landed(k_dst, k_stage.at[ch])
            landed(vbuf.at[slots], v_stage.at[ch])

        keys = kbuf[slots].reshape(CHUNK * BLK, 2 * HD)
        values = vbuf[slots].reshape(CHUNK * BLK, HD)
        scores = lax.dot_general(
            qaug[u].reshape(2 * HEADS * ROWS, 2 * HD),
            keys,
            (((1,), (1,)), ((), ())),
            preferred_element_type=jnp.float32,
        )
        old = top[u]
        new = jnp.maximum(old, jnp.max(scores, axis=1, keepdims=True))
        shrink = jnp.exp2((old - new) * LOG2_SCALE)
        weights = jnp.exp2(scores * LOG2_SCALE - new[:, :1] * LOG2_SCALE)
        top[u] = new
        tot[u] = tot[u] * shrink + jnp.sum(weights, axis=1, keepdims=True)
        acc[u] = acc[u] * shrink + jnp.dot(
            weights.astype(jnp.bfloat16), values, preferred_element_type=jnp.float32
        )

        @pl.when(ch >= CHUNKS - 2)
        def _():
            send_partials(u)

        return carry

    lax.fori_loop(0, CHUNKS, attend_chunk, 0)

    own_copy.wait_send()
    other = 1 - tp % 2
    pltpu.make_async_copy(kvown.at[other], kvown.at[other], own_recv.at[other]).wait()
    own_key = kvown[0].astype(jnp.float32)
    own_value = kvown[1].astype(jnp.float32)
    self_scores = [
        jnp.sum(qown[h].astype(jnp.float32) * own_key, axis=1, keepdims=True) for h in range(HEADS)
    ]
    for i in range(4):
        pltpu.make_async_copy(orecv.at[i], orecv.at[i], o_recv.at[i]).wait()
        s_dst = srecv.at[pl.ds(i * 8, 8)]
        pltpu.make_async_copy(s_dst, s_dst, s_recv.at[i]).wait()
    stats = srecv[...].T
    for h in range(HEADS):
        tops = [stats[:, i * 8 + h : i * 8 + h + 1] for i in range(4)]
        best = self_scores[h]
        for one in tops:
            best = jnp.maximum(best, one)
        own_weight = jnp.exp2((self_scores[h] - best) * LOG2_SCALE)
        total = own_weight
        numer = own_weight.astype(jnp.bfloat16).astype(jnp.float32) * own_value
        for i in range(4):
            scale = jnp.exp2((tops[i] - best) * LOG2_SCALE)
            total = total + scale * stats[:, i * 8 + HEADS + h : i * 8 + HEADS + h + 1]
            numer = numer + scale * orecv[i, h].astype(jnp.float32)
        att[:, h * HD : (h + 1) * HD] = (numer / total).astype(jnp.bfloat16)

    loads[2].wait()

    def columns(tile, first=0):
        return pl.ds(pl.multiple_of(first + tile * TILE, TILE), TILE)

    def project_out(tile, carry):
        for side in range(2):
            cols = columns(tile, side * TILES * TILE)
            part[:, :, :, cols] = (
                jnp.dot(att[...], wo[:, cols], preferred_element_type=jnp.float32)
                .astype(jnp.bfloat16)
                .reshape(4, 4, 16, TILE)
            )
            for d in (1, 3, 2):
                if side == 0:
                    src, t = part.at[(x + d) % 4, :, :, cols], (x + d) % 4 * 4 + y
                else:
                    src, t = part.at[:, (y + d) % 4, :, cols], x * 4 + (y + d) % 4
                dst = (rs_a, rs_b)[side].at[d - 1, :, :, columns(tile)]
                remote(
                    src, dst, rs1_send.at[side], rs1_recv.at[side, tile, d - 1], seq, t
                ).start()
        return carry

    lax.fori_loop(0, TILES, project_out, 0)

    def sum_first(tile, carry):
        for side in range(2):
            cols = columns(tile, side * TILES * TILE)
            here = columns(tile)
            landed = (rs_a, rs_b)[side]
            mid = (mid_a, mid_b)[side]
            if side == 0:
                total = part[x, :, :, cols].astype(jnp.float32)
            else:
                total = part[:, y, :, cols].astype(jnp.float32)
            for d in range(3):
                dst = landed.at[d, :, :, here]
                pltpu.make_async_copy(dst, dst, rs1_recv.at[side, tile, d]).wait()
                total = total + landed[d, :, :, here].astype(jnp.float32)
            mid[:, :, here] = total.astype(jnp.bfloat16)
            for d in (1, 3, 2):
                if side == 0:
                    src, t = mid.at[(y + d) % 4, :, here], x * 4 + (y + d) % 4
                else:
                    src, t = mid.at[(x + d) % 4, :, here], (x + d) % 4 * 4 + y
                dst = (fin_a, fin_b)[side].at[d - 1, :, here]
                remote(
                    src, dst, rs2_send.at[side], rs2_recv.at[side, tile, d - 1], seq, t
                ).start()
        return carry

    lax.fori_loop(0, TILES, sum_first, 0)

    def sum_last(tile, carry):
        for side in range(2):
            here = columns(tile)
            landed = (fin_a, fin_b)[side]
            if side == 0:
                total = mid_a[y, :, here].astype(jnp.float32)
            else:
                total = mid_b[x, :, here].astype(jnp.float32)
            for d in range(3):
                dst = landed.at[d, :, here]
                pltpu.make_async_copy(dst, dst, rs2_recv.at[side, tile, d]).wait()
                total = total + landed[d, :, here].astype(jnp.float32)
            out[:, columns(tile, side * TILES * TILE)] = total.astype(jnp.bfloat16)
        return carry

    lax.fori_loop(0, TILES, sum_last, 0)

    for i in range(2):
        landed((squares_x, squares_y)[i], sq_send.at[i])
    sent = hbuf.at[pl.ds(0, SHARDS - 1)]
    pltpu.make_async_copy(sent, sent, ag_send).wait()
    for i in range(2):
        landed(vbuf.at[pl.ds(0, SLOTS - CHUNKS)], kv_send.at[i])
        landed(vbuf.at[pl.ds(0, STAGED * CHUNK)], leg_send.at[i])
    for u in range(2):
        for j in range(2):
            same, _, there = q_copies(u, j)
            pl.when(jnp.logical_not(same))(there.wait_send)
            same, _, o_there, _, s_there = o_copies(u, j)

            @pl.when(jnp.logical_not(same))
            def _():
                o_there.wait_send()
                s_there.wait_send()

    for side in range(2):
        sent = (rs_a, rs_b)[side]
        pltpu.make_async_copy(sent, sent, rs1_send.at[side]).wait()
        sent = (fin_a, fin_b)[side]
        pltpu.make_async_copy(sent, sent, rs2_send.at[side]).wait()


def per_device(
    hidden_in,
    norm_gain,
    w_query,
    w_keyval,
    w_out,
    key_pool,
    value_pool,
    block_table,
    prefix_lengths,
    row_request,
):
    bf16, f32 = jnp.bfloat16, jnp.float32
    vmem = functools.partial(pltpu.VMEM)
    dma = pltpu.SemaphoreType.DMA
    any_spec = pl.BlockSpec(memory_space=pl.ANY)
    vmem_spec = pl.BlockSpec(memory_space=pltpu.VMEM)
    smem_spec = pl.BlockSpec(memory_space=pltpu.SMEM)
    return pl.pallas_call(
        body,
        out_shape=jax.ShapeDtypeStruct((16, 6144), bf16),
        in_specs=[any_spec, vmem_spec] + [any_spec] * 5 + [vmem_spec, smem_spec, vmem_spec],
        out_specs=vmem_spec,
        scratch_shapes=[
            vmem((SHARDS, ROWS, FEAT), bf16),
            vmem((SHARDS * FEAT, 512), bf16),
            vmem((FEAT, 6144), bf16),
            vmem((SLOTS, BLK, 2 * HD), bf16),
            vmem((SLOTS, BLK, HD), bf16),
            vmem((STAGED, CHUNK, BLK, HD), bf16),
            vmem((STAGED, CHUNK, BLK, HD), bf16),
            vmem((2, 2 * HEADS, ROWS, 2 * HD), bf16),
            vmem((HEADS, ROWS, HD), bf16),
            vmem((2, ROWS, HD), bf16),
            vmem((2, 2 * HEADS * ROWS, HD), f32),
            vmem((2, 2 * HEADS * ROWS, HD), f32),
            vmem((2, 2 * HEADS * ROWS, HD), f32),
            vmem((2, 2, HEADS, ROWS, HD), bf16),
            vmem((2, 2, 8, ROWS), f32),
            vmem((4, HEADS, ROWS, HD), bf16),
            vmem((128, ROWS), f32),
            vmem((8, ROWS), f32),
            vmem((3, 8, ROWS), f32),
            vmem((8, ROWS), f32),
            vmem((3, 8, ROWS), f32),
            vmem((HD, HD), jnp.int32),
            vmem((64, HD), jnp.int32),
            vmem((64, HD), jnp.int32),
            vmem((ROWS, FEAT), bf16),
            vmem((4, 4, 16, 6144), bf16),
            vmem((3, 4, 16, 3072), bf16),
            vmem((3, 4, 16, 3072), bf16),
            vmem((4, 16, 3072), bf16),
            vmem((4, 16, 3072), bf16),
            vmem((3, 16, 3072), bf16),
            vmem((3, 16, 3072), bf16),
            dma((4,)),
            pltpu.SemaphoreType.REGULAR,
            dma((2,)),
            dma((2, 3)),
            dma,
            dma((SHARDS, 2)),
            dma((2,)),
            dma((2,)),
            dma((CHUNKS,)),
            dma((CHUNKS,)),
            dma((CHUNKS,)),
            dma((CHUNKS,)),
            dma((2, 2)),
            dma((2, 2)),
            dma,
            dma((2,)),
            dma((2, 2)),
            dma((4,)),
            dma((2, 2)),
            dma((4,)),
            dma((2,)),
            dma((2, TILES, 3)),
            dma((2,)),
            dma((2, TILES, 3)),
        ],
        compiler_params=pltpu.CompilerParams(
            collective_id=0, has_side_effects=True, vmem_limit_bytes=60 << 20
        ),
        cost_estimate=pl.CostEstimate(
            flops=10_000_000_000, bytes_accessed=20_000_000, transcendentals=13_000_000
        ),
    )(
        hidden_in,
        norm_gain.reshape(1, SHARDS * FEAT),
        w_query,
        w_keyval,
        w_out,
        key_pool,
        value_pool,
        block_table,
        prefix_lengths,
        row_request.reshape(1, ROWS),
    )


def solution(mesh):
    return jax.shard_map(
        per_device,
        mesh=mesh,
        in_specs=(
            P("seq", "tp"),
            P(),
            P(None, "tp"),
            P(None, "tp"),
            P("tp", None),
            P(("seq", "tp"), None, None),
            P(("seq", "tp"), None, None),
            P(),
            P(),
            P("seq"),
        ),
        out_specs=P(("seq", "tp"), None),
        check_vma=False,
    )
```

```python
import functools

import jax
import jax.numpy as jnp
from jax import lax
from jax.experimental import pallas as pl
from jax.experimental.pallas import tpu as pltpu
from jax.sharding import PartitionSpec as P

MESH = pl.DeviceIdType.MESH
HD = 128
BLK = 128
ROWS = 256
FEAT = 384
SHARDS = 16
HEADS = 3
SLOTS = 64
CHUNK = 8
CHUNKS = 8
STAGED = 6
TILE = 512
TILES = 6
MASKED = -1e30
LOG2_SCALE = 1.4426950408889634 / HD**0.5


def ring_partner(y, shift):
    return (7 - (y + 4 - shift) % 4 + shift) % 4


def body(
    hidden,
    gain,
    w_query,
    w_keyval,
    w_out,
    key_pool,
    value_pool,
    table,
    lengths,
    row_req,
    out,
    hbuf,
    wqkv,
    wo,
    kbuf,
    vbuf,
    kstage,
    vstage,
    qaug,
    qown,
    kvown,
    acc,
    top,
    tot,
    osend,
    ssend,
    orecv,
    srecv,
    squares_own,
    squares_x,
    squares_mid,
    squares_y,
    table_wide,
    table_cols,
    caps,
    att,
    part,
    rs_a,
    rs_b,
    mid_a,
    mid_b,
    fin_a,
    fin_b,
    load_sem,
    plane_sem,
    sq_send,
    sq_recv,
    ag_send,
    ag_recv,
    kv_send,
    leg_send,
    k_stage,
    v_stage,
    k_recv,
    v_recv,
    q_send,
    q_recv,
    own_send,
    own_recv,
    o_send,
    o_recv,
    s_send,
    s_recv,
    rs1_send,
    rs1_recv,
    rs2_send,
    rs2_recv,
):
    seq = lax.axis_index("seq")
    tp = lax.axis_index("tp")
    x, y = tp // 4, tp % 4
    sign = 1 - 2 * (seq % 2)

    def remote(src, dst, send, recv, s, t):
        return pltpu.make_async_remote_copy(
            src, dst, send, recv, device_id=(s, t), device_id_type=MESH
        )

    def signal(sem, s, t):
        pl.semaphore_signal(sem, inc=1, device_id=(s, t), device_id_type=MESH)

    def x_peer(d):
        return (x + d) % 4 * 4 + y

    def y_peer(d):
        return x * 4 + (y + d) % 4

    barrier = pltpu.get_barrier_semaphore()
    for d in (1, 3, 2):
        signal(barrier, seq, x_peer(d))
        signal(barrier, seq, y_peer(d))
    for i in range(1, 8):
        signal(barrier, (seq + i) % 8, tp)

    own_load = pltpu.make_async_copy(hidden, hbuf.at[tp], load_sem.at[0])
    own_load.start()
    loads = [
        pltpu.make_async_copy(w_query, wqkv.at[:, pl.ds(0, 384)], load_sem.at[1]),
        pltpu.make_async_copy(w_keyval, wqkv.at[:, pl.ds(384, 128)], load_sem.at[2]),
        pltpu.make_async_copy(w_out, wo, load_sem.at[3]),
    ]
    for load in loads:
        load.start()
    own_load.wait()
    wide = hbuf[tp].astype(jnp.float32)
    own_sum = jnp.broadcast_to(jnp.sum(wide * wide, axis=1, keepdims=True), (ROWS, HD))
    squares_own[...] = own_sum.T[:8]
    pl.semaphore_wait(barrier, 13)
    signal(plane_sem, seq, x_peer(1))
    signal(plane_sem, seq, x_peer(3))

    half = ROWS // 2
    for d in (1, 3, 2):
        remote(
            squares_own, squares_x.at[d - 1], sq_send.at[0], sq_recv.at[0, d - 1], seq, x_peer(d)
        ).start()
    for d in (1, 3, 2):
        remote(hbuf.at[tp], hbuf.at[tp], ag_send, ag_recv.at[tp, 0], seq, x_peer(d)).start()
        remote(hbuf.at[tp], hbuf.at[tp], ag_send, ag_recv.at[tp, 0], seq, y_peer(d)).start()

    def place(ch):
        pair = ch // 2
        return ch % 2, ((pair + 1) // 2 + 1) % 2, pair // 2

    def is_local(ch):
        return ch // 2 == 1

    def stage(ch):
        return (ch + 6) % 8 % 6

    def send_stage(ch, carry):
        u, ix, iy = place(ch)
        back = u + ix * (3 - 2 * u)

        def send_one(i, c):
            g = (seq + i) % 8
            turn = 1 - 2 * (g % 2)
            kx = (x + 4 - turn * back) % 4
            shift = (kx % 2) * turn
            ky = ((y + 4 - shift) % 4 // 2 + iy) % 2
            lanes = pl.ds(pl.multiple_of((2 * kx + ky) * HD, HD), HD)
            k_src, v_src = key_pool.at[g, :, lanes], value_pool.at[g, :, lanes]

            def send(k_dst, v_dst):
                @pl.when(i == 0)
                def _():
                    pltpu.make_async_copy(k_src, k_dst, k_stage.at[ch]).start()
                    pltpu.make_async_copy(v_src, v_dst, v_stage.at[ch]).start()

                @pl.when(i != 0)
                def _():
                    remote(k_src, k_dst, kv_send.at[0], k_stage.at[ch], g, tp).start()
                    remote(v_src, v_dst, kv_send.at[1], v_stage.at[ch], g, tp).start()

            @pl.when(jnp.logical_not(is_local(ch)))
            def _():
                send(kstage.at[stage(ch), seq], vstage.at[stage(ch), seq])

            @pl.when(is_local(ch))
            def _():
                slot = ch * CHUNK + seq
                send(kbuf.at[slot, :, pl.ds(0, HD)], vbuf.at[slot])

            return c

        return lax.fori_loop(0, 8, send_one, carry)

    lax.fori_loop(0, 4, send_stage, 0)

    def landed(ref, sem):
        pltpu.make_async_copy(ref, ref, sem).wait()

    square_sums = squares_own[...]
    for d in range(3):
        landed(squares_x.at[d], sq_recv.at[0, d])
        square_sums = square_sums + squares_x[d]
    squares_mid[...] = square_sums
    for d in (1, 3, 2):
        remote(
            squares_mid, squares_y.at[d - 1], sq_send.at[1], sq_recv.at[1, d - 1], seq, y_peer(d)
        ).start()

    def send_leg(ch, carry):
        u, ix, iy = place(ch)
        kx = (x + 4 - sign * (u + ix * (3 - 2 * u))) % 4
        shift = (kx % 2) * sign
        xd = (kx + 4 + sign * u) % 4
        yd = iy * ring_partner(y, shift) + (1 - iy) * y
        slots = pl.ds(pl.multiple_of(ch * CHUNK, CHUNK), CHUNK)
        dest = xd * 4 + yd
        landed(kstage.at[stage(ch)], k_stage.at[ch])
        landed(vstage.at[stage(ch)], v_stage.at[ch])
        k_dst = kbuf.at[slots, :, pl.ds(0, HD)]
        remote(kstage.at[stage(ch)], k_dst, leg_send.at[0], k_recv.at[ch], seq, dest).start()
        remote(vstage.at[stage(ch)], vbuf.at[slots], leg_send.at[1], v_recv.at[ch], seq, dest).start()
        return carry

    top_rows, low_rows = pl.ds(0, half), pl.ds(half, half)
    for d in (1, 3, 2):
        from_x = x_peer(4 - d)
        landed(hbuf.at[from_x], ag_recv.at[from_x, 0])
        for e in (1, 3, 2):
            remote(
                hbuf.at[from_x, top_rows], hbuf.at[from_x, top_rows],
                ag_send, ag_recv.at[from_x, 0], seq, y_peer(e),
            ).start()
        from_y = y_peer(4 - d)
        landed(hbuf.at[from_y], ag_recv.at[from_y, 0])
        for e in (1, 3, 2):
            remote(
                hbuf.at[from_y, low_rows], hbuf.at[from_y, low_rows],
                ag_send, ag_recv.at[from_y, 1], seq, x_peer(e),
            ).start()

    pl.semaphore_wait(plane_sem, 2)

    lane = lax.broadcasted_iota(jnp.int32, (ROWS, HD), 1)
    first_request = seq // 2 * 8
    requests = jnp.broadcast_to(row_req[...], (HD, ROWS)).T
    onehot = jnp.where(requests == lane + first_request, 1.0, 0.0).astype(jnp.bfloat16)
    for u in range(2):
        for h in range(2 * HEADS):
            qaug[u, h, :, HD:] = onehot
    table_wide[...] = jnp.full_like(table_wide, -1)
    table_wide[:8, :64] = table[pl.ds(pl.multiple_of(first_request, 8), 8), :]
    table_cols[...] = table_wide[...].T[:64]
    table_lane = lax.broadcasted_iota(jnp.int32, (64, HD), 1)
    ends = jnp.zeros((64, HD), jnp.int32)
    for r in range(8):
        ends = jnp.where(table_lane == r, lengths[first_request + r], ends)
    caps[...] = jnp.clip(ends - BLK * lax.broadcasted_iota(jnp.int32, (64, HD), 0), 0, BLK)
    token = lax.broadcasted_iota(jnp.int32, (BLK, HD), 0)

    def mask_slot(slot, carry):
        ch, s = slot // 8, slot % 8
        u, ix, iy = place(ch)
        shift = ((x + 4 - sign * u) % 4) % 2 * sign
        xs = (x + 4 + sign * ix * (2 * u - 1)) % 4
        ys = iy * ring_partner(y, shift) + (1 - iy) * y
        block = (s * 16 + xs * 4 + ys) * 8 + seq
        valid = jnp.sum(jnp.where(table_cols[...] == block, caps[...], 0), axis=0, keepdims=True)
        kbuf[slot, :, HD:] = jnp.where(token < valid, 0.0, MASKED).astype(jnp.bfloat16)
        return carry

    lax.fori_loop(0, SLOTS, mask_slot, 0)
    top[...] = jnp.full_like(top, 2 * MASKED)
    tot[...] = jnp.zeros_like(tot)
    acc[...] = jnp.zeros_like(acc)

    lax.fori_loop(4, 6, send_stage, 0)
    for d in range(3):
        landed(squares_y.at[d], sq_recv.at[1, d])
        square_sums = square_sums + squares_y[d]
    square_cols = jnp.broadcast_to(square_sums[:1], (HD, ROWS)).T
    factor = lax.rsqrt(square_cols[:, :1] / (SHARDS * FEAT) + 1e-5)
    loads[0].wait()
    loads[1].wait()

    def project(t, total):
        feats = pl.ds(pl.multiple_of(t * FEAT, FEAT), FEAT)
        normed = (
            hbuf[t].astype(jnp.float32) * factor * gain[:, feats].astype(jnp.float32)
        ).astype(jnp.bfloat16)
        return total + jnp.dot(normed, wqkv[feats, :], preferred_element_type=jnp.float32)

    def project_line(i, total):
        along = i // 4
        d = i % 4
        return project((x + (1 - along) * d) % 4 * 4 + (y + along * d) % 4, total)

    def project_far(i, total):
        shard = (x + 1 + i // 3) % 4 * 4 + (y + 1 + i % 3) % 4
        landed(hbuf.at[shard, top_rows], ag_recv.at[shard, 0])
        landed(hbuf.at[shard, low_rows], ag_recv.at[shard, 1])
        return project(shard, total)

    projected = lax.fori_loop(0, 4, project_line, jnp.zeros((ROWS, 512), jnp.float32))
    projected = lax.fori_loop(5, 8, project_line, projected)
    projected = lax.fori_loop(0, 9, project_far, projected).astype(jnp.bfloat16)
    for h in range(HEADS):
        qown[h] = projected[:, h * HD : (h + 1) * HD]
    kvown[tp % 2] = projected[:, HEADS * HD :]

    own_copy = remote(
        kvown.at[tp % 2], kvown.at[tp % 2], own_send, own_recv.at[tp % 2], seq, tp + 1 - 2 * (tp % 2)
    )
    own_half = tp % 2

    def q_copies(u, j):
        t = (x + 4 + sign * u) % 4 * 4 + (y // 2 * 2 + j + 4 + x % 2 * sign) % 4
        dst = qaug.at[u, pl.ds(own_half * HEADS, HEADS), :, pl.ds(0, HD)]
        there = remote(qown, dst, q_send.at[u, j], q_recv.at[u, own_half], seq, t)
        here = pltpu.make_async_copy(qown, dst, q_recv.at[u, own_half])
        return t == tp, here, there

    for u in range(2):
        for j in range(2):
            same, here, there = q_copies(u, j)
            pl.when(same)(here.start)
            pl.when(jnp.logical_not(same))(there.start)
    own_copy.start()
    lax.fori_loop(0, 2, send_leg, 0)
    lax.fori_loop(6, CHUNKS, send_stage, 0)
    for u in range(2):
        for part_half in range(2):
            dst = qaug.at[u, pl.ds(part_half * HEADS, HEADS), :, pl.ds(0, HD)]
            pltpu.make_async_copy(dst, dst, q_recv.at[u, part_half]).wait()

    lax.fori_loop(4, 6, send_leg, 0)

    def o_copies(u, to):
        kx = (x + 4 - sign * u) % 4
        shift = kx % 2 * sign
        yy = (y + 4 - shift) % 4
        t = kx * 4 + yy // 2 * 2 + to
        index = u * 2 + yy % 2
        o_src, o_dst = osend.at[u, to], orecv.at[index]
        s_src = ssend.at[u, to]
        s_dst = srecv.at[pl.ds(pl.multiple_of(index * 8, 8), 8)]
        return (
            t == tp,
            pltpu.make_async_copy(o_src, o_dst, o_recv.at[index]),
            remote(o_src, o_dst, o_send.at[u, to], o_recv.at[index], seq, t),
            pltpu.make_async_copy(s_src, s_dst, s_recv.at[index]),
            remote(s_src, s_dst, s_send.at[u, to], s_recv.at[index], seq, t),
        )

    srecv[pl.ds(32, 96), :] = jnp.zeros((96, ROWS), jnp.float32)

    def send_partials(u):
        for to in range(2):
            stats = jnp.zeros((ROWS, HD), jnp.float32)
            for h in range(HEADS):
                rows = pl.ds((to * HEADS + h) * ROWS, ROWS)
                stats = jnp.where(lane == h, top[u, rows, :], stats)
                stats = jnp.where(lane == HEADS + h, tot[u, rows, :], stats)
                osend[u, to, h] = acc[u, rows, :].astype(jnp.bfloat16)
            ssend[u, to] = stats.T[:8]
            same, o_here_copy, o_there, s_here_copy, s_there = o_copies(u, to)

            @pl.when(same)
            def _():
                o_here_copy.start()
                s_here_copy.start()

            @pl.when(jnp.logical_not(same))
            def _():
                o_there.start()
                s_there.start()

    def attend_chunk(ch, carry):
        u = ch % 2
        slots = pl.ds(pl.multiple_of(ch * CHUNK, CHUNK), CHUNK)

        @pl.when((ch == 2) | (ch == 3))
        def _():
            send_leg(ch + 4, 0)

        k_dst = kbuf.at[slots, :, pl.ds(0, HD)]

        @pl.when(jnp.logical_not(is_local(ch)))
        def _():
            landed(k_dst, k_recv.at[ch])
            landed(vbuf.at[slots], v_recv.at[ch])

        @pl.when(is_local(ch))
        def _():
            landed(k_dst, k_stage.at[ch])
            landed(vbuf.at[slots], v_stage.at[ch])

        keys = kbuf[slots].reshape(CHUNK * BLK, 2 * HD)
        values = vbuf[slots].reshape(CHUNK * BLK, HD)
        scores = lax.dot_general(
            qaug[u].reshape(2 * HEADS * ROWS, 2 * HD),
            keys,
            (((1,), (1,)), ((), ())),
            preferred_element_type=jnp.float32,
        )
        old = top[u]
        new = jnp.maximum(old, jnp.max(scores, axis=1, keepdims=True))
        shrink = jnp.exp2((old - new) * LOG2_SCALE)
        weights = jnp.exp2(scores * LOG2_SCALE - new[:, :1] * LOG2_SCALE)
        top[u] = new
        tot[u] = tot[u] * shrink + jnp.sum(weights, axis=1, keepdims=True)
        acc[u] = acc[u] * shrink + jnp.dot(
            weights.astype(jnp.bfloat16), values, preferred_element_type=jnp.float32
        )

        @pl.when(ch >= CHUNKS - 2)
        def _():
            send_partials(u)

        return carry

    lax.fori_loop(0, CHUNKS, attend_chunk, 0)

    own_copy.wait_send()
    other = 1 - tp % 2
    pltpu.make_async_copy(kvown.at[other], kvown.at[other], own_recv.at[other]).wait()
    own_key = kvown[0].astype(jnp.float32)
    own_value = kvown[1].astype(jnp.float32)
    self_scores = [
        jnp.sum(qown[h].astype(jnp.float32) * own_key, axis=1, keepdims=True) for h in range(HEADS)
    ]
    for i in range(4):
        pltpu.make_async_copy(orecv.at[i], orecv.at[i], o_recv.at[i]).wait()
        s_dst = srecv.at[pl.ds(i * 8, 8)]
        pltpu.make_async_copy(s_dst, s_dst, s_recv.at[i]).wait()
    stats = srecv[...].T
    for h in range(HEADS):
        tops = [stats[:, i * 8 + h : i * 8 + h + 1] for i in range(4)]
        best = self_scores[h]
        for one in tops:
            best = jnp.maximum(best, one)
        own_weight = jnp.exp2((self_scores[h] - best) * LOG2_SCALE)
        total = own_weight
        numer = own_weight.astype(jnp.bfloat16).astype(jnp.float32) * own_value
        for i in range(4):
            scale = jnp.exp2((tops[i] - best) * LOG2_SCALE)
            total = total + scale * stats[:, i * 8 + HEADS + h : i * 8 + HEADS + h + 1]
            numer = numer + scale * orecv[i, h].astype(jnp.float32)
        att[:, h * HD : (h + 1) * HD] = (numer / total).astype(jnp.bfloat16)

    loads[2].wait()

    def columns(tile, first=0):
        return pl.ds(pl.multiple_of(first + tile * TILE, TILE), TILE)

    def project_out(tile, carry):
        for side in range(2):
            cols = columns(tile, side * TILES * TILE)
            part[:, :, :, cols] = (
                jnp.dot(att[...], wo[:, cols], preferred_element_type=jnp.float32)
                .astype(jnp.bfloat16)
                .reshape(4, 4, 16, TILE)
            )
            for d in (1, 3, 2):
                if side == 0:
                    src, t = part.at[(x + d) % 4, :, :, cols], (x + d) % 4 * 4 + y
                else:
                    src, t = part.at[:, (y + d) % 4, :, cols], x * 4 + (y + d) % 4
                dst = (rs_a, rs_b)[side].at[d - 1, :, :, columns(tile)]
                remote(
                    src, dst, rs1_send.at[side], rs1_recv.at[side, tile, d - 1], seq, t
                ).start()
        return carry

    lax.fori_loop(0, TILES, project_out, 0)

    def sum_first(tile, carry):
        for side in range(2):
            cols = columns(tile, side * TILES * TILE)
            here = columns(tile)
            landed = (rs_a, rs_b)[side]
            mid = (mid_a, mid_b)[side]
            if side == 0:
                total = part[x, :, :, cols].astype(jnp.float32)
            else:
                total = part[:, y, :, cols].astype(jnp.float32)
            for d in range(3):
                dst = landed.at[d, :, :, here]
                pltpu.make_async_copy(dst, dst, rs1_recv.at[side, tile, d]).wait()
                total = total + landed[d, :, :, here].astype(jnp.float32)
            mid[:, :, here] = total.astype(jnp.bfloat16)
            for d in (1, 3, 2):
                if side == 0:
                    src, t = mid.at[(y + d) % 4, :, here], x * 4 + (y + d) % 4
                else:
                    src, t = mid.at[(x + d) % 4, :, here], (x + d) % 4 * 4 + y
                dst = (fin_a, fin_b)[side].at[d - 1, :, here]
                remote(
                    src, dst, rs2_send.at[side], rs2_recv.at[side, tile, d - 1], seq, t
                ).start()
        return carry

    lax.fori_loop(0, TILES, sum_first, 0)

    def sum_last(tile, carry):
        for side in range(2):
            here = columns(tile)
            landed = (fin_a, fin_b)[side]
            if side == 0:
                total = mid_a[y, :, here].astype(jnp.float32)
            else:
                total = mid_b[x, :, here].astype(jnp.float32)
            for d in range(3):
                dst = landed.at[d, :, here]
                pltpu.make_async_copy(dst, dst, rs2_recv.at[side, tile, d]).wait()
                total = total + landed[d, :, here].astype(jnp.float32)
            out[:, columns(tile, side * TILES * TILE)] = total.astype(jnp.bfloat16)
        return carry

    lax.fori_loop(0, TILES, sum_last, 0)

    for i in range(2):
        landed((squares_x, squares_y)[i], sq_send.at[i])
    sent = hbuf.at[pl.ds(0, SHARDS - 1)]
    pltpu.make_async_copy(sent, sent, ag_send).wait()
    for i in range(2):
        landed(vbuf.at[pl.ds(0, SLOTS - CHUNKS)], kv_send.at[i])
        landed(vbuf.at[pl.ds(0, STAGED * CHUNK)], leg_send.at[i])
    for u in range(2):
        for j in range(2):
            same, _, there = q_copies(u, j)
            pl.when(jnp.logical_not(same))(there.wait_send)
            same, _, o_there, _, s_there = o_copies(u, j)

            @pl.when(jnp.logical_not(same))
            def _():
                o_there.wait_send()
                s_there.wait_send()

    for side in range(2):
        sent = (rs_a, rs_b)[side]
        pltpu.make_async_copy(sent, sent, rs1_send.at[side]).wait()
        sent = (fin_a, fin_b)[side]
        pltpu.make_async_copy(sent, sent, rs2_send.at[side]).wait()


def per_device(
    hidden_in,
    norm_gain,
    w_query,
    w_keyval,
    w_out,
    key_pool,
    value_pool,
    block_table,
    prefix_lengths,
    row_request,
):
    bf16, f32 = jnp.bfloat16, jnp.float32
    vmem = functools.partial(pltpu.VMEM)
    dma = pltpu.SemaphoreType.DMA
    any_spec = pl.BlockSpec(memory_space=pl.ANY)
    vmem_spec = pl.BlockSpec(memory_space=pltpu.VMEM)
    smem_spec = pl.BlockSpec(memory_space=pltpu.SMEM)
    return pl.pallas_call(
        body,
        out_shape=jax.ShapeDtypeStruct((16, 6144), bf16),
        in_specs=[any_spec, vmem_spec] + [any_spec] * 5 + [vmem_spec, smem_spec, vmem_spec],
        out_specs=vmem_spec,
        scratch_shapes=[
            vmem((SHARDS, ROWS, FEAT), bf16),
            vmem((SHARDS * FEAT, 512), bf16),
            vmem((FEAT, 6144), bf16),
            vmem((SLOTS, BLK, 2 * HD), bf16),
            vmem((SLOTS, BLK, HD), bf16),
            vmem((STAGED, CHUNK, BLK, HD), bf16),
            vmem((STAGED, CHUNK, BLK, HD), bf16),
            vmem((2, 2 * HEADS, ROWS, 2 * HD), bf16),
            vmem((HEADS, ROWS, HD), bf16),
            vmem((2, ROWS, HD), bf16),
            vmem((2, 2 * HEADS * ROWS, HD), f32),
            vmem((2, 2 * HEADS * ROWS, HD), f32),
            vmem((2, 2 * HEADS * ROWS, HD), f32),
            vmem((2, 2, HEADS, ROWS, HD), bf16),
            vmem((2, 2, 8, ROWS), f32),
            vmem((4, HEADS, ROWS, HD), bf16),
            vmem((128, ROWS), f32),
            vmem((8, ROWS), f32),
            vmem((3, 8, ROWS), f32),
            vmem((8, ROWS), f32),
            vmem((3, 8, ROWS), f32),
            vmem((HD, HD), jnp.int32),
            vmem((64, HD), jnp.int32),
            vmem((64, HD), jnp.int32),
            vmem((ROWS, FEAT), bf16),
            vmem((4, 4, 16, 6144), bf16),
            vmem((3, 4, 16, 3072), bf16),
            vmem((3, 4, 16, 3072), bf16),
            vmem((4, 16, 3072), bf16),
            vmem((4, 16, 3072), bf16),
            vmem((3, 16, 3072), bf16),
            vmem((3, 16, 3072), bf16),
            dma((4,)),
            pltpu.SemaphoreType.REGULAR,
            dma((2,)),
            dma((2, 3)),
            dma,
            dma((SHARDS, 2)),
            dma((2,)),
            dma((2,)),
            dma((CHUNKS,)),
            dma((CHUNKS,)),
            dma((CHUNKS,)),
            dma((CHUNKS,)),
            dma((2, 2)),
            dma((2, 2)),
            dma,
            dma((2,)),
            dma((2, 2)),
            dma((4,)),
            dma((2, 2)),
            dma((4,)),
            dma((2,)),
            dma((2, TILES, 3)),
            dma((2,)),
            dma((2, TILES, 3)),
        ],
        compiler_params=pltpu.CompilerParams(
            collective_id=0, has_side_effects=True, vmem_limit_bytes=60 << 20
        ),
        cost_estimate=pl.CostEstimate(
            flops=10_000_000_000, bytes_accessed=20_000_000, transcendentals=13_000_000
        ),
    )(
        hidden_in,
        norm_gain.reshape(1, SHARDS * FEAT),
        w_query,
        w_keyval,
        w_out,
        key_pool,
        value_pool,
        block_table,
        prefix_lengths,
        row_request.reshape(1, ROWS),
    )


def solution(mesh):
    return jax.shard_map(
        per_device,
        mesh=mesh,
        in_specs=(
            P("seq", "tp"),
            P(),
            P(None, "tp"),
            P(None, "tp"),
            P("tp", None),
            P(("seq", "tp"), None, None),
            P(("seq", "tp"), None, None),
            P(),
            P(),
            P("seq"),
        ),
        out_specs=P(("seq", "tp"), None),
        check_vma=False,
    )
```

```python
import functools

import jax
import jax.numpy as jnp
from jax import lax
from jax.experimental import pallas as pl
from jax.experimental.pallas import tpu as pltpu
from jax.sharding import PartitionSpec as P

MESH = pl.DeviceIdType.MESH
HD = 128
BLK = 128
ROWS = 256
FEAT = 384
SHARDS = 16
HEADS = 3
SLOTS = 64
CHUNK = 8
CHUNKS = 8
STAGED = 6
TILE = 512
TILES = 6
MASKED = -1e30
LOG2_SCALE = 1.4426950408889634 / HD**0.5


def ring_partner(y, shift):
    return (7 - (y + 4 - shift) % 4 + shift) % 4


def body(
    hidden,
    gain,
    w_query,
    w_keyval,
    w_out,
    key_pool,
    value_pool,
    table,
    lengths,
    row_req,
    out,
    hbuf,
    wqkv,
    wo,
    kbuf,
    vbuf,
    kstage,
    vstage,
    qaug,
    qown,
    kvown,
    acc,
    top,
    tot,
    osend,
    ssend,
    orecv,
    srecv,
    squares_own,
    squares_x,
    squares_mid,
    squares_y,
    table_wide,
    table_cols,
    caps,
    att,
    part,
    rs_a,
    rs_b,
    via_a,
    via_b,
    mid_a,
    mid_b,
    fin_a,
    fin_b,
    load_sem,
    plane_sem,
    sq_send,
    sq_recv,
    ag_send,
    ag_recv,
    kv_send,
    leg_send,
    k_stage,
    v_stage,
    k_recv,
    v_recv,
    q_send,
    q_recv,
    own_send,
    own_recv,
    o_send,
    o_recv,
    s_send,
    s_recv,
    via_send,
    via_recv,
    rs1_send,
    rs1_recv,
    rs2_send,
    rs2_recv,
):
    seq = lax.axis_index("seq")
    tp = lax.axis_index("tp")
    x, y = tp // 4, tp % 4
    sign = 1 - 2 * (seq % 2)

    def remote(src, dst, send, recv, s, t):
        return pltpu.make_async_remote_copy(
            src, dst, send, recv, device_id=(s, t), device_id_type=MESH
        )

    def signal(sem, s, t):
        pl.semaphore_signal(sem, inc=1, device_id=(s, t), device_id_type=MESH)

    def x_peer(d):
        return (x + d) % 4 * 4 + y

    def y_peer(d):
        return x * 4 + (y + d) % 4

    barrier = pltpu.get_barrier_semaphore()
    for d in (1, 3, 2):
        signal(barrier, seq, x_peer(d))
        signal(barrier, seq, y_peer(d))
    for i in range(1, 8):
        signal(barrier, (seq + i) % 8, tp)

    own_load = pltpu.make_async_copy(hidden, hbuf.at[tp], load_sem.at[0])
    own_load.start()
    loads = [
        pltpu.make_async_copy(w_query, wqkv.at[:, pl.ds(0, 384)], load_sem.at[1]),
        pltpu.make_async_copy(w_keyval, wqkv.at[:, pl.ds(384, 128)], load_sem.at[2]),
        pltpu.make_async_copy(w_out, wo, load_sem.at[3]),
    ]
    for load in loads:
        load.start()
    own_load.wait()
    wide = hbuf[tp].astype(jnp.float32)
    own_sum = jnp.broadcast_to(jnp.sum(wide * wide, axis=1, keepdims=True), (ROWS, HD))
    squares_own[...] = own_sum.T[:8]
    pl.semaphore_wait(barrier, 13)
    signal(plane_sem, seq, x_peer(1))
    signal(plane_sem, seq, x_peer(3))

    half, quarter = ROWS // 2, ROWS // 4
    for d in (1, 3, 2):
        remote(
            squares_own, squares_x.at[d - 1], sq_send.at[0], sq_recv.at[0, d - 1], seq, x_peer(d)
        ).start()
    def forward(shard, first, rows, index, t):
        block = hbuf.at[shard, pl.ds(first, rows)]
        remote(block, block, ag_send, ag_recv.at[shard, index], seq, t).start()

    for d in (1, 3):
        forward(tp, 0, ROWS, 0, x_peer(d))
        forward(tp, 0, ROWS, 0, y_peer(d))

    def place(ch):
        pair = ch // 2
        return ch % 2, ((pair + 1) // 2 + 1) % 2, pair // 2

    def is_local(ch):
        return ch // 2 == 1

    def stage(ch):
        return (ch + 6) % 8 % 6

    def send_stage(ch, carry):
        u, ix, iy = place(ch)
        back = u + ix * (3 - 2 * u)

        def send_one(i, c):
            g = (seq + i) % 8
            turn = 1 - 2 * (g % 2)
            kx = (x + 4 - turn * back) % 4
            shift = (kx % 2) * turn
            ky = ((y + 4 - shift) % 4 // 2 + iy) % 2
            lanes = pl.ds(pl.multiple_of((2 * kx + ky) * HD, HD), HD)
            k_src, v_src = key_pool.at[g, :, lanes], value_pool.at[g, :, lanes]

            def send(k_dst, v_dst):
                @pl.when(i == 0)
                def _():
                    pltpu.make_async_copy(k_src, k_dst, k_stage.at[ch]).start()
                    pltpu.make_async_copy(v_src, v_dst, v_stage.at[ch]).start()

                @pl.when(i != 0)
                def _():
                    remote(k_src, k_dst, kv_send.at[0], k_stage.at[ch], g, tp).start()
                    remote(v_src, v_dst, kv_send.at[1], v_stage.at[ch], g, tp).start()

            @pl.when(jnp.logical_not(is_local(ch)))
            def _():
                send(kstage.at[stage(ch), seq], vstage.at[stage(ch), seq])

            @pl.when(is_local(ch))
            def _():
                slot = ch * CHUNK + seq
                send(kbuf.at[slot, :, pl.ds(0, HD)], vbuf.at[slot])

            return c

        return lax.fori_loop(0, 8, send_one, carry)

    lax.fori_loop(0, 4, send_stage, 0)

    def landed(ref, sem):
        pltpu.make_async_copy(ref, ref, sem).wait()

    square_sums = squares_own[...]
    for d in range(3):
        landed(squares_x.at[d], sq_recv.at[0, d])
        square_sums = square_sums + squares_x[d]
    squares_mid[...] = square_sums
    for d in (1, 3, 2):
        remote(
            squares_mid, squares_y.at[d - 1], sq_send.at[1], sq_recv.at[1, d - 1], seq, y_peer(d)
        ).start()

    def send_leg(ch, carry):
        u, ix, iy = place(ch)
        kx = (x + 4 - sign * (u + ix * (3 - 2 * u))) % 4
        shift = (kx % 2) * sign
        xd = (kx + 4 + sign * u) % 4
        yd = iy * ring_partner(y, shift) + (1 - iy) * y
        slots = pl.ds(pl.multiple_of(ch * CHUNK, CHUNK), CHUNK)
        dest = xd * 4 + yd
        landed(kstage.at[stage(ch)], k_stage.at[ch])
        landed(vstage.at[stage(ch)], v_stage.at[ch])
        k_dst = kbuf.at[slots, :, pl.ds(0, HD)]
        remote(kstage.at[stage(ch)], k_dst, leg_send.at[0], k_recv.at[ch], seq, dest).start()
        remote(vstage.at[stage(ch)], vbuf.at[slots], leg_send.at[1], v_recv.at[ch], seq, dest).start()
        return carry

    def arrived(shard, first, rows, index):
        landed(hbuf.at[shard, pl.ds(first, rows)], ag_recv.at[shard, index])

    for d in (3, 1):
        shard = x_peer(d)
        arrived(shard, 0, ROWS, 0)
        forward(shard, 0 if d == 3 else half, half, 0 if d == 3 else 1, x_peer(4 - d))
        forward(shard, 0, half, 0, y_peer(1))
        forward(shard, 0, half, 0, y_peer(3))
        shard = y_peer(d)
        arrived(shard, 0, ROWS, 0)
        forward(shard, half if d == 3 else 0, half, 1 if d == 3 else 0, y_peer(4 - d))
        forward(shard, half, half, 2, x_peer(1))
        forward(shard, half, half, 2, x_peer(3))
    shard = x_peer(2)
    arrived(shard, 0, half, 0)
    forward(shard, 0, half, 0, y_peer(1))
    forward(shard, 0, half, 0, y_peer(3))
    shard = y_peer(2)
    arrived(shard, half, half, 1)
    forward(shard, half, half, 2, x_peer(1))
    forward(shard, half, half, 2, x_peer(3))
    for e in (3, 1, 2):
        for d in (3, 1):
            shard = (x + e) % 4 * 4 + (y + d) % 4
            arrived(shard, 0, half, 0)
            forward(shard, 0 if d == 3 else quarter, quarter, 0 if d == 3 else 1, y_peer(4 - d))
            shard = (x + d) % 4 * 4 + (y + e) % 4
            arrived(shard, half, half, 2)
            forward(
                shard, half if d == 3 else half + quarter, quarter, 2 if d == 3 else 3, x_peer(4 - d)
            )

    pl.semaphore_wait(plane_sem, 2)

    lax.fori_loop(4, 6, send_stage, 0)
    for d in range(3):
        landed(squares_y.at[d], sq_recv.at[1, d])
        square_sums = square_sums + squares_y[d]
    square_cols = jnp.broadcast_to(square_sums[:1], (HD, ROWS)).T
    factor = lax.rsqrt(square_cols[:, :1] / (SHARDS * FEAT) + 1e-5)
    loads[0].wait()
    loads[1].wait()

    def project(t, total):
        feats = pl.ds(pl.multiple_of(t * FEAT, FEAT), FEAT)
        normed = (
            hbuf[t].astype(jnp.float32) * factor * gain[:, feats].astype(jnp.float32)
        ).astype(jnp.bfloat16)
        return total + jnp.dot(normed, wqkv[feats, :], preferred_element_type=jnp.float32)

    def project_line(i, total):
        along = i // 4
        d = i % 4
        return project((x + (1 - along) * d) % 4 * 4 + (y + along * d) % 4, total)

    def project_far(i, total):
        return project((x + 1 + i // 3) % 4 * 4 + (y + 1 + i % 3) % 4, total)

    arrived(x_peer(2), half, half, 1)
    arrived(y_peer(2), 0, half, 0)
    projected = lax.fori_loop(0, 4, project_line, jnp.zeros((ROWS, 512), jnp.float32))
    projected = lax.fori_loop(5, 8, project_line, projected)
    for e in (3, 1, 2):
        shard = (x + e) % 4 * 4 + (y + 2) % 4
        arrived(shard, 0, quarter, 0)
        arrived(shard, quarter, quarter, 1)
        shard = (x + 2) % 4 * 4 + (y + e) % 4
        arrived(shard, half, quarter, 2)
        arrived(shard, half + quarter, quarter, 3)
    projected = lax.fori_loop(0, 9, project_far, projected).astype(jnp.bfloat16)
    for h in range(HEADS):
        qown[h] = projected[:, h * HD : (h + 1) * HD]
    kvown[tp % 2] = projected[:, HEADS * HD :]

    own_copy = remote(
        kvown.at[tp % 2], kvown.at[tp % 2], own_send, own_recv.at[tp % 2], seq, tp + 1 - 2 * (tp % 2)
    )
    own_half = tp % 2

    def q_copies(u, j):
        t = (x + 4 + sign * u) % 4 * 4 + (y // 2 * 2 + j + 4 + x % 2 * sign) % 4
        dst = qaug.at[u, pl.ds(own_half * HEADS, HEADS), :, pl.ds(0, HD)]
        there = remote(qown, dst, q_send.at[u, j], q_recv.at[u, own_half], seq, t)
        here = pltpu.make_async_copy(qown, dst, q_recv.at[u, own_half])
        return t == tp, here, there

    for u in range(2):
        for j in range(2):
            same, here, there = q_copies(u, j)
            pl.when(same)(here.start)
            pl.when(jnp.logical_not(same))(there.start)
    own_copy.start()
    lax.fori_loop(0, 2, send_leg, 0)
    lax.fori_loop(6, CHUNKS, send_stage, 0)
    lane = lax.broadcasted_iota(jnp.int32, (ROWS, HD), 1)
    first_request = seq // 2 * 8
    requests = jnp.broadcast_to(row_req[...], (HD, ROWS)).T
    onehot = jnp.where(requests == lane + first_request, 1.0, 0.0).astype(jnp.bfloat16)
    for u in range(2):
        for h in range(2 * HEADS):
            qaug[u, h, :, HD:] = onehot
    table_wide[...] = jnp.full_like(table_wide, -1)
    table_wide[:8, :64] = table[pl.ds(pl.multiple_of(first_request, 8), 8), :]
    table_cols[...] = table_wide[...].T[:64]
    table_lane = lax.broadcasted_iota(jnp.int32, (64, HD), 1)
    ends = jnp.zeros((64, HD), jnp.int32)
    for r in range(8):
        ends = jnp.where(table_lane == r, lengths[first_request + r], ends)
    caps[...] = jnp.clip(ends - BLK * lax.broadcasted_iota(jnp.int32, (64, HD), 0), 0, BLK)
    token = lax.broadcasted_iota(jnp.int32, (BLK, HD), 0)

    def mask_slot(slot, carry):
        ch, s = slot // 8, slot % 8
        u, ix, iy = place(ch)
        shift = ((x + 4 - sign * u) % 4) % 2 * sign
        xs = (x + 4 + sign * ix * (2 * u - 1)) % 4
        ys = iy * ring_partner(y, shift) + (1 - iy) * y
        block = (s * 16 + xs * 4 + ys) * 8 + seq
        valid = jnp.sum(jnp.where(table_cols[...] == block, caps[...], 0), axis=0, keepdims=True)
        kbuf[slot, :, HD:] = jnp.where(token < valid, 0.0, MASKED).astype(jnp.bfloat16)
        return carry

    lax.fori_loop(0, SLOTS, mask_slot, 0)
    top[...] = jnp.full_like(top, 2 * MASKED)
    tot[...] = jnp.zeros_like(tot)
    acc[...] = jnp.zeros_like(acc)

    for u in range(2):
        for part_half in range(2):
            dst = qaug.at[u, pl.ds(part_half * HEADS, HEADS), :, pl.ds(0, HD)]
            pltpu.make_async_copy(dst, dst, q_recv.at[u, part_half]).wait()

    lax.fori_loop(4, 6, send_leg, 0)

    def o_copies(u, to):
        kx = (x + 4 - sign * u) % 4
        shift = kx % 2 * sign
        yy = (y + 4 - shift) % 4
        t = kx * 4 + yy // 2 * 2 + to
        index = u * 2 + yy % 2
        o_src, o_dst = osend.at[u, to], orecv.at[index]
        s_src = ssend.at[u, to]
        s_dst = srecv.at[pl.ds(pl.multiple_of(index * 8, 8), 8)]
        return (
            t == tp,
            pltpu.make_async_copy(o_src, o_dst, o_recv.at[index]),
            remote(o_src, o_dst, o_send.at[u, to], o_recv.at[index], seq, t),
            pltpu.make_async_copy(s_src, s_dst, s_recv.at[index]),
            remote(s_src, s_dst, s_send.at[u, to], s_recv.at[index], seq, t),
        )

    srecv[pl.ds(32, 96), :] = jnp.zeros((96, ROWS), jnp.float32)

    def send_partials(u):
        for to in range(2):
            stats = jnp.zeros((ROWS, HD), jnp.float32)
            for h in range(HEADS):
                rows = pl.ds((to * HEADS + h) * ROWS, ROWS)
                stats = jnp.where(lane == h, top[u, rows, :], stats)
                stats = jnp.where(lane == HEADS + h, tot[u, rows, :], stats)
                osend[u, to, h] = acc[u, rows, :].astype(jnp.bfloat16)
            ssend[u, to] = stats.T[:8]
            same, o_here_copy, o_there, s_here_copy, s_there = o_copies(u, to)

            @pl.when(same)
            def _():
                o_here_copy.start()
                s_here_copy.start()

            @pl.when(jnp.logical_not(same))
            def _():
                o_there.start()
                s_there.start()

    def attend_chunk(ch, carry):
        u = ch % 2
        slots = pl.ds(pl.multiple_of(ch * CHUNK, CHUNK), CHUNK)

        @pl.when((ch == 2) | (ch == 3))
        def _():
            send_leg(ch + 4, 0)

        k_dst = kbuf.at[slots, :, pl.ds(0, HD)]

        @pl.when(jnp.logical_not(is_local(ch)))
        def _():
            landed(k_dst, k_recv.at[ch])
            landed(vbuf.at[slots], v_recv.at[ch])

        @pl.when(is_local(ch))
        def _():
            landed(k_dst, k_stage.at[ch])
            landed(vbuf.at[slots], v_stage.at[ch])

        keys = kbuf[slots].reshape(CHUNK * BLK, 2 * HD)
        values = vbuf[slots].reshape(CHUNK * BLK, HD)
        scores = lax.dot_general(
            qaug[u].reshape(2 * HEADS * ROWS, 2 * HD),
            keys,
            (((1,), (1,)), ((), ())),
            preferred_element_type=jnp.float32,
        )
        old = top[u]
        new = jnp.maximum(old, jnp.max(scores, axis=1, keepdims=True))
        shrink = jnp.exp2((old - new) * LOG2_SCALE)
        weights = jnp.exp2(scores * LOG2_SCALE - new[:, :1] * LOG2_SCALE)
        top[u] = new
        tot[u] = tot[u] * shrink + jnp.sum(weights, axis=1, keepdims=True)
        acc[u] = acc[u] * shrink + jnp.dot(
            weights.astype(jnp.bfloat16), values, preferred_element_type=jnp.float32
        )

        @pl.when(ch >= CHUNKS - 2)
        def _():
            send_partials(u)

        return carry

    lax.fori_loop(0, CHUNKS, attend_chunk, 0)

    own_copy.wait_send()
    other = 1 - tp % 2
    pltpu.make_async_copy(kvown.at[other], kvown.at[other], own_recv.at[other]).wait()
    own_key = kvown[0].astype(jnp.float32)
    own_value = kvown[1].astype(jnp.float32)
    self_scores = [
        jnp.sum(qown[h].astype(jnp.float32) * own_key, axis=1, keepdims=True) for h in range(HEADS)
    ]
    for i in range(4):
        pltpu.make_async_copy(orecv.at[i], orecv.at[i], o_recv.at[i]).wait()
        s_dst = srecv.at[pl.ds(i * 8, 8)]
        pltpu.make_async_copy(s_dst, s_dst, s_recv.at[i]).wait()
    stats = srecv[...].T
    for h in range(HEADS):
        tops = [stats[:, i * 8 + h : i * 8 + h + 1] for i in range(4)]
        best = self_scores[h]
        for one in tops:
            best = jnp.maximum(best, one)
        own_weight = jnp.exp2((self_scores[h] - best) * LOG2_SCALE)
        total = own_weight
        numer = own_weight.astype(jnp.bfloat16).astype(jnp.float32) * own_value
        for i in range(4):
            scale = jnp.exp2((tops[i] - best) * LOG2_SCALE)
            total = total + scale * stats[:, i * 8 + HEADS + h : i * 8 + HEADS + h + 1]
            numer = numer + scale * orecv[i, h].astype(jnp.float32)
        att[:, h * HD : (h + 1) * HD] = (numer / total).astype(jnp.bfloat16)

    loads[2].wait()

    def columns(tile, first=0, width=TILE):
        return pl.ds(pl.multiple_of(first + tile * TILE, TILE // 2), width)

    def half_columns(tile):
        return pl.ds(pl.multiple_of(tile * (TILE // 2), TILE // 2), TILE // 2)

    def first(side):
        return side * TILES * TILE

    def ring_peer(side, d):
        return (x_peer, y_peer)[side](d)

    def ring_block(side, d, cols):
        if side == 0:
            return part.at[(x + d) % 4, :, :, cols]
        return part.at[:, (y + d) % 4, :, cols]

    def project_out(tile, carry):
        for side in range(2):
            cols = columns(tile, side * TILES * TILE)
            part[:, :, :, cols] = (
                jnp.dot(att[...], wo[:, cols], preferred_element_type=jnp.float32)
                .astype(jnp.bfloat16)
                .reshape(4, 4, 16, TILE)
            )
            for d in (1, 3):
                src = ring_block(side, 2, columns(tile, first(side) + (TILE // 2 if d == 3 else 0), TILE // 2))
                dst = (via_a, via_b)[side].at[d // 2, :, :, half_columns(tile)]
                remote(
                    src, dst, via_send.at[side], via_recv.at[side, tile, d // 2], seq, ring_peer(side, d)
                ).start()
        return carry

    lax.fori_loop(0, TILES, project_out, 0)

    def relay(tile, carry):
        for side in range(2):
            via = (via_a, via_b)[side]
            for d in (1, 3):
                passing = via.at[d // 2, :, :, half_columns(tile)]
                landed(passing, via_recv.at[side, tile, d // 2])
                block = ring_block(
                    side, d, columns(tile, first(side) + (TILE // 2 if d == 3 else 0), TILE // 2)
                )
                block[...] = (
                    block[...].astype(jnp.float32) + passing[...].astype(jnp.float32)
                ).astype(jnp.bfloat16)
                remote(
                    ring_block(side, d, columns(tile, first(side))),
                    (rs_a, rs_b)[side].at[d // 2, :, :, columns(tile)],
                    rs1_send.at[side], rs1_recv.at[side, tile, d // 2], seq, ring_peer(side, d),
                ).start()
        return carry

    lax.fori_loop(0, TILES, relay, 0)

    def sum_first(tile, carry):
        for side in range(2):
            here = columns(tile)
            arriving = (rs_a, rs_b)[side]
            mid = (mid_a, mid_b)[side]
            total = ring_block(side, 0, columns(tile, first(side)))[...].astype(jnp.float32)
            for d in range(2):
                dst = arriving.at[d, :, :, here]
                landed(dst, rs1_recv.at[side, tile, d])
                total = total + dst[...].astype(jnp.float32)
            mid[:, :, here] = total.astype(jnp.bfloat16)
            for d in (1, 3, 2):
                if side == 0:
                    src, t = mid.at[(y + d) % 4, :, here], x * 4 + (y + d) % 4
                else:
                    src, t = mid.at[(x + d) % 4, :, here], (x + d) % 4 * 4 + y
                dst = (fin_a, fin_b)[side].at[d - 1, :, here]
                remote(
                    src, dst, rs2_send.at[side], rs2_recv.at[side, tile, d - 1], seq, t
                ).start()
        return carry

    lax.fori_loop(0, TILES, sum_first, 0)

    def sum_last(tile, carry):
        for side in range(2):
            here = columns(tile)
            arriving = (fin_a, fin_b)[side]
            if side == 0:
                total = mid_a[y, :, here].astype(jnp.float32)
            else:
                total = mid_b[x, :, here].astype(jnp.float32)
            for d in range(3):
                dst = arriving.at[d, :, here]
                pltpu.make_async_copy(dst, dst, rs2_recv.at[side, tile, d]).wait()
                total = total + arriving[d, :, here].astype(jnp.float32)
            out[:, columns(tile, side * TILES * TILE)] = total.astype(jnp.bfloat16)
        return carry

    lax.fori_loop(0, TILES, sum_last, 0)

    for i in range(2):
        landed((squares_x, squares_y)[i], sq_send.at[i])
    sent = hbuf.at[pl.ds(0, SHARDS - 1)]
    pltpu.make_async_copy(sent, sent, ag_send).wait()
    for i in range(2):
        landed(vbuf.at[pl.ds(0, SLOTS - CHUNKS)], kv_send.at[i])
        landed(vbuf.at[pl.ds(0, STAGED * CHUNK)], leg_send.at[i])
    for u in range(2):
        for j in range(2):
            same, _, there = q_copies(u, j)
            pl.when(jnp.logical_not(same))(there.wait_send)
            same, _, o_there, _, s_there = o_copies(u, j)

            @pl.when(jnp.logical_not(same))
            def _():
                o_there.wait_send()
                s_there.wait_send()

    for side in range(2):
        landed((via_a, via_b)[side], via_send.at[side])
        sent = (rs_a, rs_b)[side]
        pltpu.make_async_copy(sent, sent, rs1_send.at[side]).wait()
        sent = (fin_a, fin_b)[side]
        pltpu.make_async_copy(sent, sent, rs2_send.at[side]).wait()


def per_device(
    hidden_in,
    norm_gain,
    w_query,
    w_keyval,
    w_out,
    key_pool,
    value_pool,
    block_table,
    prefix_lengths,
    row_request,
):
    bf16, f32 = jnp.bfloat16, jnp.float32
    vmem = functools.partial(pltpu.VMEM)
    dma = pltpu.SemaphoreType.DMA
    any_spec = pl.BlockSpec(memory_space=pl.ANY)
    vmem_spec = pl.BlockSpec(memory_space=pltpu.VMEM)
    smem_spec = pl.BlockSpec(memory_space=pltpu.SMEM)
    return pl.pallas_call(
        body,
        out_shape=jax.ShapeDtypeStruct((16, 6144), bf16),
        in_specs=[any_spec, vmem_spec] + [any_spec] * 5 + [vmem_spec, smem_spec, vmem_spec],
        out_specs=vmem_spec,
        scratch_shapes=[
            vmem((SHARDS, ROWS, FEAT), bf16),
            vmem((SHARDS * FEAT, 512), bf16),
            vmem((FEAT, 6144), bf16),
            vmem((SLOTS, BLK, 2 * HD), bf16),
            vmem((SLOTS, BLK, HD), bf16),
            vmem((STAGED, CHUNK, BLK, HD), bf16),
            vmem((STAGED, CHUNK, BLK, HD), bf16),
            vmem((2, 2 * HEADS, ROWS, 2 * HD), bf16),
            vmem((HEADS, ROWS, HD), bf16),
            vmem((2, ROWS, HD), bf16),
            vmem((2, 2 * HEADS * ROWS, HD), f32),
            vmem((2, 2 * HEADS * ROWS, HD), f32),
            vmem((2, 2 * HEADS * ROWS, HD), f32),
            vmem((2, 2, HEADS, ROWS, HD), bf16),
            vmem((2, 2, 8, ROWS), f32),
            vmem((4, HEADS, ROWS, HD), bf16),
            vmem((128, ROWS), f32),
            vmem((8, ROWS), f32),
            vmem((3, 8, ROWS), f32),
            vmem((8, ROWS), f32),
            vmem((3, 8, ROWS), f32),
            vmem((HD, HD), jnp.int32),
            vmem((64, HD), jnp.int32),
            vmem((64, HD), jnp.int32),
            vmem((ROWS, FEAT), bf16),
            vmem((4, 4, 16, 6144), bf16),
            vmem((2, 4, 16, 3072), bf16),
            vmem((2, 4, 16, 3072), bf16),
            vmem((2, 4, 16, 1536), bf16),
            vmem((2, 4, 16, 1536), bf16),
            vmem((4, 16, 3072), bf16),
            vmem((4, 16, 3072), bf16),
            vmem((3, 16, 3072), bf16),
            vmem((3, 16, 3072), bf16),
            dma((4,)),
            pltpu.SemaphoreType.REGULAR,
            dma((2,)),
            dma((2, 3)),
            dma,
            dma((SHARDS, 4)),
            dma((2,)),
            dma((2,)),
            dma((CHUNKS,)),
            dma((CHUNKS,)),
            dma((CHUNKS,)),
            dma((CHUNKS,)),
            dma((2, 2)),
            dma((2, 2)),
            dma,
            dma((2,)),
            dma((2, 2)),
            dma((4,)),
            dma((2, 2)),
            dma((4,)),
            dma((2,)),
            dma((2, TILES, 2)),
            dma((2,)),
            dma((2, TILES, 2)),
            dma((2,)),
            dma((2, TILES, 3)),
        ],
        compiler_params=pltpu.CompilerParams(
            collective_id=0, has_side_effects=True, vmem_limit_bytes=60 << 20
        ),
        cost_estimate=pl.CostEstimate(
            flops=10_000_000_000, bytes_accessed=20_000_000, transcendentals=13_000_000
        ),
    )(
        hidden_in,
        norm_gain.reshape(1, SHARDS * FEAT),
        w_query,
        w_keyval,
        w_out,
        key_pool,
        value_pool,
        block_table,
        prefix_lengths,
        row_request.reshape(1, ROWS),
    )


def solution(mesh):
    return jax.shard_map(
        per_device,
        mesh=mesh,
        in_specs=(
            P("seq", "tp"),
            P(),
            P(None, "tp"),
            P(None, "tp"),
            P("tp", None),
            P(("seq", "tp"), None, None),
            P(("seq", "tp"), None, None),
            P(),
            P(),
            P("seq"),
        ),
        out_specs=P(("seq", "tp"), None),
        check_vma=False,
    )
```

```python
import functools

import jax
import jax.numpy as jnp
from jax import lax
from jax.experimental import pallas as pl
from jax.experimental.pallas import tpu as pltpu
from jax.sharding import PartitionSpec as P

MESH = pl.DeviceIdType.MESH
HD = 128
BLK = 128
ROWS = 256
FEAT = 384
SHARDS = 16
HEADS = 3
SLOTS = 64
CHUNK = 8
CHUNKS = 8
STAGED = 6
TILE = 512
TILES = 6
MASKED = -1e30
LOG2_SCALE = 1.4426950408889634 / HD**0.5


def ring_partner(y, shift):
    return (7 - (y + 4 - shift) % 4 + shift) % 4


def body(
    hidden,
    gain,
    w_query,
    w_keyval,
    w_out,
    key_pool,
    value_pool,
    table,
    lengths,
    row_req,
    out,
    hbuf,
    wqkv,
    wo,
    kbuf,
    vbuf,
    kstage,
    vstage,
    qaug,
    qown,
    kvown,
    acc,
    top,
    tot,
    osend,
    ssend,
    orecv,
    srecv,
    squares_own,
    squares_x,
    squares_mid,
    squares_y,
    table_wide,
    table_cols,
    caps,
    att,
    part,
    rs_a,
    rs_b,
    via_a,
    via_b,
    mid_a,
    mid_b,
    fin_a,
    fin_b,
    load_sem,
    plane_sem,
    sq_send,
    sq_recv,
    ag_send,
    ag_recv,
    kv_send,
    leg_send,
    k_stage,
    v_stage,
    k_recv,
    v_recv,
    q_send,
    q_recv,
    own_send,
    own_recv,
    o_send,
    o_recv,
    s_send,
    s_recv,
    via_send,
    via_recv,
    rs1_send,
    rs1_recv,
    rs2_send,
    rs2_recv,
):
    seq = lax.axis_index("seq")
    tp = lax.axis_index("tp")
    x, y = tp // 4, tp % 4
    sign = 1 - 2 * (seq % 2)

    def remote(src, dst, send, recv, s, t):
        return pltpu.make_async_remote_copy(
            src, dst, send, recv, device_id=(s, t), device_id_type=MESH
        )

    def signal(sem, s, t):
        pl.semaphore_signal(sem, inc=1, device_id=(s, t), device_id_type=MESH)

    def x_peer(d):
        return (x + d) % 4 * 4 + y

    def y_peer(d):
        return x * 4 + (y + d) % 4

    barrier = pltpu.get_barrier_semaphore()
    for d in (1, 3, 2):
        signal(barrier, seq, x_peer(d))
        signal(barrier, seq, y_peer(d))
    for i in range(1, 8):
        signal(barrier, (seq + i) % 8, tp)

    own_load = pltpu.make_async_copy(hidden, hbuf.at[tp], load_sem.at[0])
    own_load.start()
    loads = [
        pltpu.make_async_copy(w_query, wqkv.at[:, pl.ds(0, 384)], load_sem.at[1]),
        pltpu.make_async_copy(w_keyval, wqkv.at[:, pl.ds(384, 128)], load_sem.at[2]),
        pltpu.make_async_copy(w_out, wo, load_sem.at[3]),
    ]
    for load in loads:
        load.start()
    own_load.wait()
    wide = hbuf[tp].astype(jnp.float32)
    own_sum = jnp.broadcast_to(jnp.sum(wide * wide, axis=1, keepdims=True), (ROWS, HD))
    squares_own[...] = own_sum.T[:8]
    pl.semaphore_wait(barrier, 13)
    signal(plane_sem, seq, x_peer(1))
    signal(plane_sem, seq, x_peer(3))

    half, quarter = ROWS // 2, ROWS // 4
    for d in (1, 3, 2):
        remote(
            squares_own, squares_x.at[d - 1], sq_send.at[0], sq_recv.at[0, d - 1], seq, x_peer(d)
        ).start()
    def forward(shard, first, rows, index, t):
        block = hbuf.at[shard, pl.ds(first, rows)]
        remote(block, block, ag_send, ag_recv.at[shard, index], seq, t).start()

    for d in (1, 3):
        forward(tp, 0, half, 0, x_peer(d))
        forward(tp, half, half, 1, y_peer(d))
    for d in (1, 3):
        forward(tp, half, half, 1, x_peer(d))
        forward(tp, 0, half, 0, y_peer(d))

    def place(ch):
        pair = ch // 2
        return ch % 2, ((pair + 1) // 2 + 1) % 2, pair // 2

    def is_local(ch):
        return ch // 2 == 1

    def stage(ch):
        return (ch + 6) % 8 % 6

    def send_stage(ch, carry):
        u, ix, iy = place(ch)
        back = u + ix * (3 - 2 * u)

        def send_one(i, c):
            g = (seq + i) % 8
            turn = 1 - 2 * (g % 2)
            kx = (x + 4 - turn * back) % 4
            shift = (kx % 2) * turn
            ky = ((y + 4 - shift) % 4 // 2 + iy) % 2
            lanes = pl.ds(pl.multiple_of((2 * kx + ky) * HD, HD), HD)
            k_src, v_src = key_pool.at[g, :, lanes], value_pool.at[g, :, lanes]

            def send(k_dst, v_dst):
                @pl.when(i == 0)
                def _():
                    pltpu.make_async_copy(k_src, k_dst, k_stage.at[ch]).start()
                    pltpu.make_async_copy(v_src, v_dst, v_stage.at[ch]).start()

                @pl.when(i != 0)
                def _():
                    remote(k_src, k_dst, kv_send.at[0], k_stage.at[ch], g, tp).start()
                    remote(v_src, v_dst, kv_send.at[1], v_stage.at[ch], g, tp).start()

            @pl.when(jnp.logical_not(is_local(ch)))
            def _():
                send(kstage.at[stage(ch), seq], vstage.at[stage(ch), seq])

            @pl.when(is_local(ch))
            def _():
                slot = ch * CHUNK + seq
                send(kbuf.at[slot, :, pl.ds(0, HD)], vbuf.at[slot])

            return c

        return lax.fori_loop(0, 8, send_one, carry)

    lax.fori_loop(0, 4, send_stage, 0)

    def landed(ref, sem):
        pltpu.make_async_copy(ref, ref, sem).wait()

    square_sums = squares_own[...]
    for d in range(3):
        landed(squares_x.at[d], sq_recv.at[0, d])
        square_sums = square_sums + squares_x[d]
    squares_mid[...] = square_sums
    for d in (1, 3, 2):
        remote(
            squares_mid, squares_y.at[d - 1], sq_send.at[1], sq_recv.at[1, d - 1], seq, y_peer(d)
        ).start()

    def send_leg(ch, carry):
        u, ix, iy = place(ch)
        kx = (x + 4 - sign * (u + ix * (3 - 2 * u))) % 4
        shift = (kx % 2) * sign
        xd = (kx + 4 + sign * u) % 4
        yd = iy * ring_partner(y, shift) + (1 - iy) * y
        slots = pl.ds(pl.multiple_of(ch * CHUNK, CHUNK), CHUNK)
        dest = xd * 4 + yd
        landed(kstage.at[stage(ch)], k_stage.at[ch])
        landed(vstage.at[stage(ch)], v_stage.at[ch])
        k_dst = kbuf.at[slots, :, pl.ds(0, HD)]
        remote(kstage.at[stage(ch)], k_dst, leg_send.at[0], k_recv.at[ch], seq, dest).start()
        remote(vstage.at[stage(ch)], vbuf.at[slots], leg_send.at[1], v_recv.at[ch], seq, dest).start()
        return carry

    def arrived(shard, first, rows, index):
        landed(hbuf.at[shard, pl.ds(first, rows)], ag_recv.at[shard, index])

    for d in (3, 1):
        shard = x_peer(d)
        arrived(shard, 0, half, 0)
        forward(shard, 0, half, 0, y_peer(1))
        forward(shard, 0, half, 0, y_peer(3))
        if d == 3:
            forward(shard, 0, half, 0, x_peer(1))
        shard = y_peer(d)
        arrived(shard, half, half, 1)
        forward(shard, half, half, 2, x_peer(1))
        forward(shard, half, half, 2, x_peer(3))
        if d == 3:
            forward(shard, half, half, 1, y_peer(1))
    for d in (1, 3):
        arrived(x_peer(d), half, half, 1)
        arrived(y_peer(d), 0, half, 0)
        if d == 1:
            forward(x_peer(d), half, half, 1, x_peer(3))
            forward(y_peer(d), 0, half, 0, y_peer(3))
    shard = x_peer(2)
    arrived(shard, 0, half, 0)
    forward(shard, 0, half, 0, y_peer(1))
    forward(shard, 0, half, 0, y_peer(3))
    shard = y_peer(2)
    arrived(shard, half, half, 1)
    forward(shard, half, half, 2, x_peer(1))
    forward(shard, half, half, 2, x_peer(3))
    for e in (3, 1, 2):
        for d in (3, 1):
            shard = (x + e) % 4 * 4 + (y + d) % 4
            arrived(shard, 0, half, 0)
            forward(shard, 0 if d == 3 else quarter, quarter, 0 if d == 3 else 1, y_peer(4 - d))
            shard = (x + d) % 4 * 4 + (y + e) % 4
            arrived(shard, half, half, 2)
            forward(
                shard, half if d == 3 else half + quarter, quarter, 2 if d == 3 else 3, x_peer(4 - d)
            )

    pl.semaphore_wait(plane_sem, 2)

    lax.fori_loop(4, 6, send_stage, 0)
    for d in range(3):
        landed(squares_y.at[d], sq_recv.at[1, d])
        square_sums = square_sums + squares_y[d]
    square_cols = jnp.broadcast_to(square_sums[:1], (HD, ROWS)).T
    factor = lax.rsqrt(square_cols[:, :1] / (SHARDS * FEAT) + 1e-5)
    loads[0].wait()
    loads[1].wait()

    def project(t, total):
        feats = pl.ds(pl.multiple_of(t * FEAT, FEAT), FEAT)
        normed = (
            hbuf[t].astype(jnp.float32) * factor * gain[:, feats].astype(jnp.float32)
        ).astype(jnp.bfloat16)
        return total + jnp.dot(normed, wqkv[feats, :], preferred_element_type=jnp.float32)

    def project_line(i, total):
        along = i // 4
        d = i % 4
        return project((x + (1 - along) * d) % 4 * 4 + (y + along * d) % 4, total)

    def project_far(i, total):
        return project((x + 1 + i // 3) % 4 * 4 + (y + 1 + i % 3) % 4, total)

    arrived(x_peer(2), half, half, 1)
    arrived(y_peer(2), 0, half, 0)
    projected = lax.fori_loop(0, 4, project_line, jnp.zeros((ROWS, 512), jnp.float32))
    projected = lax.fori_loop(5, 8, project_line, projected)
    for e in (3, 1, 2):
        shard = (x + e) % 4 * 4 + (y + 2) % 4
        arrived(shard, 0, quarter, 0)
        arrived(shard, quarter, quarter, 1)
        shard = (x + 2) % 4 * 4 + (y + e) % 4
        arrived(shard, half, quarter, 2)
        arrived(shard, half + quarter, quarter, 3)
    projected = lax.fori_loop(0, 9, project_far, projected).astype(jnp.bfloat16)
    for h in range(HEADS):
        qown[h] = projected[:, h * HD : (h + 1) * HD]
    kvown[tp % 2] = projected[:, HEADS * HD :]

    own_copy = remote(
        kvown.at[tp % 2], kvown.at[tp % 2], own_send, own_recv.at[tp % 2], seq, tp + 1 - 2 * (tp % 2)
    )
    own_half = tp % 2

    def q_copies(u, j):
        t = (x + 4 + sign * u) % 4 * 4 + (y // 2 * 2 + j + 4 + x % 2 * sign) % 4
        dst = qaug.at[u, pl.ds(own_half * HEADS, HEADS), :, pl.ds(0, HD)]
        there = remote(qown, dst, q_send.at[u, j], q_recv.at[u, own_half], seq, t)
        here = pltpu.make_async_copy(qown, dst, q_recv.at[u, own_half])
        return t == tp, here, there

    for u in range(2):
        for j in range(2):
            same, here, there = q_copies(u, j)
            pl.when(same)(here.start)
            pl.when(jnp.logical_not(same))(there.start)
    own_copy.start()
    lax.fori_loop(0, 2, send_leg, 0)
    lax.fori_loop(6, CHUNKS, send_stage, 0)
    lane = lax.broadcasted_iota(jnp.int32, (ROWS, HD), 1)
    first_request = seq // 2 * 8
    requests = jnp.broadcast_to(row_req[...], (HD, ROWS)).T
    onehot = jnp.where(requests == lane + first_request, 1.0, 0.0).astype(jnp.bfloat16)
    for u in range(2):
        for h in range(2 * HEADS):
            qaug[u, h, :, HD:] = onehot
    table_wide[...] = jnp.full_like(table_wide, -1)
    table_wide[:8, :64] = table[pl.ds(pl.multiple_of(first_request, 8), 8), :]
    table_cols[...] = table_wide[...].T[:64]
    table_lane = lax.broadcasted_iota(jnp.int32, (64, HD), 1)
    ends = jnp.zeros((64, HD), jnp.int32)
    for r in range(8):
        ends = jnp.where(table_lane == r, lengths[first_request + r], ends)
    caps[...] = jnp.clip(ends - BLK * lax.broadcasted_iota(jnp.int32, (64, HD), 0), 0, BLK)
    token = lax.broadcasted_iota(jnp.int32, (BLK, HD), 0)

    def mask_slot(slot, carry):
        ch, s = slot // 8, slot % 8
        u, ix, iy = place(ch)
        shift = ((x + 4 - sign * u) % 4) % 2 * sign
        xs = (x + 4 + sign * ix * (2 * u - 1)) % 4
        ys = iy * ring_partner(y, shift) + (1 - iy) * y
        block = (s * 16 + xs * 4 + ys) * 8 + seq
        valid = jnp.sum(jnp.where(table_cols[...] == block, caps[...], 0), axis=0, keepdims=True)
        kbuf[slot, :, HD:] = jnp.where(token < valid, 0.0, MASKED).astype(jnp.bfloat16)
        return carry

    lax.fori_loop(0, SLOTS, mask_slot, 0)
    top[...] = jnp.full_like(top, 2 * MASKED)
    tot[...] = jnp.zeros_like(tot)
    acc[...] = jnp.zeros_like(acc)

    for u in range(2):
        for part_half in range(2):
            dst = qaug.at[u, pl.ds(part_half * HEADS, HEADS), :, pl.ds(0, HD)]
            pltpu.make_async_copy(dst, dst, q_recv.at[u, part_half]).wait()

    lax.fori_loop(4, 6, send_leg, 0)

    def o_copies(u, to):
        kx = (x + 4 - sign * u) % 4
        shift = kx % 2 * sign
        yy = (y + 4 - shift) % 4
        t = kx * 4 + yy // 2 * 2 + to
        index = u * 2 + yy % 2
        o_src, o_dst = osend.at[u, to], orecv.at[index]
        s_src = ssend.at[u, to]
        s_dst = srecv.at[pl.ds(pl.multiple_of(index * 8, 8), 8)]
        return (
            t == tp,
            pltpu.make_async_copy(o_src, o_dst, o_recv.at[index]),
            remote(o_src, o_dst, o_send.at[u, to], o_recv.at[index], seq, t),
            pltpu.make_async_copy(s_src, s_dst, s_recv.at[index]),
            remote(s_src, s_dst, s_send.at[u, to], s_recv.at[index], seq, t),
        )

    srecv[pl.ds(32, 96), :] = jnp.zeros((96, ROWS), jnp.float32)

    def send_partials(u):
        for to in range(2):
            stats = jnp.zeros((ROWS, HD), jnp.float32)
            for h in range(HEADS):
                rows = pl.ds((to * HEADS + h) * ROWS, ROWS)
                stats = jnp.where(lane == h, top[u, rows, :], stats)
                stats = jnp.where(lane == HEADS + h, tot[u, rows, :], stats)
                osend[u, to, h] = acc[u, rows, :].astype(jnp.bfloat16)
            ssend[u, to] = stats.T[:8]
            same, o_here_copy, o_there, s_here_copy, s_there = o_copies(u, to)

            @pl.when(same)
            def _():
                o_here_copy.start()
                s_here_copy.start()

            @pl.when(jnp.logical_not(same))
            def _():
                o_there.start()
                s_there.start()

    def attend_chunk(ch, carry):
        u = ch % 2
        slots = pl.ds(pl.multiple_of(ch * CHUNK, CHUNK), CHUNK)

        @pl.when((ch == 2) | (ch == 3))
        def _():
            send_leg(ch + 4, 0)

        k_dst = kbuf.at[slots, :, pl.ds(0, HD)]

        @pl.when(jnp.logical_not(is_local(ch)))
        def _():
            landed(k_dst, k_recv.at[ch])
            landed(vbuf.at[slots], v_recv.at[ch])

        @pl.when(is_local(ch))
        def _():
            landed(k_dst, k_stage.at[ch])
            landed(vbuf.at[slots], v_stage.at[ch])

        keys = kbuf[slots].reshape(CHUNK * BLK, 2 * HD)
        values = vbuf[slots].reshape(CHUNK * BLK, HD)
        scores = lax.dot_general(
            qaug[u].reshape(2 * HEADS * ROWS, 2 * HD),
            keys,
            (((1,), (1,)), ((), ())),
            preferred_element_type=jnp.float32,
        )
        old = top[u]
        new = jnp.maximum(old, jnp.max(scores, axis=1, keepdims=True))
        shrink = jnp.exp2((old - new) * LOG2_SCALE)
        weights = jnp.exp2(scores * LOG2_SCALE - new[:, :1] * LOG2_SCALE)
        top[u] = new
        tot[u] = tot[u] * shrink + jnp.sum(weights, axis=1, keepdims=True)
        acc[u] = acc[u] * shrink + jnp.dot(
            weights.astype(jnp.bfloat16), values, preferred_element_type=jnp.float32
        )

        @pl.when(ch >= CHUNKS - 2)
        def _():
            send_partials(u)

        return carry

    lax.fori_loop(0, CHUNKS, attend_chunk, 0)

    own_copy.wait_send()
    other = 1 - tp % 2
    pltpu.make_async_copy(kvown.at[other], kvown.at[other], own_recv.at[other]).wait()
    own_key = kvown[0].astype(jnp.float32)
    own_value = kvown[1].astype(jnp.float32)
    self_scores = [
        jnp.sum(qown[h].astype(jnp.float32) * own_key, axis=1, keepdims=True) for h in range(HEADS)
    ]
    for i in range(4):
        pltpu.make_async_copy(orecv.at[i], orecv.at[i], o_recv.at[i]).wait()
        s_dst = srecv.at[pl.ds(i * 8, 8)]
        pltpu.make_async_copy(s_dst, s_dst, s_recv.at[i]).wait()
    stats = srecv[...].T
    for h in range(HEADS):
        tops = [stats[:, i * 8 + h : i * 8 + h + 1] for i in range(4)]
        best = self_scores[h]
        for one in tops:
            best = jnp.maximum(best, one)
        own_weight = jnp.exp2((self_scores[h] - best) * LOG2_SCALE)
        total = own_weight
        numer = own_weight.astype(jnp.bfloat16).astype(jnp.float32) * own_value
        for i in range(4):
            scale = jnp.exp2((tops[i] - best) * LOG2_SCALE)
            total = total + scale * stats[:, i * 8 + HEADS + h : i * 8 + HEADS + h + 1]
            numer = numer + scale * orecv[i, h].astype(jnp.float32)
        att[:, h * HD : (h + 1) * HD] = (numer / total).astype(jnp.bfloat16)

    loads[2].wait()

    def columns(tile, first=0, width=TILE):
        return pl.ds(pl.multiple_of(first + tile * TILE, TILE // 2), width)

    def half_columns(tile):
        return pl.ds(pl.multiple_of(tile * (TILE // 2), TILE // 2), TILE // 2)

    def first(side):
        return side * TILES * TILE

    def ring_peer(side, d):
        return (x_peer, y_peer)[side](d)

    def ring_block(side, d, cols):
        if side == 0:
            return part.at[(x + d) % 4, :, :, cols]
        return part.at[:, (y + d) % 4, :, cols]

    def project_out(tile, carry):
        for side in range(2):
            cols = columns(tile, side * TILES * TILE)
            part[:, :, :, cols] = (
                jnp.dot(att[...], wo[:, cols], preferred_element_type=jnp.float32)
                .astype(jnp.bfloat16)
                .reshape(4, 4, 16, TILE)
            )
            for d in (1, 3):
                src = ring_block(side, 2, columns(tile, first(side) + (TILE // 2 if d == 3 else 0), TILE // 2))
                dst = (via_a, via_b)[side].at[d // 2, :, :, half_columns(tile)]
                remote(
                    src, dst, via_send.at[side], via_recv.at[side, tile, d // 2], seq, ring_peer(side, d)
                ).start()
        return carry

    lax.fori_loop(0, TILES, project_out, 0)

    def relay(tile, carry):
        for side in range(2):
            via = (via_a, via_b)[side]
            for d in (1, 3):
                passing = via.at[d // 2, :, :, half_columns(tile)]
                landed(passing, via_recv.at[side, tile, d // 2])
                block = ring_block(
                    side, d, columns(tile, first(side) + (TILE // 2 if d == 3 else 0), TILE // 2)
                )
                block[...] = (
                    block[...].astype(jnp.float32) + passing[...].astype(jnp.float32)
                ).astype(jnp.bfloat16)
                remote(
                    ring_block(side, d, columns(tile, first(side))),
                    (rs_a, rs_b)[side].at[d // 2, :, :, columns(tile)],
                    rs1_send.at[side], rs1_recv.at[side, tile, d // 2], seq, ring_peer(side, d),
                ).start()
        return carry

    lax.fori_loop(0, TILES, relay, 0)

    def sum_first(tile, carry):
        for side in range(2):
            here = columns(tile)
            arriving = (rs_a, rs_b)[side]
            mid = (mid_a, mid_b)[side]
            total = ring_block(side, 0, columns(tile, first(side)))[...].astype(jnp.float32)
            for d in range(2):
                dst = arriving.at[d, :, :, here]
                landed(dst, rs1_recv.at[side, tile, d])
                total = total + dst[...].astype(jnp.float32)
            mid[:, :, here] = total.astype(jnp.bfloat16)
            for d in (1, 3, 2):
                if side == 0:
                    src, t = mid.at[(y + d) % 4, :, here], x * 4 + (y + d) % 4
                else:
                    src, t = mid.at[(x + d) % 4, :, here], (x + d) % 4 * 4 + y
                dst = (fin_a, fin_b)[side].at[d - 1, :, here]
                remote(
                    src, dst, rs2_send.at[side], rs2_recv.at[side, tile, d - 1], seq, t
                ).start()
        return carry

    lax.fori_loop(0, TILES, sum_first, 0)

    def sum_last(tile, carry):
        for side in range(2):
            here = columns(tile)
            arriving = (fin_a, fin_b)[side]
            if side == 0:
                total = mid_a[y, :, here].astype(jnp.float32)
            else:
                total = mid_b[x, :, here].astype(jnp.float32)
            for d in range(3):
                dst = arriving.at[d, :, here]
                pltpu.make_async_copy(dst, dst, rs2_recv.at[side, tile, d]).wait()
                total = total + arriving[d, :, here].astype(jnp.float32)
            out[:, columns(tile, side * TILES * TILE)] = total.astype(jnp.bfloat16)
        return carry

    lax.fori_loop(0, TILES, sum_last, 0)

    for i in range(2):
        landed((squares_x, squares_y)[i], sq_send.at[i])
    sent = hbuf.at[pl.ds(0, SHARDS - 1)]
    pltpu.make_async_copy(sent, sent, ag_send).wait()
    for i in range(2):
        landed(vbuf.at[pl.ds(0, SLOTS - CHUNKS)], kv_send.at[i])
        landed(vbuf.at[pl.ds(0, STAGED * CHUNK)], leg_send.at[i])
    for u in range(2):
        for j in range(2):
            same, _, there = q_copies(u, j)
            pl.when(jnp.logical_not(same))(there.wait_send)
            same, _, o_there, _, s_there = o_copies(u, j)

            @pl.when(jnp.logical_not(same))
            def _():
                o_there.wait_send()
                s_there.wait_send()

    for side in range(2):
        landed((via_a, via_b)[side], via_send.at[side])
        sent = (rs_a, rs_b)[side]
        pltpu.make_async_copy(sent, sent, rs1_send.at[side]).wait()
        sent = (fin_a, fin_b)[side]
        pltpu.make_async_copy(sent, sent, rs2_send.at[side]).wait()


def per_device(
    hidden_in,
    norm_gain,
    w_query,
    w_keyval,
    w_out,
    key_pool,
    value_pool,
    block_table,
    prefix_lengths,
    row_request,
):
    bf16, f32 = jnp.bfloat16, jnp.float32
    vmem = functools.partial(pltpu.VMEM)
    dma = pltpu.SemaphoreType.DMA
    any_spec = pl.BlockSpec(memory_space=pl.ANY)
    vmem_spec = pl.BlockSpec(memory_space=pltpu.VMEM)
    smem_spec = pl.BlockSpec(memory_space=pltpu.SMEM)
    return pl.pallas_call(
        body,
        out_shape=jax.ShapeDtypeStruct((16, 6144), bf16),
        in_specs=[any_spec, vmem_spec] + [any_spec] * 5 + [vmem_spec, smem_spec, vmem_spec],
        out_specs=vmem_spec,
        scratch_shapes=[
            vmem((SHARDS, ROWS, FEAT), bf16),
            vmem((SHARDS * FEAT, 512), bf16),
            vmem((FEAT, 6144), bf16),
            vmem((SLOTS, BLK, 2 * HD), bf16),
            vmem((SLOTS, BLK, HD), bf16),
            vmem((STAGED, CHUNK, BLK, HD), bf16),
            vmem((STAGED, CHUNK, BLK, HD), bf16),
            vmem((2, 2 * HEADS, ROWS, 2 * HD), bf16),
            vmem((HEADS, ROWS, HD), bf16),
            vmem((2, ROWS, HD), bf16),
            vmem((2, 2 * HEADS * ROWS, HD), f32),
            vmem((2, 2 * HEADS * ROWS, HD), f32),
            vmem((2, 2 * HEADS * ROWS, HD), f32),
            vmem((2, 2, HEADS, ROWS, HD), bf16),
            vmem((2, 2, 8, ROWS), f32),
            vmem((4, HEADS, ROWS, HD), bf16),
            vmem((128, ROWS), f32),
            vmem((8, ROWS), f32),
            vmem((3, 8, ROWS), f32),
            vmem((8, ROWS), f32),
            vmem((3, 8, ROWS), f32),
            vmem((HD, HD), jnp.int32),
            vmem((64, HD), jnp.int32),
            vmem((64, HD), jnp.int32),
            vmem((ROWS, FEAT), bf16),
            vmem((4, 4, 16, 6144), bf16),
            vmem((2, 4, 16, 3072), bf16),
            vmem((2, 4, 16, 3072), bf16),
            vmem((2, 4, 16, 1536), bf16),
            vmem((2, 4, 16, 1536), bf16),
            vmem((4, 16, 3072), bf16),
            vmem((4, 16, 3072), bf16),
            vmem((3, 16, 3072), bf16),
            vmem((3, 16, 3072), bf16),
            dma((4,)),
            pltpu.SemaphoreType.REGULAR,
            dma((2,)),
            dma((2, 3)),
            dma,
            dma((SHARDS, 4)),
            dma((2,)),
            dma((2,)),
            dma((CHUNKS,)),
            dma((CHUNKS,)),
            dma((CHUNKS,)),
            dma((CHUNKS,)),
            dma((2, 2)),
            dma((2, 2)),
            dma,
            dma((2,)),
            dma((2, 2)),
            dma((4,)),
            dma((2, 2)),
            dma((4,)),
            dma((2,)),
            dma((2, TILES, 2)),
            dma((2,)),
            dma((2, TILES, 2)),
            dma((2,)),
            dma((2, TILES, 3)),
        ],
        compiler_params=pltpu.CompilerParams(
            collective_id=0, has_side_effects=True, vmem_limit_bytes=60 << 20
        ),
        cost_estimate=pl.CostEstimate(
            flops=10_000_000_000, bytes_accessed=20_000_000, transcendentals=13_000_000
        ),
    )(
        hidden_in,
        norm_gain.reshape(1, SHARDS * FEAT),
        w_query,
        w_keyval,
        w_out,
        key_pool,
        value_pool,
        block_table,
        prefix_lengths,
        row_request.reshape(1, ROWS),
    )


def solution(mesh):
    return jax.shard_map(
        per_device,
        mesh=mesh,
        in_specs=(
            P("seq", "tp"),
            P(),
            P(None, "tp"),
            P(None, "tp"),
            P("tp", None),
            P(("seq", "tp"), None, None),
            P(("seq", "tp"), None, None),
            P(),
            P(),
            P("seq"),
        ),
        out_specs=P(("seq", "tp"), None),
        check_vma=False,
    )
```

```python
import functools

import jax
import jax.numpy as jnp
from jax import lax
from jax.experimental import pallas as pl
from jax.experimental.pallas import tpu as pltpu
from jax.sharding import PartitionSpec as P

MESH = pl.DeviceIdType.MESH
HD = 128
BLK = 128
ROWS = 256
FEAT = 384
SHARDS = 16
HEADS = 3
SLOTS = 64
CHUNK = 8
CHUNKS = 8
STAGED = 6
TILE = 512
TILES = 6
MASKED = -1e30
LOG2_SCALE = 1.4426950408889634 / HD**0.5


def ring_partner(y, shift):
    return (7 - (y + 4 - shift) % 4 + shift) % 4


def body(
    hidden,
    gain,
    w_query,
    w_keyval,
    w_out,
    key_pool,
    value_pool,
    table,
    lengths,
    row_req,
    out,
    hbuf,
    wqkv,
    wo,
    kbuf,
    vbuf,
    kstage,
    vstage,
    qaug,
    qown,
    kvown,
    acc,
    top,
    tot,
    osend,
    ssend,
    orecv,
    srecv,
    squares_own,
    squares_x,
    squares_mid,
    squares_y,
    table_wide,
    table_cols,
    caps,
    att,
    part,
    rs_a,
    rs_b,
    via_a,
    via_b,
    mid_a,
    mid_b,
    fin_a,
    fin_b,
    load_sem,
    plane_sem,
    sq_send,
    sq_recv,
    ag_send,
    ag_recv,
    kv_send,
    leg_send,
    k_stage,
    v_stage,
    k_recv,
    v_recv,
    q_send,
    q_recv,
    own_send,
    own_recv,
    o_send,
    o_recv,
    s_send,
    s_recv,
    via_send,
    via_recv,
    rs1_send,
    rs1_recv,
    rs2_send,
    rs2_recv,
):
    seq = lax.axis_index("seq")
    tp = lax.axis_index("tp")
    x, y = tp // 4, tp % 4
    sign = 1 - 2 * (seq % 2)

    def remote(src, dst, send, recv, s, t):
        return pltpu.make_async_remote_copy(
            src, dst, send, recv, device_id=(s, t), device_id_type=MESH
        )

    def signal(sem, s, t):
        pl.semaphore_signal(sem, inc=1, device_id=(s, t), device_id_type=MESH)

    def x_peer(d):
        return (x + d) % 4 * 4 + y

    def y_peer(d):
        return x * 4 + (y + d) % 4

    barrier = pltpu.get_barrier_semaphore()
    for d in (1, 3, 2):
        signal(barrier, seq, x_peer(d))
        signal(barrier, seq, y_peer(d))
    for i in range(1, 8):
        signal(barrier, (seq + i) % 8, tp)

    own_load = pltpu.make_async_copy(hidden, hbuf.at[tp], load_sem.at[0])
    own_load.start()
    loads = [
        pltpu.make_async_copy(w_query, wqkv.at[:, pl.ds(0, 384)], load_sem.at[1]),
        pltpu.make_async_copy(w_keyval, wqkv.at[:, pl.ds(384, 128)], load_sem.at[2]),
        pltpu.make_async_copy(w_out, wo, load_sem.at[3]),
    ]
    for load in loads:
        load.start()
    own_load.wait()
    wide = hbuf[tp].astype(jnp.float32)
    own_sum = jnp.broadcast_to(jnp.sum(wide * wide, axis=1, keepdims=True), (ROWS, HD))
    squares_own[...] = own_sum.T[:8]
    pl.semaphore_wait(barrier, 13)
    signal(plane_sem, seq, x_peer(1))
    signal(plane_sem, seq, x_peer(3))

    half, quarter = ROWS // 2, ROWS // 4
    for d in (1, 3, 2):
        remote(
            squares_own, squares_x.at[d - 1], sq_send.at[0], sq_recv.at[0, d - 1], seq, x_peer(d)
        ).start()
    def forward(shard, first, rows, index, t):
        block = hbuf.at[shard, pl.ds(first, rows)]
        remote(block, block, ag_send, ag_recv.at[shard, index], seq, t).start()

    for d in (1, 3):
        forward(tp, 0, half, 0, x_peer(d))
        forward(tp, half, half, 1, y_peer(d))
    for d in (1, 3):
        forward(tp, half, half, 1, x_peer(d))
        forward(tp, 0, half, 0, y_peer(d))

    def place(ch):
        pair = ch // 2
        return ch % 2, ((pair + 1) // 2 + 1) % 2, pair // 2

    def is_local(ch):
        return ch // 2 == 1

    def stage(ch):
        return (ch + 6) % 8 % 6

    def send_stage(ch, carry):
        u, ix, iy = place(ch)
        back = u + ix * (3 - 2 * u)

        def send_one(i, c):
            g = (seq + i) % 8
            turn = 1 - 2 * (g % 2)
            kx = (x + 4 - turn * back) % 4
            shift = (kx % 2) * turn
            ky = ((y + 4 - shift) % 4 // 2 + iy) % 2
            lanes = pl.ds(pl.multiple_of((2 * kx + ky) * HD, HD), HD)
            k_src, v_src = key_pool.at[g, :, lanes], value_pool.at[g, :, lanes]

            def send(k_dst, v_dst):
                @pl.when(i == 0)
                def _():
                    pltpu.make_async_copy(k_src, k_dst, k_stage.at[ch]).start()
                    pltpu.make_async_copy(v_src, v_dst, v_stage.at[ch]).start()

                @pl.when(i != 0)
                def _():
                    remote(k_src, k_dst, kv_send.at[0], k_stage.at[ch], g, tp).start()
                    remote(v_src, v_dst, kv_send.at[1], v_stage.at[ch], g, tp).start()

            @pl.when(jnp.logical_not(is_local(ch)))
            def _():
                send(kstage.at[stage(ch), seq], vstage.at[stage(ch), seq])

            @pl.when(is_local(ch))
            def _():
                slot = ch * CHUNK + seq
                send(kbuf.at[slot, :, pl.ds(0, HD)], vbuf.at[slot])

            return c

        return lax.fori_loop(0, 8, send_one, carry)

    lax.fori_loop(0, 4, send_stage, 0)

    def landed(ref, sem):
        pltpu.make_async_copy(ref, ref, sem).wait()

    square_sums = squares_own[...]
    for d in range(3):
        landed(squares_x.at[d], sq_recv.at[0, d])
        square_sums = square_sums + squares_x[d]
    squares_mid[...] = square_sums
    for d in (1, 3, 2):
        remote(
            squares_mid, squares_y.at[d - 1], sq_send.at[1], sq_recv.at[1, d - 1], seq, y_peer(d)
        ).start()

    def send_leg(ch, carry):
        u, ix, iy = place(ch)
        kx = (x + 4 - sign * (u + ix * (3 - 2 * u))) % 4
        shift = (kx % 2) * sign
        xd = (kx + 4 + sign * u) % 4
        yd = iy * ring_partner(y, shift) + (1 - iy) * y
        slots = pl.ds(pl.multiple_of(ch * CHUNK, CHUNK), CHUNK)
        dest = xd * 4 + yd
        landed(kstage.at[stage(ch)], k_stage.at[ch])
        landed(vstage.at[stage(ch)], v_stage.at[ch])
        k_dst = kbuf.at[slots, :, pl.ds(0, HD)]
        remote(kstage.at[stage(ch)], k_dst, leg_send.at[0], k_recv.at[ch], seq, dest).start()
        remote(vstage.at[stage(ch)], vbuf.at[slots], leg_send.at[1], v_recv.at[ch], seq, dest).start()
        return carry

    def arrived(shard, first, rows, index):
        landed(hbuf.at[shard, pl.ds(first, rows)], ag_recv.at[shard, index])

    for d in (3, 1):
        shard = x_peer(d)
        arrived(shard, 0, half, 0)
        forward(shard, 0, half, 0, y_peer(1))
        forward(shard, 0, half, 0, y_peer(3))
        if d == 3:
            forward(shard, 0, half, 0, x_peer(1))
        shard = y_peer(d)
        arrived(shard, half, half, 1)
        forward(shard, half, half, 2, x_peer(1))
        forward(shard, half, half, 2, x_peer(3))
        if d == 3:
            forward(shard, half, half, 1, y_peer(1))
    for d in (1, 3):
        arrived(x_peer(d), half, half, 1)
        arrived(y_peer(d), 0, half, 0)
        if d == 1:
            forward(x_peer(d), half, half, 1, x_peer(3))
            forward(y_peer(d), 0, half, 0, y_peer(3))
    shard = x_peer(2)
    arrived(shard, 0, half, 0)
    forward(shard, 0, half, 0, y_peer(1))
    forward(shard, 0, half, 0, y_peer(3))
    shard = y_peer(2)
    arrived(shard, half, half, 1)
    forward(shard, half, half, 2, x_peer(1))
    forward(shard, half, half, 2, x_peer(3))
    for e in (3, 1, 2):
        for d in (3, 1):
            shard = (x + e) % 4 * 4 + (y + d) % 4
            arrived(shard, 0, half, 0)
            forward(shard, 0 if d == 3 else quarter, quarter, 0 if d == 3 else 1, y_peer(4 - d))
            shard = (x + d) % 4 * 4 + (y + e) % 4
            arrived(shard, half, half, 2)
            forward(
                shard, half if d == 3 else half + quarter, quarter, 2 if d == 3 else 3, x_peer(4 - d)
            )

    pl.semaphore_wait(plane_sem, 2)

    lax.fori_loop(4, 6, send_stage, 0)
    for d in range(3):
        landed(squares_y.at[d], sq_recv.at[1, d])
        square_sums = square_sums + squares_y[d]
    square_cols = jnp.broadcast_to(square_sums[:1], (HD, ROWS)).T
    factor = lax.rsqrt(square_cols[:, :1] / (SHARDS * FEAT) + 1e-5)
    loads[0].wait()
    loads[1].wait()

    def project(t, total):
        feats = pl.ds(pl.multiple_of(t * FEAT, FEAT), FEAT)
        normed = (
            hbuf[t].astype(jnp.float32) * factor * gain[:, feats].astype(jnp.float32)
        ).astype(jnp.bfloat16)
        return total + jnp.dot(normed, wqkv[feats, :], preferred_element_type=jnp.float32)

    def project_line(i, total):
        along = i // 4
        d = i % 4
        return project((x + (1 - along) * d) % 4 * 4 + (y + along * d) % 4, total)

    def project_far(i, total):
        return project((x + 1 + i // 3) % 4 * 4 + (y + 1 + i % 3) % 4, total)

    arrived(x_peer(2), half, half, 1)
    arrived(y_peer(2), 0, half, 0)
    projected = lax.fori_loop(0, 4, project_line, jnp.zeros((ROWS, 512), jnp.float32))
    projected = lax.fori_loop(5, 8, project_line, projected)
    for e in (3, 1, 2):
        shard = (x + e) % 4 * 4 + (y + 2) % 4
        arrived(shard, 0, quarter, 0)
        arrived(shard, quarter, quarter, 1)
        shard = (x + 2) % 4 * 4 + (y + e) % 4
        arrived(shard, half, quarter, 2)
        arrived(shard, half + quarter, quarter, 3)
    projected = lax.fori_loop(0, 9, project_far, projected).astype(jnp.bfloat16)
    for h in range(HEADS):
        qown[h] = projected[:, h * HD : (h + 1) * HD]
    kvown[tp % 2] = projected[:, HEADS * HD :]

    own_copy = remote(
        kvown.at[tp % 2], kvown.at[tp % 2], own_send, own_recv.at[tp % 2], seq, tp + 1 - 2 * (tp % 2)
    )
    own_half = tp % 2

    def q_copies(u, j):
        t = (x + 4 + sign * u) % 4 * 4 + (y // 2 * 2 + j + 4 + x % 2 * sign) % 4
        dst = qaug.at[u, pl.ds(own_half * HEADS, HEADS), :, pl.ds(0, HD)]
        there = remote(qown, dst, q_send.at[u, j], q_recv.at[u, own_half], seq, t)
        here = pltpu.make_async_copy(qown, dst, q_recv.at[u, own_half])
        return t == tp, here, there

    for u in range(2):
        for j in range(2):
            same, here, there = q_copies(u, j)
            pl.when(same)(here.start)
            pl.when(jnp.logical_not(same))(there.start)
    own_copy.start()
    lax.fori_loop(6, CHUNKS, send_stage, 0)
    lane = lax.broadcasted_iota(jnp.int32, (ROWS, HD), 1)
    first_request = seq // 2 * 8
    requests = jnp.broadcast_to(row_req[...], (HD, ROWS)).T
    onehot = jnp.where(requests == lane + first_request, 1.0, 0.0).astype(jnp.bfloat16)
    for u in range(2):
        for h in range(2 * HEADS):
            qaug[u, h, :, HD:] = onehot
    table_wide[...] = jnp.full_like(table_wide, -1)
    table_wide[:8, :64] = table[pl.ds(pl.multiple_of(first_request, 8), 8), :]
    table_cols[...] = table_wide[...].T[:64]
    table_lane = lax.broadcasted_iota(jnp.int32, (64, HD), 1)
    ends = jnp.zeros((64, HD), jnp.int32)
    for r in range(8):
        ends = jnp.where(table_lane == r, lengths[first_request + r], ends)
    caps[...] = jnp.clip(ends - BLK * lax.broadcasted_iota(jnp.int32, (64, HD), 0), 0, BLK)
    token = lax.broadcasted_iota(jnp.int32, (BLK, HD), 0)

    def mask_slot(slot, carry):
        ch, s = slot // 8, slot % 8
        u, ix, iy = place(ch)
        shift = ((x + 4 - sign * u) % 4) % 2 * sign
        xs = (x + 4 + sign * ix * (2 * u - 1)) % 4
        ys = iy * ring_partner(y, shift) + (1 - iy) * y
        block = (s * 16 + xs * 4 + ys) * 8 + seq
        valid = jnp.sum(jnp.where(table_cols[...] == block, caps[...], 0), axis=0, keepdims=True)
        kbuf[slot, :, HD:] = jnp.where(token < valid, 0.0, MASKED).astype(jnp.bfloat16)
        return carry

    lax.fori_loop(0, SLOTS, mask_slot, 0)
    top[...] = jnp.full_like(top, 2 * MASKED)
    tot[...] = jnp.zeros_like(tot)
    acc[...] = jnp.zeros_like(acc)

    for u in range(2):
        for part_half in range(2):
            dst = qaug.at[u, pl.ds(part_half * HEADS, HEADS), :, pl.ds(0, HD)]
            pltpu.make_async_copy(dst, dst, q_recv.at[u, part_half]).wait()

    lax.fori_loop(0, 2, send_leg, 0)
    lax.fori_loop(4, 6, send_leg, 0)

    def o_copies(u, to):
        kx = (x + 4 - sign * u) % 4
        shift = kx % 2 * sign
        yy = (y + 4 - shift) % 4
        t = kx * 4 + yy // 2 * 2 + to
        index = u * 2 + yy % 2
        o_src, o_dst = osend.at[u, to], orecv.at[index]
        s_src = ssend.at[u, to]
        s_dst = srecv.at[u, pl.ds(pl.multiple_of(yy % 2 * 8, 8), 8)]
        return (
            t == tp,
            pltpu.make_async_copy(o_src, o_dst, o_recv.at[index]),
            remote(o_src, o_dst, o_send.at[u, to], o_recv.at[index], seq, t),
            pltpu.make_async_copy(s_src, s_dst, s_recv.at[index]),
            remote(s_src, s_dst, s_send.at[u, to], s_recv.at[index], seq, t),
        )

    srecv[:, pl.ds(16, 112), :] = jnp.zeros((2, 112, ROWS), jnp.float32)

    def send_partials(u, to):
        stats = jnp.zeros((ROWS, HD), jnp.float32)
        for h in range(HEADS):
            rows = pl.ds(pl.multiple_of((to * HEADS + h) * ROWS, ROWS), ROWS)
            stats = jnp.where(lane == h, top[u, rows, :], stats)
            stats = jnp.where(lane == HEADS + h, tot[u, rows, :], stats)
            osend[u, to, h] = acc[u, rows, :].astype(jnp.bfloat16)
        ssend[u, to] = stats.T[:8]
        same, o_here_copy, o_there, s_here_copy, s_there = o_copies(u, to)

        @pl.when(same)
        def _():
            o_here_copy.start()
            s_here_copy.start()

        @pl.when(jnp.logical_not(same))
        def _():
            o_there.start()
            s_there.start()

    def attend_chunk(i, carry):
        late = i // 4
        ch = (1 - late) * ((i + 2) % 4) + late * i
        u = ch % 2
        slots = pl.ds(pl.multiple_of(ch * CHUNK, CHUNK), CHUNK)

        @pl.when((i == 3) | (i == 4))
        def _():
            send_leg(i + 3, 0)

        k_dst = kbuf.at[slots, :, pl.ds(0, HD)]

        @pl.when(jnp.logical_not(is_local(ch)))
        def _():
            landed(k_dst, k_recv.at[ch])
            landed(vbuf.at[slots], v_recv.at[ch])

        @pl.when(is_local(ch))
        def _():
            landed(k_dst, k_stage.at[ch])
            landed(vbuf.at[slots], v_stage.at[ch])

        keys = kbuf[slots].reshape(CHUNK * BLK, 2 * HD)
        values = vbuf[slots].reshape(CHUNK * BLK, HD)

        def attend(first_head, heads):
            rows = pl.ds(pl.multiple_of(first_head * ROWS, ROWS), heads * ROWS)
            scores = lax.dot_general(
                qaug[u, pl.ds(first_head, heads)].reshape(heads * ROWS, 2 * HD),
                keys,
                (((1,), (1,)), ((), ())),
                preferred_element_type=jnp.float32,
            )
            old = top[u, rows, :]
            new = jnp.maximum(old, jnp.max(scores, axis=1, keepdims=True))
            shrink = jnp.exp2((old - new) * LOG2_SCALE)
            weights = jnp.exp2(scores * LOG2_SCALE - new[:, :1] * LOG2_SCALE)
            top[u, rows, :] = new
            tot[u, rows, :] = tot[u, rows, :] * shrink + jnp.sum(weights, axis=1, keepdims=True)
            acc[u, rows, :] = acc[u, rows, :] * shrink + jnp.dot(
                weights.astype(jnp.bfloat16), values, preferred_element_type=jnp.float32
            )

        @pl.when(ch < CHUNKS - 2)
        def _():
            attend(0, 2 * HEADS)

        @pl.when(ch >= CHUNKS - 2)
        def _():
            def attend_owner(to, c):
                attend(to * HEADS, HEADS)
                send_partials(u, to)
                return c

            lax.fori_loop(0, 2, attend_owner, 0)

        return carry

    lax.fori_loop(0, CHUNKS, attend_chunk, 0)

    own_copy.wait_send()
    other = 1 - tp % 2
    pltpu.make_async_copy(kvown.at[other], kvown.at[other], own_recv.at[other]).wait()
    own_key = kvown[0].astype(jnp.float32)
    own_value = kvown[1].astype(jnp.float32)
    self_scores = [
        jnp.sum(qown[h].astype(jnp.float32) * own_key, axis=1, keepdims=True) for h in range(HEADS)
    ]
    bests = list(self_scores)
    totals = [jnp.ones((ROWS, 1), jnp.float32)] * HEADS
    numers = [None] * HEADS
    for u in range(2):
        for j in range(2):
            landed(orecv.at[2 * u + j], o_recv.at[2 * u + j])
            landed(srecv.at[u, pl.ds(j * 8, 8)], s_recv.at[2 * u + j])
        stats = srecv[u].T
        for h in range(HEADS):
            tops = [stats[:, j * 8 + h : j * 8 + h + 1] for j in range(2)]
            best = jnp.maximum(jnp.maximum(tops[0], tops[1]), bests[h])
            if u == 0:
                own_weight = jnp.exp2((self_scores[h] - best) * LOG2_SCALE)
                total = own_weight
                numer = own_weight.astype(jnp.bfloat16).astype(jnp.float32) * own_value
            else:
                shrink = jnp.exp2((bests[h] - best) * LOG2_SCALE)
                total = totals[h] * shrink
                numer = numers[h] * shrink
            for j in range(2):
                scale = jnp.exp2((tops[j] - best) * LOG2_SCALE)
                total = total + scale * stats[:, j * 8 + HEADS + h : j * 8 + HEADS + h + 1]
                numer = numer + scale * orecv[2 * u + j, h].astype(jnp.float32)
            bests[h], totals[h], numers[h] = best, total, numer
    for h in range(HEADS):
        att[:, h * HD : (h + 1) * HD] = (numers[h] / totals[h]).astype(jnp.bfloat16)

    loads[2].wait()

    def columns(tile, first=0, width=TILE):
        return pl.ds(pl.multiple_of(first + tile * TILE, TILE // 2), width)

    def half_columns(tile):
        return pl.ds(pl.multiple_of(tile * (TILE // 2), TILE // 2), TILE // 2)

    def first(side):
        return side * TILES * TILE

    def ring_peer(side, d):
        return (x_peer, y_peer)[side](d)

    def ring_block(side, d, cols):
        if side == 0:
            return part.at[(x + d) % 4, :, :, cols]
        return part.at[:, (y + d) % 4, :, cols]

    def project_out(tile, carry):
        for side in range(2):
            cols = columns(tile, side * TILES * TILE)
            part[:, :, :, cols] = (
                jnp.dot(att[...], wo[:, cols], preferred_element_type=jnp.float32)
                .astype(jnp.bfloat16)
                .reshape(4, 4, 16, TILE)
            )
            for d in (1, 3):
                src = ring_block(side, 2, columns(tile, first(side) + (TILE // 2 if d == 3 else 0), TILE // 2))
                dst = (via_a, via_b)[side].at[d // 2, :, :, half_columns(tile)]
                remote(
                    src, dst, via_send.at[side], via_recv.at[side, tile, d // 2], seq, ring_peer(side, d)
                ).start()
        return carry

    lax.fori_loop(0, TILES, project_out, 0)

    def relay(tile, carry):
        for side in range(2):
            via = (via_a, via_b)[side]
            for d in (1, 3):
                passing = via.at[d // 2, :, :, half_columns(tile)]
                landed(passing, via_recv.at[side, tile, d // 2])
                block = ring_block(
                    side, d, columns(tile, first(side) + (TILE // 2 if d == 3 else 0), TILE // 2)
                )
                block[...] = (
                    block[...].astype(jnp.float32) + passing[...].astype(jnp.float32)
                ).astype(jnp.bfloat16)
                remote(
                    ring_block(side, d, columns(tile, first(side))),
                    (rs_a, rs_b)[side].at[d // 2, :, :, columns(tile)],
                    rs1_send.at[side], rs1_recv.at[side, tile, d // 2], seq, ring_peer(side, d),
                ).start()
        return carry

    lax.fori_loop(0, TILES, relay, 0)

    def sum_first(tile, carry):
        for side in range(2):
            here = columns(tile)
            arriving = (rs_a, rs_b)[side]
            mid = (mid_a, mid_b)[side]
            total = ring_block(side, 0, columns(tile, first(side)))[...].astype(jnp.float32)
            for d in range(2):
                dst = arriving.at[d, :, :, here]
                landed(dst, rs1_recv.at[side, tile, d])
                total = total + dst[...].astype(jnp.float32)
            mid[:, :, here] = total.astype(jnp.bfloat16)
            for d in (1, 3, 2):
                if side == 0:
                    src, t = mid.at[(y + d) % 4, :, here], x * 4 + (y + d) % 4
                else:
                    src, t = mid.at[(x + d) % 4, :, here], (x + d) % 4 * 4 + y
                dst = (fin_a, fin_b)[side].at[d - 1, :, here]
                remote(
                    src, dst, rs2_send.at[side], rs2_recv.at[side, tile, d - 1], seq, t
                ).start()
        return carry

    lax.fori_loop(0, TILES, sum_first, 0)

    def sum_last(tile, carry):
        for side in range(2):
            here = columns(tile)
            arriving = (fin_a, fin_b)[side]
            if side == 0:
                total = mid_a[y, :, here].astype(jnp.float32)
            else:
                total = mid_b[x, :, here].astype(jnp.float32)
            for d in range(3):
                dst = arriving.at[d, :, here]
                pltpu.make_async_copy(dst, dst, rs2_recv.at[side, tile, d]).wait()
                total = total + arriving[d, :, here].astype(jnp.float32)
            out[:, columns(tile, side * TILES * TILE)] = total.astype(jnp.bfloat16)
        return carry

    lax.fori_loop(0, TILES, sum_last, 0)

    for i in range(2):
        landed((squares_x, squares_y)[i], sq_send.at[i])
    sent = hbuf.at[pl.ds(0, SHARDS - 1)]
    pltpu.make_async_copy(sent, sent, ag_send).wait()
    for i in range(2):
        landed(vbuf.at[pl.ds(0, SLOTS - CHUNKS)], kv_send.at[i])
        landed(vbuf.at[pl.ds(0, STAGED * CHUNK)], leg_send.at[i])
    for u in range(2):
        for j in range(2):
            same, _, there = q_copies(u, j)
            pl.when(jnp.logical_not(same))(there.wait_send)
            same, _, o_there, _, s_there = o_copies(u, j)

            @pl.when(jnp.logical_not(same))
            def _():
                o_there.wait_send()
                s_there.wait_send()

    for side in range(2):
        landed((via_a, via_b)[side], via_send.at[side])
        sent = (rs_a, rs_b)[side]
        pltpu.make_async_copy(sent, sent, rs1_send.at[side]).wait()
        sent = (fin_a, fin_b)[side]
        pltpu.make_async_copy(sent, sent, rs2_send.at[side]).wait()


def per_device(
    hidden_in,
    norm_gain,
    w_query,
    w_keyval,
    w_out,
    key_pool,
    value_pool,
    block_table,
    prefix_lengths,
    row_request,
):
    bf16, f32 = jnp.bfloat16, jnp.float32
    vmem = functools.partial(pltpu.VMEM)
    dma = pltpu.SemaphoreType.DMA
    any_spec = pl.BlockSpec(memory_space=pl.ANY)
    vmem_spec = pl.BlockSpec(memory_space=pltpu.VMEM)
    smem_spec = pl.BlockSpec(memory_space=pltpu.SMEM)
    return pl.pallas_call(
        body,
        out_shape=jax.ShapeDtypeStruct((16, 6144), bf16),
        in_specs=[any_spec, vmem_spec] + [any_spec] * 5 + [vmem_spec, smem_spec, vmem_spec],
        out_specs=vmem_spec,
        scratch_shapes=[
            vmem((SHARDS, ROWS, FEAT), bf16),
            vmem((SHARDS * FEAT, 512), bf16),
            vmem((FEAT, 6144), bf16),
            vmem((SLOTS, BLK, 2 * HD), bf16),
            vmem((SLOTS, BLK, HD), bf16),
            vmem((STAGED, CHUNK, BLK, HD), bf16),
            vmem((STAGED, CHUNK, BLK, HD), bf16),
            vmem((2, 2 * HEADS, ROWS, 2 * HD), bf16),
            vmem((HEADS, ROWS, HD), bf16),
            vmem((2, ROWS, HD), bf16),
            vmem((2, 2 * HEADS * ROWS, HD), f32),
            vmem((2, 2 * HEADS * ROWS, HD), f32),
            vmem((2, 2 * HEADS * ROWS, HD), f32),
            vmem((2, 2, HEADS, ROWS, HD), bf16),
            vmem((2, 2, 8, ROWS), f32),
            vmem((4, HEADS, ROWS, HD), bf16),
            vmem((2, 128, ROWS), f32),
            vmem((8, ROWS), f32),
            vmem((3, 8, ROWS), f32),
            vmem((8, ROWS), f32),
            vmem((3, 8, ROWS), f32),
            vmem((HD, HD), jnp.int32),
            vmem((64, HD), jnp.int32),
            vmem((64, HD), jnp.int32),
            vmem((ROWS, FEAT), bf16),
            vmem((4, 4, 16, 6144), bf16),
            vmem((2, 4, 16, 3072), bf16),
            vmem((2, 4, 16, 3072), bf16),
            vmem((2, 4, 16, 1536), bf16),
            vmem((2, 4, 16, 1536), bf16),
            vmem((4, 16, 3072), bf16),
            vmem((4, 16, 3072), bf16),
            vmem((3, 16, 3072), bf16),
            vmem((3, 16, 3072), bf16),
            dma((4,)),
            pltpu.SemaphoreType.REGULAR,
            dma((2,)),
            dma((2, 3)),
            dma,
            dma((SHARDS, 4)),
            dma((2,)),
            dma((2,)),
            dma((CHUNKS,)),
            dma((CHUNKS,)),
            dma((CHUNKS,)),
            dma((CHUNKS,)),
            dma((2, 2)),
            dma((2, 2)),
            dma,
            dma((2,)),
            dma((2, 2)),
            dma((4,)),
            dma((2, 2)),
            dma((4,)),
            dma((2,)),
            dma((2, TILES, 2)),
            dma((2,)),
            dma((2, TILES, 2)),
            dma((2,)),
            dma((2, TILES, 3)),
        ],
        compiler_params=pltpu.CompilerParams(
            collective_id=0, has_side_effects=True, vmem_limit_bytes=60 << 20
        ),
        cost_estimate=pl.CostEstimate(
            flops=10_000_000_000, bytes_accessed=20_000_000, transcendentals=13_000_000
        ),
    )(
        hidden_in,
        norm_gain.reshape(1, SHARDS * FEAT),
        w_query,
        w_keyval,
        w_out,
        key_pool,
        value_pool,
        block_table,
        prefix_lengths,
        row_request.reshape(1, ROWS),
    )


def solution(mesh):
    return jax.shard_map(
        per_device,
        mesh=mesh,
        in_specs=(
            P("seq", "tp"),
            P(),
            P(None, "tp"),
            P(None, "tp"),
            P("tp", None),
            P(("seq", "tp"), None, None),
            P(("seq", "tp"), None, None),
            P(),
            P(),
            P("seq"),
        ),
        out_specs=P(("seq", "tp"), None),
        check_vma=False,
    )
```

```python
import functools

import jax
import jax.numpy as jnp
from jax import lax
from jax.experimental import pallas as pl
from jax.experimental.pallas import tpu as pltpu
from jax.sharding import PartitionSpec as P

MESH = pl.DeviceIdType.MESH
HD = 128
BLK = 128
ROWS = 256
FEAT = 384
SHARDS = 16
HEADS = 3
SLOTS = 64
CHUNK = 8
CHUNKS = 8
STAGED = 6
TILE = 512
TILES = 6
MASKED = -1e30
LOG2_SCALE = 1.4426950408889634 / HD**0.5


def ring_partner(y, shift):
    return (7 - (y + 4 - shift) % 4 + shift) % 4


def body(
    hidden,
    gain,
    w_query,
    w_keyval,
    w_out,
    key_pool,
    value_pool,
    table,
    lengths,
    row_req,
    out,
    hbuf,
    wqkv,
    wo,
    kbuf,
    vbuf,
    kstage,
    vstage,
    qaug,
    qown,
    kvown,
    acc,
    top,
    tot,
    osend,
    ssend,
    orecv,
    srecv,
    squares_own,
    squares_x,
    squares_mid,
    squares_y,
    table_wide,
    table_cols,
    caps,
    att,
    part,
    rs_a,
    rs_b,
    via_a,
    via_b,
    mid_a,
    mid_b,
    fin_a,
    fin_b,
    load_sem,
    plane_sem,
    sq_send,
    sq_recv,
    ag_send,
    ag_recv,
    kv_send,
    leg_send,
    k_stage,
    v_stage,
    k_recv,
    v_recv,
    q_send,
    q_recv,
    own_send,
    own_recv,
    o_send,
    o_recv,
    s_send,
    s_recv,
    via_send,
    via_recv,
    rs1_send,
    rs1_recv,
    rs2_send,
    rs2_recv,
):
    seq = lax.axis_index("seq")
    tp = lax.axis_index("tp")
    x, y = tp // 4, tp % 4
    sign = 1 - 2 * (seq % 2)

    def remote(src, dst, send, recv, s, t):
        return pltpu.make_async_remote_copy(
            src, dst, send, recv, device_id=(s, t), device_id_type=MESH
        )

    def signal(sem, s, t):
        pl.semaphore_signal(sem, inc=1, device_id=(s, t), device_id_type=MESH)

    def x_peer(d):
        return (x + d) % 4 * 4 + y

    def y_peer(d):
        return x * 4 + (y + d) % 4

    barrier = pltpu.get_barrier_semaphore()
    for d in (1, 3, 2):
        signal(barrier, seq, x_peer(d))
        signal(barrier, seq, y_peer(d))
    for i in range(1, 8):
        signal(barrier, (seq + i) % 8, tp)

    own_load = pltpu.make_async_copy(hidden, hbuf.at[tp], load_sem.at[0])
    own_load.start()
    loads = [
        pltpu.make_async_copy(w_query, wqkv.at[:, pl.ds(0, 384)], load_sem.at[1]),
        pltpu.make_async_copy(w_keyval, wqkv.at[:, pl.ds(384, 128)], load_sem.at[2]),
        pltpu.make_async_copy(w_out, wo, load_sem.at[3]),
    ]
    for load in loads:
        load.start()
    own_load.wait()
    wide = hbuf[tp].astype(jnp.float32)
    own_sum = jnp.broadcast_to(jnp.sum(wide * wide, axis=1, keepdims=True), (ROWS, HD))
    squares_own[...] = own_sum.T[:8]
    pl.semaphore_wait(barrier, 13)
    signal(plane_sem, seq, x_peer(1))
    signal(plane_sem, seq, x_peer(3))

    half, quarter = ROWS // 2, ROWS // 4
    for d in (1, 3, 2):
        remote(
            squares_own, squares_x.at[d - 1], sq_send.at[0], sq_recv.at[0, d - 1], seq, x_peer(d)
        ).start()
    def forward(shard, first, rows, index, t):
        block = hbuf.at[shard, pl.ds(first, rows)]
        remote(block, block, ag_send, ag_recv.at[shard, index], seq, t).start()

    for d in (1, 3):
        forward(tp, 0, half, 0, x_peer(d))
        forward(tp, half, half, 1, y_peer(d))
    for d in (1, 3):
        forward(tp, half, half, 1, x_peer(d))
        forward(tp, 0, half, 0, y_peer(d))

    def place(ch):
        pair = ch // 2
        return ch % 2, ((pair + 1) // 2 + 1) % 2, pair // 2

    def is_local(ch):
        return ch // 2 == 1

    def stage(ch):
        return (ch + 6) % 8 % 6

    def send_stage(ch, carry):
        u, ix, iy = place(ch)
        back = u + ix * (3 - 2 * u)

        def send_one(i, c):
            g = (seq + i) % 8
            turn = 1 - 2 * (g % 2)
            kx = (x + 4 - turn * back) % 4
            shift = (kx % 2) * turn
            ky = ((y + 4 - shift) % 4 // 2 + iy) % 2
            lanes = pl.ds(pl.multiple_of((2 * kx + ky) * HD, HD), HD)
            k_src, v_src = key_pool.at[g, :, lanes], value_pool.at[g, :, lanes]

            def send(k_dst, v_dst):
                @pl.when(i == 0)
                def _():
                    pltpu.make_async_copy(k_src, k_dst, k_stage.at[ch]).start()
                    pltpu.make_async_copy(v_src, v_dst, v_stage.at[ch]).start()

                @pl.when(i != 0)
                def _():
                    remote(k_src, k_dst, kv_send.at[0], k_stage.at[ch], g, tp).start()
                    remote(v_src, v_dst, kv_send.at[1], v_stage.at[ch], g, tp).start()

            @pl.when(jnp.logical_not(is_local(ch)))
            def _():
                send(kstage.at[stage(ch), seq], vstage.at[stage(ch), seq])

            @pl.when(is_local(ch))
            def _():
                slot = ch * CHUNK + seq
                send(kbuf.at[slot, :, pl.ds(0, HD)], vbuf.at[slot])

            return c

        return lax.fori_loop(0, 8, send_one, carry)

    lax.fori_loop(0, 4, send_stage, 0)

    def landed(ref, sem):
        pltpu.make_async_copy(ref, ref, sem).wait()

    square_sums = squares_own[...]
    for d in range(3):
        landed(squares_x.at[d], sq_recv.at[0, d])
        square_sums = square_sums + squares_x[d]
    squares_mid[...] = square_sums
    for d in (1, 3, 2):
        remote(
            squares_mid, squares_y.at[d - 1], sq_send.at[1], sq_recv.at[1, d - 1], seq, y_peer(d)
        ).start()

    def send_leg(ch, carry):
        u, ix, iy = place(ch)
        kx = (x + 4 - sign * (u + ix * (3 - 2 * u))) % 4
        shift = (kx % 2) * sign
        xd = (kx + 4 + sign * u) % 4
        yd = iy * ring_partner(y, shift) + (1 - iy) * y
        slots = pl.ds(pl.multiple_of(ch * CHUNK, CHUNK), CHUNK)
        dest = xd * 4 + yd
        landed(kstage.at[stage(ch)], k_stage.at[ch])
        landed(vstage.at[stage(ch)], v_stage.at[ch])
        k_dst = kbuf.at[slots, :, pl.ds(0, HD)]
        remote(kstage.at[stage(ch)], k_dst, leg_send.at[0], k_recv.at[ch], seq, dest).start()
        remote(vstage.at[stage(ch)], vbuf.at[slots], leg_send.at[1], v_recv.at[ch], seq, dest).start()
        return carry

    def arrived(shard, first, rows, index):
        landed(hbuf.at[shard, pl.ds(first, rows)], ag_recv.at[shard, index])

    for d in (3, 1):
        shard = x_peer(d)
        arrived(shard, 0, half, 0)
        forward(shard, 0, half, 0, y_peer(1))
        forward(shard, 0, half, 0, y_peer(3))
        if d == 3:
            forward(shard, 0, half, 0, x_peer(1))
        shard = y_peer(d)
        arrived(shard, half, half, 1)
        forward(shard, half, half, 2, x_peer(1))
        forward(shard, half, half, 2, x_peer(3))
        if d == 3:
            forward(shard, half, half, 1, y_peer(1))
    for d in (1, 3):
        arrived(x_peer(d), half, half, 1)
        arrived(y_peer(d), 0, half, 0)
        if d == 1:
            forward(x_peer(d), half, half, 1, x_peer(3))
            forward(y_peer(d), 0, half, 0, y_peer(3))
    lax.fori_loop(4, CHUNKS, send_stage, 0)
    shard = x_peer(2)
    arrived(shard, 0, half, 0)
    forward(shard, 0, half, 0, y_peer(1))
    forward(shard, 0, half, 0, y_peer(3))
    shard = y_peer(2)
    arrived(shard, half, half, 1)
    forward(shard, half, half, 2, x_peer(1))
    forward(shard, half, half, 2, x_peer(3))
    for e in (3, 1, 2):
        for d in (3, 1):
            shard = (x + e) % 4 * 4 + (y + d) % 4
            arrived(shard, 0, half, 0)
            forward(shard, 0 if d == 3 else quarter, quarter, 0 if d == 3 else 1, y_peer(4 - d))
            shard = (x + d) % 4 * 4 + (y + e) % 4
            arrived(shard, half, half, 2)
            forward(
                shard, half if d == 3 else half + quarter, quarter, 2 if d == 3 else 3, x_peer(4 - d)
            )

    pl.semaphore_wait(plane_sem, 2)

    for d in range(3):
        landed(squares_y.at[d], sq_recv.at[1, d])
        square_sums = square_sums + squares_y[d]
    square_cols = jnp.broadcast_to(square_sums[:1], (HD, ROWS)).T
    factor = lax.rsqrt(square_cols[:, :1] / (SHARDS * FEAT) + 1e-5)
    loads[0].wait()
    loads[1].wait()

    def project(t, total):
        feats = pl.ds(pl.multiple_of(t * FEAT, FEAT), FEAT)
        normed = (
            hbuf[t].astype(jnp.float32) * factor * gain[:, feats].astype(jnp.float32)
        ).astype(jnp.bfloat16)
        return total + jnp.dot(normed, wqkv[feats, :], preferred_element_type=jnp.float32)

    def project_line(i, total):
        along = i // 4
        d = i % 4
        return project((x + (1 - along) * d) % 4 * 4 + (y + along * d) % 4, total)

    def project_far(i, total):
        return project((x + 1 + i // 3) % 4 * 4 + (y + 1 + i % 3) % 4, total)

    arrived(x_peer(2), half, half, 1)
    arrived(y_peer(2), 0, half, 0)
    projected = lax.fori_loop(0, 4, project_line, jnp.zeros((ROWS, 512), jnp.float32))
    projected = lax.fori_loop(5, 8, project_line, projected)
    for e in (3, 1, 2):
        shard = (x + e) % 4 * 4 + (y + 2) % 4
        arrived(shard, 0, quarter, 0)
        arrived(shard, quarter, quarter, 1)
        shard = (x + 2) % 4 * 4 + (y + e) % 4
        arrived(shard, half, quarter, 2)
        arrived(shard, half + quarter, quarter, 3)
    projected = lax.fori_loop(0, 9, project_far, projected).astype(jnp.bfloat16)
    for h in range(HEADS):
        qown[h] = projected[:, h * HD : (h + 1) * HD]
    kvown[tp % 2] = projected[:, HEADS * HD :]

    own_copy = remote(
        kvown.at[tp % 2], kvown.at[tp % 2], own_send, own_recv.at[tp % 2], seq, tp + 1 - 2 * (tp % 2)
    )
    own_half = tp % 2

    def q_copies(u, j):
        t = (x + 4 + sign * u) % 4 * 4 + (y // 2 * 2 + j + 4 + x % 2 * sign) % 4
        dst = qaug.at[u, pl.ds(own_half * HEADS, HEADS), :, pl.ds(0, HD)]
        there = remote(qown, dst, q_send.at[u, j], q_recv.at[u, own_half], seq, t)
        here = pltpu.make_async_copy(qown, dst, q_recv.at[u, own_half])
        return t == tp, here, there

    for u in (1, 0):
        for j in range(2):
            same, here, there = q_copies(u, j)
            pl.when(same)(here.start)
            pl.when(jnp.logical_not(same))(there.start)
    own_copy.start()
    lane = lax.broadcasted_iota(jnp.int32, (ROWS, HD), 1)
    first_request = seq // 2 * 8
    requests = jnp.broadcast_to(row_req[...], (HD, ROWS)).T
    onehot = jnp.where(requests == lane + first_request, 1.0, 0.0).astype(jnp.bfloat16)
    for u in range(2):
        for h in range(2 * HEADS):
            qaug[u, h, :, HD:] = onehot
    table_wide[...] = jnp.full_like(table_wide, -1)
    table_wide[:8, :64] = table[pl.ds(pl.multiple_of(first_request, 8), 8), :]
    table_cols[...] = table_wide[...].T[:64]
    table_lane = lax.broadcasted_iota(jnp.int32, (64, HD), 1)
    ends = jnp.zeros((64, HD), jnp.int32)
    for r in range(8):
        ends = jnp.where(table_lane == r, lengths[first_request + r], ends)
    caps[...] = jnp.clip(ends - BLK * lax.broadcasted_iota(jnp.int32, (64, HD), 0), 0, BLK)
    token = lax.broadcasted_iota(jnp.int32, (BLK, HD), 0)

    def mask_slot(slot, carry):
        ch, s = slot // 8, slot % 8
        u, ix, iy = place(ch)
        shift = ((x + 4 - sign * u) % 4) % 2 * sign
        xs = (x + 4 + sign * ix * (2 * u - 1)) % 4
        ys = iy * ring_partner(y, shift) + (1 - iy) * y
        block = (s * 16 + xs * 4 + ys) * 8 + seq
        valid = jnp.sum(jnp.where(table_cols[...] == block, caps[...], 0), axis=0, keepdims=True)
        kbuf[slot, :, HD:] = jnp.where(token < valid, 0.0, MASKED).astype(jnp.bfloat16)
        return carry

    lax.fori_loop(0, SLOTS, mask_slot, 0)
    top[...] = jnp.full_like(top, 2 * MASKED)
    tot[...] = jnp.zeros_like(tot)
    acc[...] = jnp.zeros_like(acc)

    for u in range(2):
        for part_half in range(2):
            dst = qaug.at[u, pl.ds(part_half * HEADS, HEADS), :, pl.ds(0, HD)]
            pltpu.make_async_copy(dst, dst, q_recv.at[u, part_half]).wait()

    lax.fori_loop(0, 2, send_leg, 0)
    lax.fori_loop(4, 6, send_leg, 0)

    def o_copies(u, to):
        kx = (x + 4 - sign * u) % 4
        shift = kx % 2 * sign
        yy = (y + 4 - shift) % 4
        t = kx * 4 + yy // 2 * 2 + to
        index = u * 2 + yy % 2
        o_src, o_dst = osend.at[u, to], orecv.at[index]
        s_src = ssend.at[u, to]
        s_dst = srecv.at[u, pl.ds(pl.multiple_of(yy % 2 * 8, 8), 8)]
        return (
            t == tp,
            pltpu.make_async_copy(o_src, o_dst, o_recv.at[index]),
            remote(o_src, o_dst, o_send.at[u, to], o_recv.at[index], seq, t),
            pltpu.make_async_copy(s_src, s_dst, s_recv.at[index]),
            remote(s_src, s_dst, s_send.at[u, to], s_recv.at[index], seq, t),
        )

    srecv[:, pl.ds(16, 112), :] = jnp.zeros((2, 112, ROWS), jnp.float32)

    def send_partials(u, to):
        stats = jnp.zeros((ROWS, HD), jnp.float32)
        for h in range(HEADS):
            rows = pl.ds(pl.multiple_of((to * HEADS + h) * ROWS, ROWS), ROWS)
            stats = jnp.where(lane == h, top[u, rows, :], stats)
            stats = jnp.where(lane == HEADS + h, tot[u, rows, :], stats)
            osend[u, to, h] = acc[u, rows, :].astype(jnp.bfloat16)
        ssend[u, to] = stats.T[:8]
        same, o_here_copy, o_there, s_here_copy, s_there = o_copies(u, to)

        @pl.when(same)
        def _():
            o_here_copy.start()
            s_here_copy.start()

        @pl.when(jnp.logical_not(same))
        def _():
            o_there.start()
            s_there.start()

    def attend_chunk(i, carry):
        late = i // 4
        ch = (1 - late) * ((i + 2) % 4) + late * i
        u = ch % 2
        slots = pl.ds(pl.multiple_of(ch * CHUNK, CHUNK), CHUNK)

        @pl.when((i == 3) | (i == 4))
        def _():
            send_leg(i + 3, 0)

        k_dst = kbuf.at[slots, :, pl.ds(0, HD)]

        @pl.when(jnp.logical_not(is_local(ch)))
        def _():
            landed(k_dst, k_recv.at[ch])
            landed(vbuf.at[slots], v_recv.at[ch])

        @pl.when(is_local(ch))
        def _():
            landed(k_dst, k_stage.at[ch])
            landed(vbuf.at[slots], v_stage.at[ch])

        keys = kbuf[slots].reshape(CHUNK * BLK, 2 * HD)
        values = vbuf[slots].reshape(CHUNK * BLK, HD)

        def attend(first_head, heads):
            rows = pl.ds(pl.multiple_of(first_head * ROWS, ROWS), heads * ROWS)
            scores = lax.dot_general(
                qaug[u, pl.ds(first_head, heads)].reshape(heads * ROWS, 2 * HD),
                keys,
                (((1,), (1,)), ((), ())),
                preferred_element_type=jnp.float32,
            )
            old = top[u, rows, :]
            new = jnp.maximum(old, jnp.max(scores, axis=1, keepdims=True))
            shrink = jnp.exp2((old - new) * LOG2_SCALE)
            weights = jnp.exp2(scores * LOG2_SCALE - new[:, :1] * LOG2_SCALE)
            top[u, rows, :] = new
            tot[u, rows, :] = tot[u, rows, :] * shrink + jnp.sum(weights, axis=1, keepdims=True)
            acc[u, rows, :] = acc[u, rows, :] * shrink + jnp.dot(
                weights.astype(jnp.bfloat16), values, preferred_element_type=jnp.float32
            )

        @pl.when(ch < CHUNKS - 2)
        def _():
            attend(0, 2 * HEADS)

        @pl.when(ch >= CHUNKS - 2)
        def _():
            def attend_owner(to, c):
                attend(to * HEADS, HEADS)
                send_partials(u, to)
                return c

            lax.fori_loop(0, 2, attend_owner, 0)

        return carry

    lax.fori_loop(0, CHUNKS, attend_chunk, 0)

    own_copy.wait_send()
    other = 1 - tp % 2
    pltpu.make_async_copy(kvown.at[other], kvown.at[other], own_recv.at[other]).wait()
    own_key = kvown[0].astype(jnp.float32)
    own_value = kvown[1].astype(jnp.float32)
    self_scores = [
        jnp.sum(qown[h].astype(jnp.float32) * own_key, axis=1, keepdims=True) for h in range(HEADS)
    ]
    bests = list(self_scores)
    totals = [jnp.ones((ROWS, 1), jnp.float32)] * HEADS
    numers = [None] * HEADS
    for u in range(2):
        for j in range(2):
            landed(orecv.at[2 * u + j], o_recv.at[2 * u + j])
            landed(srecv.at[u, pl.ds(j * 8, 8)], s_recv.at[2 * u + j])
        stats = srecv[u].T
        for h in range(HEADS):
            tops = [stats[:, j * 8 + h : j * 8 + h + 1] for j in range(2)]
            best = jnp.maximum(jnp.maximum(tops[0], tops[1]), bests[h])
            if u == 0:
                own_weight = jnp.exp2((self_scores[h] - best) * LOG2_SCALE)
                total = own_weight
                numer = own_weight.astype(jnp.bfloat16).astype(jnp.float32) * own_value
            else:
                shrink = jnp.exp2((bests[h] - best) * LOG2_SCALE)
                total = totals[h] * shrink
                numer = numers[h] * shrink
            for j in range(2):
                scale = jnp.exp2((tops[j] - best) * LOG2_SCALE)
                total = total + scale * stats[:, j * 8 + HEADS + h : j * 8 + HEADS + h + 1]
                numer = numer + scale * orecv[2 * u + j, h].astype(jnp.float32)
            bests[h], totals[h], numers[h] = best, total, numer
    for h in range(HEADS):
        att[:, h * HD : (h + 1) * HD] = (numers[h] / totals[h]).astype(jnp.bfloat16)

    loads[2].wait()

    def columns(tile, first=0, width=TILE):
        return pl.ds(pl.multiple_of(first + tile * TILE, TILE // 2), width)

    def half_columns(tile):
        return pl.ds(pl.multiple_of(tile * (TILE // 2), TILE // 2), TILE // 2)

    def first(side):
        return side * TILES * TILE

    def ring_peer(side, d):
        return (x_peer, y_peer)[side](d)

    def ring_block(side, d, cols):
        if side == 0:
            return part.at[(x + d) % 4, :, :, cols]
        return part.at[:, (y + d) % 4, :, cols]

    def project_out(tile, carry):
        for side in range(2):
            cols = columns(tile, side * TILES * TILE)
            part[:, :, :, cols] = (
                jnp.dot(att[...], wo[:, cols], preferred_element_type=jnp.float32)
                .astype(jnp.bfloat16)
                .reshape(4, 4, 16, TILE)
            )
            for d in (1, 3):
                src = ring_block(side, 2, columns(tile, first(side) + (TILE // 2 if d == 3 else 0), TILE // 2))
                dst = (via_a, via_b)[side].at[d // 2, :, :, half_columns(tile)]
                remote(
                    src, dst, via_send.at[side], via_recv.at[side, tile, d // 2], seq, ring_peer(side, d)
                ).start()
        return carry

    lax.fori_loop(0, TILES, project_out, 0)

    def relay(tile, carry):
        for side in range(2):
            via = (via_a, via_b)[side]
            for d in (1, 3):
                passing = via.at[d // 2, :, :, half_columns(tile)]
                landed(passing, via_recv.at[side, tile, d // 2])
                block = ring_block(
                    side, d, columns(tile, first(side) + (TILE // 2 if d == 3 else 0), TILE // 2)
                )
                block[...] = (
                    block[...].astype(jnp.float32) + passing[...].astype(jnp.float32)
                ).astype(jnp.bfloat16)
                remote(
                    ring_block(side, d, columns(tile, first(side))),
                    (rs_a, rs_b)[side].at[d // 2, :, :, columns(tile)],
                    rs1_send.at[side], rs1_recv.at[side, tile, d // 2], seq, ring_peer(side, d),
                ).start()
        return carry

    lax.fori_loop(0, TILES, relay, 0)

    def sum_first(tile, carry):
        for side in range(2):
            here = columns(tile)
            arriving = (rs_a, rs_b)[side]
            mid = (mid_a, mid_b)[side]
            total = ring_block(side, 0, columns(tile, first(side)))[...].astype(jnp.float32)
            for d in range(2):
                dst = arriving.at[d, :, :, here]
                landed(dst, rs1_recv.at[side, tile, d])
                total = total + dst[...].astype(jnp.float32)
            mid[:, :, here] = total.astype(jnp.bfloat16)
            for d in (1, 3, 2):
                if side == 0:
                    src, t = mid.at[(y + d) % 4, :, here], x * 4 + (y + d) % 4
                else:
                    src, t = mid.at[(x + d) % 4, :, here], (x + d) % 4 * 4 + y
                dst = (fin_a, fin_b)[side].at[d - 1, :, here]
                remote(
                    src, dst, rs2_send.at[side], rs2_recv.at[side, tile, d - 1], seq, t
                ).start()
        return carry

    lax.fori_loop(0, TILES, sum_first, 0)

    def sum_last(tile, carry):
        for side in range(2):
            here = columns(tile)
            arriving = (fin_a, fin_b)[side]
            if side == 0:
                total = mid_a[y, :, here].astype(jnp.float32)
            else:
                total = mid_b[x, :, here].astype(jnp.float32)
            for d in range(3):
                dst = arriving.at[d, :, here]
                pltpu.make_async_copy(dst, dst, rs2_recv.at[side, tile, d]).wait()
                total = total + arriving[d, :, here].astype(jnp.float32)
            out[:, columns(tile, side * TILES * TILE)] = total.astype(jnp.bfloat16)
        return carry

    lax.fori_loop(0, TILES, sum_last, 0)

    for i in range(2):
        landed((squares_x, squares_y)[i], sq_send.at[i])
    sent = hbuf.at[pl.ds(0, SHARDS - 1)]
    pltpu.make_async_copy(sent, sent, ag_send).wait()
    for i in range(2):
        landed(vbuf.at[pl.ds(0, SLOTS - CHUNKS)], kv_send.at[i])
        landed(vbuf.at[pl.ds(0, STAGED * CHUNK)], leg_send.at[i])
    for u in range(2):
        for j in range(2):
            same, _, there = q_copies(u, j)
            pl.when(jnp.logical_not(same))(there.wait_send)
            same, _, o_there, _, s_there = o_copies(u, j)

            @pl.when(jnp.logical_not(same))
            def _():
                o_there.wait_send()
                s_there.wait_send()

    for side in range(2):
        landed((via_a, via_b)[side], via_send.at[side])
        sent = (rs_a, rs_b)[side]
        pltpu.make_async_copy(sent, sent, rs1_send.at[side]).wait()
        sent = (fin_a, fin_b)[side]
        pltpu.make_async_copy(sent, sent, rs2_send.at[side]).wait()


def per_device(
    hidden_in,
    norm_gain,
    w_query,
    w_keyval,
    w_out,
    key_pool,
    value_pool,
    block_table,
    prefix_lengths,
    row_request,
):
    bf16, f32 = jnp.bfloat16, jnp.float32
    vmem = functools.partial(pltpu.VMEM)
    dma = pltpu.SemaphoreType.DMA
    any_spec = pl.BlockSpec(memory_space=pl.ANY)
    vmem_spec = pl.BlockSpec(memory_space=pltpu.VMEM)
    smem_spec = pl.BlockSpec(memory_space=pltpu.SMEM)
    return pl.pallas_call(
        body,
        out_shape=jax.ShapeDtypeStruct((16, 6144), bf16),
        in_specs=[any_spec, vmem_spec] + [any_spec] * 5 + [vmem_spec, smem_spec, vmem_spec],
        out_specs=vmem_spec,
        scratch_shapes=[
            vmem((SHARDS, ROWS, FEAT), bf16),
            vmem((SHARDS * FEAT, 512), bf16),
            vmem((FEAT, 6144), bf16),
            vmem((SLOTS, BLK, 2 * HD), bf16),
            vmem((SLOTS, BLK, HD), bf16),
            vmem((STAGED, CHUNK, BLK, HD), bf16),
            vmem((STAGED, CHUNK, BLK, HD), bf16),
            vmem((2, 2 * HEADS, ROWS, 2 * HD), bf16),
            vmem((HEADS, ROWS, HD), bf16),
            vmem((2, ROWS, HD), bf16),
            vmem((2, 2 * HEADS * ROWS, HD), f32),
            vmem((2, 2 * HEADS * ROWS, HD), f32),
            vmem((2, 2 * HEADS * ROWS, HD), f32),
            vmem((2, 2, HEADS, ROWS, HD), bf16),
            vmem((2, 2, 8, ROWS), f32),
            vmem((4, HEADS, ROWS, HD), bf16),
            vmem((2, 128, ROWS), f32),
            vmem((8, ROWS), f32),
            vmem((3, 8, ROWS), f32),
            vmem((8, ROWS), f32),
            vmem((3, 8, ROWS), f32),
            vmem((HD, HD), jnp.int32),
            vmem((64, HD), jnp.int32),
            vmem((64, HD), jnp.int32),
            vmem((ROWS, FEAT), bf16),
            vmem((4, 4, 16, 6144), bf16),
            vmem((2, 4, 16, 3072), bf16),
            vmem((2, 4, 16, 3072), bf16),
            vmem((2, 4, 16, 1536), bf16),
            vmem((2, 4, 16, 1536), bf16),
            vmem((4, 16, 3072), bf16),
            vmem((4, 16, 3072), bf16),
            vmem((3, 16, 3072), bf16),
            vmem((3, 16, 3072), bf16),
            dma((4,)),
            pltpu.SemaphoreType.REGULAR,
            dma((2,)),
            dma((2, 3)),
            dma,
            dma((SHARDS, 4)),
            dma((2,)),
            dma((2,)),
            dma((CHUNKS,)),
            dma((CHUNKS,)),
            dma((CHUNKS,)),
            dma((CHUNKS,)),
            dma((2, 2)),
            dma((2, 2)),
            dma,
            dma((2,)),
            dma((2, 2)),
            dma((4,)),
            dma((2, 2)),
            dma((4,)),
            dma((2,)),
            dma((2, TILES, 2)),
            dma((2,)),
            dma((2, TILES, 2)),
            dma((2,)),
            dma((2, TILES, 3)),
        ],
        compiler_params=pltpu.CompilerParams(
            collective_id=0, has_side_effects=True, vmem_limit_bytes=60 << 20
        ),
        cost_estimate=pl.CostEstimate(
            flops=10_000_000_000, bytes_accessed=20_000_000, transcendentals=13_000_000
        ),
    )(
        hidden_in,
        norm_gain.reshape(1, SHARDS * FEAT),
        w_query,
        w_keyval,
        w_out,
        key_pool,
        value_pool,
        block_table,
        prefix_lengths,
        row_request.reshape(1, ROWS),
    )


def solution(mesh):
    return jax.shard_map(
        per_device,
        mesh=mesh,
        in_specs=(
            P("seq", "tp"),
            P(),
            P(None, "tp"),
            P(None, "tp"),
            P("tp", None),
            P(("seq", "tp"), None, None),
            P(("seq", "tp"), None, None),
            P(),
            P(),
            P("seq"),
        ),
        out_specs=P(("seq", "tp"), None),
        check_vma=False,
    )
```

```python
import functools

import jax
import jax.numpy as jnp
from jax import lax
from jax.experimental import pallas as pl
from jax.experimental.pallas import tpu as pltpu
from jax.sharding import PartitionSpec as P

MESH = pl.DeviceIdType.MESH
HD = 128
BLK = 128
ROWS = 256
FEAT = 384
SHARDS = 16
HEADS = 3
SLOTS = 64
CHUNK = 8
CHUNKS = 8
STAGED = 6
TILE = 1024
TILES = 3
MASKED = -1e30
LOG2_SCALE = 1.4426950408889634 / HD**0.5


def ring_partner(y, shift):
    return (7 - (y + 4 - shift) % 4 + shift) % 4


def body(
    hidden,
    gain,
    w_query,
    w_keyval,
    w_out,
    key_pool,
    value_pool,
    table,
    lengths,
    row_req,
    out,
    hbuf,
    wqkv,
    wo,
    kbuf,
    vbuf,
    kstage,
    vstage,
    qaug,
    qown,
    kvown,
    acc,
    top,
    tot,
    osend,
    ssend,
    orecv,
    srecv,
    squares_own,
    squares_x,
    squares_mid,
    squares_y,
    table_wide,
    table_cols,
    caps,
    att,
    part,
    rs_a,
    rs_b,
    via_a,
    via_b,
    mid_a,
    mid_b,
    fin_a,
    fin_b,
    load_sem,
    plane_sem,
    sq_send,
    sq_recv,
    ag_send,
    ag_recv,
    kv_send,
    leg_send,
    k_stage,
    v_stage,
    k_recv,
    v_recv,
    q_send,
    q_recv,
    own_send,
    own_recv,
    o_send,
    o_recv,
    s_send,
    s_recv,
    via_send,
    via_recv,
    rs1_send,
    rs1_recv,
    rs2_send,
    rs2_recv,
):
    seq = lax.axis_index("seq")
    tp = lax.axis_index("tp")
    x, y = tp // 4, tp % 4
    sign = 1 - 2 * (seq % 2)

    def remote(src, dst, send, recv, s, t):
        return pltpu.make_async_remote_copy(
            src, dst, send, recv, device_id=(s, t), device_id_type=MESH
        )

    def signal(sem, s, t):
        pl.semaphore_signal(sem, inc=1, device_id=(s, t), device_id_type=MESH)

    def x_peer(d):
        return (x + d) % 4 * 4 + y

    def y_peer(d):
        return x * 4 + (y + d) % 4

    barrier = pltpu.get_barrier_semaphore()
    for d in (1, 3, 2):
        signal(barrier, seq, x_peer(d))
        signal(barrier, seq, y_peer(d))
    for i in range(1, 8):
        signal(barrier, (seq + i) % 8, tp)

    own_load = pltpu.make_async_copy(hidden, hbuf.at[tp], load_sem.at[0])
    own_load.start()
    loads = [
        pltpu.make_async_copy(w_query, wqkv.at[:, pl.ds(0, 384)], load_sem.at[1]),
        pltpu.make_async_copy(w_keyval, wqkv.at[:, pl.ds(384, 128)], load_sem.at[2]),
        pltpu.make_async_copy(w_out, wo, load_sem.at[3]),
    ]
    for load in loads:
        load.start()
    own_load.wait()
    wide = hbuf[tp].astype(jnp.float32)
    own_sum = jnp.broadcast_to(jnp.sum(wide * wide, axis=1, keepdims=True), (ROWS, HD))
    squares_own[...] = own_sum.T[:8]
    pl.semaphore_wait(barrier, 13)
    signal(plane_sem, seq, x_peer(1))
    signal(plane_sem, seq, x_peer(3))

    half, quarter = ROWS // 2, ROWS // 4
    for d in (1, 3, 2):
        remote(
            squares_own, squares_x.at[d - 1], sq_send.at[0], sq_recv.at[0, d - 1], seq, x_peer(d)
        ).start()
    def forward(shard, first, rows, index, t):
        block = hbuf.at[shard, pl.ds(first, rows)]
        remote(block, block, ag_send, ag_recv.at[shard, index], seq, t).start()

    for d in (1, 3):
        forward(tp, 0, half, 0, x_peer(d))
        forward(tp, half, half, 1, y_peer(d))
    for d in (1, 3):
        forward(tp, half, half, 1, x_peer(d))
        forward(tp, 0, half, 0, y_peer(d))

    def place(ch):
        pair = ch // 2
        return ch % 2, ((pair + 1) // 2 + 1) % 2, pair // 2

    def is_local(ch):
        return ch // 2 == 1

    def stage(ch):
        return (ch + 6) % 8 % 6

    def send_stage(ch, carry):
        u, ix, iy = place(ch)
        back = u + ix * (3 - 2 * u)

        def send_one(i, c):
            g = (seq + i) % 8
            turn = 1 - 2 * (g % 2)
            kx = (x + 4 - turn * back) % 4
            shift = (kx % 2) * turn
            ky = ((y + 4 - shift) % 4 // 2 + iy) % 2
            lanes = pl.ds(pl.multiple_of((2 * kx + ky) * HD, HD), HD)
            k_src, v_src = key_pool.at[g, :, lanes], value_pool.at[g, :, lanes]

            def send(k_dst, v_dst):
                @pl.when(i == 0)
                def _():
                    pltpu.make_async_copy(k_src, k_dst, k_stage.at[ch]).start()
                    pltpu.make_async_copy(v_src, v_dst, v_stage.at[ch]).start()

                @pl.when(i != 0)
                def _():
                    remote(k_src, k_dst, kv_send.at[0], k_stage.at[ch], g, tp).start()
                    remote(v_src, v_dst, kv_send.at[1], v_stage.at[ch], g, tp).start()

            @pl.when(jnp.logical_not(is_local(ch)))
            def _():
                send(kstage.at[stage(ch), seq], vstage.at[stage(ch), seq])

            @pl.when(is_local(ch))
            def _():
                slot = ch * CHUNK + seq
                send(kbuf.at[slot, :, pl.ds(0, HD)], vbuf.at[slot])

            return c

        return lax.fori_loop(0, 8, send_one, carry)

    lax.fori_loop(0, 4, send_stage, 0)

    def landed(ref, sem):
        pltpu.make_async_copy(ref, ref, sem).wait()

    square_sums = squares_own[...]
    for d in range(3):
        landed(squares_x.at[d], sq_recv.at[0, d])
        square_sums = square_sums + squares_x[d]
    squares_mid[...] = square_sums
    for d in (1, 3, 2):
        remote(
            squares_mid, squares_y.at[d - 1], sq_send.at[1], sq_recv.at[1, d - 1], seq, y_peer(d)
        ).start()

    def send_leg(ch, carry):
        u, ix, iy = place(ch)
        kx = (x + 4 - sign * (u + ix * (3 - 2 * u))) % 4
        shift = (kx % 2) * sign
        xd = (kx + 4 + sign * u) % 4
        yd = iy * ring_partner(y, shift) + (1 - iy) * y
        slots = pl.ds(pl.multiple_of(ch * CHUNK, CHUNK), CHUNK)
        dest = xd * 4 + yd
        landed(kstage.at[stage(ch)], k_stage.at[ch])
        landed(vstage.at[stage(ch)], v_stage.at[ch])
        k_dst = kbuf.at[slots, :, pl.ds(0, HD)]
        remote(kstage.at[stage(ch)], k_dst, leg_send.at[0], k_recv.at[ch], seq, dest).start()
        remote(vstage.at[stage(ch)], vbuf.at[slots], leg_send.at[1], v_recv.at[ch], seq, dest).start()
        return carry

    def arrived(shard, first, rows, index):
        landed(hbuf.at[shard, pl.ds(first, rows)], ag_recv.at[shard, index])

    for d in (3, 1):
        shard = x_peer(d)
        arrived(shard, 0, half, 0)
        forward(shard, 0, half, 0, y_peer(1))
        forward(shard, 0, half, 0, y_peer(3))
        if d == 3:
            forward(shard, 0, half, 0, x_peer(1))
        shard = y_peer(d)
        arrived(shard, half, half, 1)
        forward(shard, half, half, 2, x_peer(1))
        forward(shard, half, half, 2, x_peer(3))
        if d == 3:
            forward(shard, half, half, 1, y_peer(1))
    for d in (1, 3):
        arrived(x_peer(d), half, half, 1)
        arrived(y_peer(d), 0, half, 0)
        if d == 1:
            forward(x_peer(d), half, half, 1, x_peer(3))
            forward(y_peer(d), 0, half, 0, y_peer(3))
    lax.fori_loop(4, CHUNKS, send_stage, 0)
    shard = x_peer(2)
    arrived(shard, 0, half, 0)
    forward(shard, 0, half, 0, y_peer(1))
    forward(shard, 0, half, 0, y_peer(3))
    shard = y_peer(2)
    arrived(shard, half, half, 1)
    forward(shard, half, half, 2, x_peer(1))
    forward(shard, half, half, 2, x_peer(3))
    for e in (3, 1, 2):
        for d in (3, 1):
            shard = (x + e) % 4 * 4 + (y + d) % 4
            arrived(shard, 0, half, 0)
            forward(shard, 0 if d == 3 else quarter, quarter, 0 if d == 3 else 1, y_peer(4 - d))
            shard = (x + d) % 4 * 4 + (y + e) % 4
            arrived(shard, half, half, 2)
            forward(
                shard, half if d == 3 else half + quarter, quarter, 2 if d == 3 else 3, x_peer(4 - d)
            )

    pl.semaphore_wait(plane_sem, 2)

    for d in range(3):
        landed(squares_y.at[d], sq_recv.at[1, d])
        square_sums = square_sums + squares_y[d]
    square_cols = jnp.broadcast_to(square_sums[:1], (HD, ROWS)).T
    factor = lax.rsqrt(square_cols[:, :1] / (SHARDS * FEAT) + 1e-5)
    loads[0].wait()
    loads[1].wait()

    def project(t, total):
        feats = pl.ds(pl.multiple_of(t * FEAT, FEAT), FEAT)
        normed = (
            hbuf[t].astype(jnp.float32) * factor * gain[:, feats].astype(jnp.float32)
        ).astype(jnp.bfloat16)
        return total + jnp.dot(normed, wqkv[feats, :], preferred_element_type=jnp.float32)

    def project_line(i, total):
        along = i // 4
        d = i % 4
        return project((x + (1 - along) * d) % 4 * 4 + (y + along * d) % 4, total)

    def project_far(i, total):
        return project((x + 1 + i // 3) % 4 * 4 + (y + 1 + i % 3) % 4, total)

    arrived(x_peer(2), half, half, 1)
    arrived(y_peer(2), 0, half, 0)
    projected = lax.fori_loop(0, 4, project_line, jnp.zeros((ROWS, 512), jnp.float32))
    projected = lax.fori_loop(5, 8, project_line, projected)
    for e in (3, 1, 2):
        shard = (x + e) % 4 * 4 + (y + 2) % 4
        arrived(shard, 0, quarter, 0)
        arrived(shard, quarter, quarter, 1)
        shard = (x + 2) % 4 * 4 + (y + e) % 4
        arrived(shard, half, quarter, 2)
        arrived(shard, half + quarter, quarter, 3)
    projected = lax.fori_loop(0, 9, project_far, projected).astype(jnp.bfloat16)
    for h in range(HEADS):
        qown[h] = projected[:, h * HD : (h + 1) * HD]
    kvown[tp % 2] = projected[:, HEADS * HD :]

    own_copy = remote(
        kvown.at[tp % 2], kvown.at[tp % 2], own_send, own_recv.at[tp % 2], seq, tp + 1 - 2 * (tp % 2)
    )
    own_half = tp % 2

    def q_copies(u, j):
        t = (x + 4 + sign * u) % 4 * 4 + (y // 2 * 2 + j + 4 + x % 2 * sign) % 4
        dst = qaug.at[u, pl.ds(own_half * HEADS, HEADS), :, pl.ds(0, HD)]
        there = remote(qown, dst, q_send.at[u, j], q_recv.at[u, own_half], seq, t)
        here = pltpu.make_async_copy(qown, dst, q_recv.at[u, own_half])
        return t == tp, here, there

    for u in (1, 0):
        for j in range(2):
            same, here, there = q_copies(u, j)
            pl.when(same)(here.start)
            pl.when(jnp.logical_not(same))(there.start)
    own_copy.start()
    lane = lax.broadcasted_iota(jnp.int32, (ROWS, HD), 1)
    first_request = seq // 2 * 8
    requests = jnp.broadcast_to(row_req[...], (HD, ROWS)).T
    onehot = jnp.where(requests == lane + first_request, 1.0, 0.0).astype(jnp.bfloat16)
    for u in range(2):
        for h in range(2 * HEADS):
            qaug[u, h, :, HD:] = onehot
    table_wide[...] = jnp.full_like(table_wide, -1)
    table_wide[:8, :64] = table[pl.ds(pl.multiple_of(first_request, 8), 8), :]
    table_cols[...] = table_wide[...].T[:64]
    table_lane = lax.broadcasted_iota(jnp.int32, (64, HD), 1)
    ends = jnp.zeros((64, HD), jnp.int32)
    for r in range(8):
        ends = jnp.where(table_lane == r, lengths[first_request + r], ends)
    caps[...] = jnp.clip(ends - BLK * lax.broadcasted_iota(jnp.int32, (64, HD), 0), 0, BLK)
    token = lax.broadcasted_iota(jnp.int32, (BLK, HD), 0)

    def mask_slot(slot, carry):
        ch, s = slot // 8, slot % 8
        u, ix, iy = place(ch)
        shift = ((x + 4 - sign * u) % 4) % 2 * sign
        xs = (x + 4 + sign * ix * (2 * u - 1)) % 4
        ys = iy * ring_partner(y, shift) + (1 - iy) * y
        block = (s * 16 + xs * 4 + ys) * 8 + seq
        valid = jnp.sum(jnp.where(table_cols[...] == block, caps[...], 0), axis=0, keepdims=True)
        kbuf[slot, :, HD:] = jnp.where(token < valid, 0.0, MASKED).astype(jnp.bfloat16)
        return carry

    lax.fori_loop(0, SLOTS, mask_slot, 0)
    top[...] = jnp.full_like(top, 2 * MASKED)
    tot[...] = jnp.zeros_like(tot)
    acc[...] = jnp.zeros_like(acc)

    for u in range(2):
        for part_half in range(2):
            dst = qaug.at[u, pl.ds(part_half * HEADS, HEADS), :, pl.ds(0, HD)]
            pltpu.make_async_copy(dst, dst, q_recv.at[u, part_half]).wait()

    lax.fori_loop(0, 2, send_leg, 0)
    lax.fori_loop(4, 6, send_leg, 0)

    def o_copies(u, to):
        kx = (x + 4 - sign * u) % 4
        shift = kx % 2 * sign
        yy = (y + 4 - shift) % 4
        t = kx * 4 + yy // 2 * 2 + to
        index = u * 2 + yy % 2
        o_src, o_dst = osend.at[u, to], orecv.at[index]
        s_src = ssend.at[u, to]
        s_dst = srecv.at[u, pl.ds(pl.multiple_of(yy % 2 * 8, 8), 8)]
        return (
            t == tp,
            pltpu.make_async_copy(o_src, o_dst, o_recv.at[index]),
            remote(o_src, o_dst, o_send.at[u, to], o_recv.at[index], seq, t),
            pltpu.make_async_copy(s_src, s_dst, s_recv.at[index]),
            remote(s_src, s_dst, s_send.at[u, to], s_recv.at[index], seq, t),
        )

    srecv[:, pl.ds(16, 112), :] = jnp.zeros((2, 112, ROWS), jnp.float32)

    def send_partials(u, to):
        stats = jnp.zeros((ROWS, HD), jnp.float32)
        for h in range(HEADS):
            rows = pl.ds(pl.multiple_of((to * HEADS + h) * ROWS, ROWS), ROWS)
            stats = jnp.where(lane == h, top[u, rows, :], stats)
            stats = jnp.where(lane == HEADS + h, tot[u, rows, :], stats)
            osend[u, to, h] = acc[u, rows, :].astype(jnp.bfloat16)
        ssend[u, to] = stats.T[:8]
        same, o_here_copy, o_there, s_here_copy, s_there = o_copies(u, to)

        @pl.when(same)
        def _():
            o_here_copy.start()
            s_here_copy.start()

        @pl.when(jnp.logical_not(same))
        def _():
            o_there.start()
            s_there.start()

    def attend_chunk(i, carry):
        late = i // 4
        ch = (1 - late) * ((i + 2) % 4) + late * i
        u = ch % 2
        slots = pl.ds(pl.multiple_of(ch * CHUNK, CHUNK), CHUNK)

        @pl.when((i == 3) | (i == 4))
        def _():
            send_leg(i + 3, 0)

        k_dst = kbuf.at[slots, :, pl.ds(0, HD)]

        @pl.when(jnp.logical_not(is_local(ch)))
        def _():
            landed(k_dst, k_recv.at[ch])
            landed(vbuf.at[slots], v_recv.at[ch])

        @pl.when(is_local(ch))
        def _():
            landed(k_dst, k_stage.at[ch])
            landed(vbuf.at[slots], v_stage.at[ch])

        keys = kbuf[slots].reshape(CHUNK * BLK, 2 * HD)
        values = vbuf[slots].reshape(CHUNK * BLK, HD)

        def attend(first_head, heads):
            rows = pl.ds(pl.multiple_of(first_head * ROWS, ROWS), heads * ROWS)
            scores = lax.dot_general(
                qaug[u, pl.ds(first_head, heads)].reshape(heads * ROWS, 2 * HD),
                keys,
                (((1,), (1,)), ((), ())),
                preferred_element_type=jnp.float32,
            )
            old = top[u, rows, :]
            new = jnp.maximum(old, jnp.max(scores, axis=1, keepdims=True))
            shrink = jnp.exp2((old - new) * LOG2_SCALE)
            weights = jnp.exp2(scores * LOG2_SCALE - new[:, :1] * LOG2_SCALE)
            top[u, rows, :] = new
            tot[u, rows, :] = tot[u, rows, :] * shrink + jnp.sum(weights, axis=1, keepdims=True)
            acc[u, rows, :] = acc[u, rows, :] * shrink + jnp.dot(
                weights.astype(jnp.bfloat16), values, preferred_element_type=jnp.float32
            )

        @pl.when(ch < CHUNKS - 2)
        def _():
            attend(0, 2 * HEADS)

        @pl.when(ch >= CHUNKS - 2)
        def _():
            def attend_owner(to, c):
                attend(to * HEADS, HEADS)
                send_partials(u, to)
                return c

            lax.fori_loop(0, 2, attend_owner, 0)

        return carry

    lax.fori_loop(0, CHUNKS, attend_chunk, 0)

    own_copy.wait_send()
    other = 1 - tp % 2
    pltpu.make_async_copy(kvown.at[other], kvown.at[other], own_recv.at[other]).wait()
    own_key = kvown[0].astype(jnp.float32)
    own_value = kvown[1].astype(jnp.float32)
    self_scores = [
        jnp.sum(qown[h].astype(jnp.float32) * own_key, axis=1, keepdims=True) for h in range(HEADS)
    ]
    bests = list(self_scores)
    totals = [jnp.ones((ROWS, 1), jnp.float32)] * HEADS
    numers = [None] * HEADS
    for u in range(2):
        for j in range(2):
            landed(orecv.at[2 * u + j], o_recv.at[2 * u + j])
            landed(srecv.at[u, pl.ds(j * 8, 8)], s_recv.at[2 * u + j])
        stats = srecv[u].T
        for h in range(HEADS):
            tops = [stats[:, j * 8 + h : j * 8 + h + 1] for j in range(2)]
            best = jnp.maximum(jnp.maximum(tops[0], tops[1]), bests[h])
            if u == 0:
                own_weight = jnp.exp2((self_scores[h] - best) * LOG2_SCALE)
                total = own_weight
                numer = own_weight.astype(jnp.bfloat16).astype(jnp.float32) * own_value
            else:
                shrink = jnp.exp2((bests[h] - best) * LOG2_SCALE)
                total = totals[h] * shrink
                numer = numers[h] * shrink
            for j in range(2):
                scale = jnp.exp2((tops[j] - best) * LOG2_SCALE)
                total = total + scale * stats[:, j * 8 + HEADS + h : j * 8 + HEADS + h + 1]
                numer = numer + scale * orecv[2 * u + j, h].astype(jnp.float32)
            bests[h], totals[h], numers[h] = best, total, numer
    for h in range(HEADS):
        att[:, h * HD : (h + 1) * HD] = (numers[h] / totals[h]).astype(jnp.bfloat16)

    loads[2].wait()

    def columns(tile, first=0, width=TILE):
        return pl.ds(pl.multiple_of(first + tile * TILE, TILE // 2), width)

    def half_columns(tile):
        return pl.ds(pl.multiple_of(tile * (TILE // 2), TILE // 2), TILE // 2)

    def first(side):
        return side * TILES * TILE

    def ring_peer(side, d):
        return (x_peer, y_peer)[side](d)

    def ring_block(side, d, cols):
        if side == 0:
            return part.at[(x + d) % 4, :, :, cols]
        return part.at[:, (y + d) % 4, :, cols]

    def project_out(tile, carry):
        for side in range(2):
            cols = columns(tile, side * TILES * TILE)
            part[:, :, :, cols] = (
                jnp.dot(att[...], wo[:, cols], preferred_element_type=jnp.float32)
                .astype(jnp.bfloat16)
                .reshape(4, 4, 16, TILE)
            )
            for d in (1, 3):
                src = ring_block(side, 2, columns(tile, first(side) + (TILE // 2 if d == 3 else 0), TILE // 2))
                dst = (via_a, via_b)[side].at[d // 2, :, :, half_columns(tile)]
                remote(
                    src, dst, via_send.at[side], via_recv.at[side, tile, d // 2], seq, ring_peer(side, d)
                ).start()
        return carry

    lax.fori_loop(0, TILES, project_out, 0)

    def relay(tile, carry):
        for side in range(2):
            via = (via_a, via_b)[side]
            for d in (1, 3):
                passing = via.at[d // 2, :, :, half_columns(tile)]
                landed(passing, via_recv.at[side, tile, d // 2])
                block = ring_block(
                    side, d, columns(tile, first(side) + (TILE // 2 if d == 3 else 0), TILE // 2)
                )
                block[...] = (
                    block[...].astype(jnp.float32) + passing[...].astype(jnp.float32)
                ).astype(jnp.bfloat16)
                remote(
                    ring_block(side, d, columns(tile, first(side))),
                    (rs_a, rs_b)[side].at[d // 2, :, :, columns(tile)],
                    rs1_send.at[side], rs1_recv.at[side, tile, d // 2], seq, ring_peer(side, d),
                ).start()
        return carry

    lax.fori_loop(0, TILES, relay, 0)

    def sum_first(tile, carry):
        for side in range(2):
            here = columns(tile)
            arriving = (rs_a, rs_b)[side]
            mid = (mid_a, mid_b)[side]
            total = ring_block(side, 0, columns(tile, first(side)))[...].astype(jnp.float32)
            for d in range(2):
                dst = arriving.at[d, :, :, here]
                landed(dst, rs1_recv.at[side, tile, d])
                total = total + dst[...].astype(jnp.float32)
            mid[:, :, here] = total.astype(jnp.bfloat16)
            for d in (1, 3, 2):
                if side == 0:
                    src, t = mid.at[(y + d) % 4, :, here], x * 4 + (y + d) % 4
                else:
                    src, t = mid.at[(x + d) % 4, :, here], (x + d) % 4 * 4 + y
                dst = (fin_a, fin_b)[side].at[d - 1, :, here]
                remote(
                    src, dst, rs2_send.at[side], rs2_recv.at[side, tile, d - 1], seq, t
                ).start()
        return carry

    lax.fori_loop(0, TILES, sum_first, 0)

    def sum_last(tile, carry):
        for side in range(2):
            here = columns(tile)
            arriving = (fin_a, fin_b)[side]
            if side == 0:
                total = mid_a[y, :, here].astype(jnp.float32)
            else:
                total = mid_b[x, :, here].astype(jnp.float32)
            for d in range(3):
                dst = arriving.at[d, :, here]
                pltpu.make_async_copy(dst, dst, rs2_recv.at[side, tile, d]).wait()
                total = total + arriving[d, :, here].astype(jnp.float32)
            out[:, columns(tile, side * TILES * TILE)] = total.astype(jnp.bfloat16)
        return carry

    lax.fori_loop(0, TILES, sum_last, 0)

    for i in range(2):
        landed((squares_x, squares_y)[i], sq_send.at[i])
    sent = hbuf.at[pl.ds(0, SHARDS - 1)]
    pltpu.make_async_copy(sent, sent, ag_send).wait()
    for i in range(2):
        landed(vbuf.at[pl.ds(0, SLOTS - CHUNKS)], kv_send.at[i])
        landed(vbuf.at[pl.ds(0, STAGED * CHUNK)], leg_send.at[i])
    for u in range(2):
        for j in range(2):
            same, _, there = q_copies(u, j)
            pl.when(jnp.logical_not(same))(there.wait_send)
            same, _, o_there, _, s_there = o_copies(u, j)

            @pl.when(jnp.logical_not(same))
            def _():
                o_there.wait_send()
                s_there.wait_send()

    for side in range(2):
        landed((via_a, via_b)[side], via_send.at[side])
        sent = (rs_a, rs_b)[side]
        pltpu.make_async_copy(sent, sent, rs1_send.at[side]).wait()
        sent = (fin_a, fin_b)[side]
        pltpu.make_async_copy(sent, sent, rs2_send.at[side]).wait()


def per_device(
    hidden_in,
    norm_gain,
    w_query,
    w_keyval,
    w_out,
    key_pool,
    value_pool,
    block_table,
    prefix_lengths,
    row_request,
):
    bf16, f32 = jnp.bfloat16, jnp.float32
    vmem = functools.partial(pltpu.VMEM)
    dma = pltpu.SemaphoreType.DMA
    any_spec = pl.BlockSpec(memory_space=pl.ANY)
    vmem_spec = pl.BlockSpec(memory_space=pltpu.VMEM)
    smem_spec = pl.BlockSpec(memory_space=pltpu.SMEM)
    return pl.pallas_call(
        body,
        out_shape=jax.ShapeDtypeStruct((16, 6144), bf16),
        in_specs=[any_spec, vmem_spec] + [any_spec] * 5 + [vmem_spec, smem_spec, vmem_spec],
        out_specs=vmem_spec,
        scratch_shapes=[
            vmem((SHARDS, ROWS, FEAT), bf16),
            vmem((SHARDS * FEAT, 512), bf16),
            vmem((FEAT, 6144), bf16),
            vmem((SLOTS, BLK, 2 * HD), bf16),
            vmem((SLOTS, BLK, HD), bf16),
            vmem((STAGED, CHUNK, BLK, HD), bf16),
            vmem((STAGED, CHUNK, BLK, HD), bf16),
            vmem((2, 2 * HEADS, ROWS, 2 * HD), bf16),
            vmem((HEADS, ROWS, HD), bf16),
            vmem((2, ROWS, HD), bf16),
            vmem((2, 2 * HEADS * ROWS, HD), f32),
            vmem((2, 2 * HEADS * ROWS, HD), f32),
            vmem((2, 2 * HEADS * ROWS, HD), f32),
            vmem((2, 2, HEADS, ROWS, HD), bf16),
            vmem((2, 2, 8, ROWS), f32),
            vmem((4, HEADS, ROWS, HD), bf16),
            vmem((2, 128, ROWS), f32),
            vmem((8, ROWS), f32),
            vmem((3, 8, ROWS), f32),
            vmem((8, ROWS), f32),
            vmem((3, 8, ROWS), f32),
            vmem((HD, HD), jnp.int32),
            vmem((64, HD), jnp.int32),
            vmem((64, HD), jnp.int32),
            vmem((ROWS, FEAT), bf16),
            vmem((4, 4, 16, 6144), bf16),
            vmem((2, 4, 16, 3072), bf16),
            vmem((2, 4, 16, 3072), bf16),
            vmem((2, 4, 16, 1536), bf16),
            vmem((2, 4, 16, 1536), bf16),
            vmem((4, 16, 3072), bf16),
            vmem((4, 16, 3072), bf16),
            vmem((3, 16, 3072), bf16),
            vmem((3, 16, 3072), bf16),
            dma((4,)),
            pltpu.SemaphoreType.REGULAR,
            dma((2,)),
            dma((2, 3)),
            dma,
            dma((SHARDS, 4)),
            dma((2,)),
            dma((2,)),
            dma((CHUNKS,)),
            dma((CHUNKS,)),
            dma((CHUNKS,)),
            dma((CHUNKS,)),
            dma((2, 2)),
            dma((2, 2)),
            dma,
            dma((2,)),
            dma((2, 2)),
            dma((4,)),
            dma((2, 2)),
            dma((4,)),
            dma((2,)),
            dma((2, TILES, 2)),
            dma((2,)),
            dma((2, TILES, 2)),
            dma((2,)),
            dma((2, TILES, 3)),
        ],
        compiler_params=pltpu.CompilerParams(
            collective_id=0, has_side_effects=True, vmem_limit_bytes=60 << 20
        ),
        cost_estimate=pl.CostEstimate(
            flops=10_000_000_000, bytes_accessed=20_000_000, transcendentals=13_000_000
        ),
    )(
        hidden_in,
        norm_gain.reshape(1, SHARDS * FEAT),
        w_query,
        w_keyval,
        w_out,
        key_pool,
        value_pool,
        block_table,
        prefix_lengths,
        row_request.reshape(1, ROWS),
    )


def solution(mesh):
    return jax.shard_map(
        per_device,
        mesh=mesh,
        in_specs=(
            P("seq", "tp"),
            P(),
            P(None, "tp"),
            P(None, "tp"),
            P("tp", None),
            P(("seq", "tp"), None, None),
            P(("seq", "tp"), None, None),
            P(),
            P(),
            P("seq"),
        ),
        out_specs=P(("seq", "tp"), None),
        check_vma=False,
    )
```
